32 devices in a mesh: dp: 8 (over y, x, core), fsdp: 4 (over z).
Axes of the slice: x: 2, y: 2, z: 4, core: 2. Of those that a mesh axis runs over, the one named last changes fastest.
Arguments:
- tokens: bfloat16 [16384, 768], P(('dp', 'fsdp')), may hold values from -6 to 6
- doc_ids: int32 [16384], P(('dp', 'fsdp')), may hold values from 0 to 127, as said below
- pass_embed: bfloat16 [768], P(('dp', 'fsdp')), may hold values from -6 to 6
- ln1_gain: bfloat16 [768], P(('dp', 'fsdp')), may hold values from 0.5 to 1.5
- w_qkv: bfloat16 [768, 2304], P(('dp', 'fsdp')), may hold values from -0.21875 to 0.21875
- w_out: bfloat16 [768, 768], P(('dp', 'fsdp')), may hold values from -0.75 to 0.75
- ln2_gain: bfloat16 [768], P(('dp', 'fsdp')), may hold values from 0.5 to 1.5
- w_up: bfloat16 [768, 3072], P(('dp', 'fsdp')), may hold values from -0.21875 to 0.21875
- w_down: bfloat16 [3072, 768], P(('dp', 'fsdp')), may hold values from -0.109375 to 0.109375
- cotangent: bfloat16 [16384, 768], P(('dp', 'fsdp')), may hold values from -6 to 6
Outputs:
- layer_out: bfloat16 [16384, 768], P(('dp', 'fsdp'))
- tokens_grad: float32 [16384, 768], P(('dp', 'fsdp'))
- embed_grad: float32 [768], P(('dp', 'fsdp'))
- ln1_grad: float32 [768], P(('dp', 'fsdp'))
- qkv_grad: float32 [768, 2304], P(('dp', 'fsdp'))
- wout_grad: float32 [768, 768], P(('dp', 'fsdp'))
- ln2_grad: float32 [768], P(('dp', 'fsdp'))
- up_grad: float32 [768, 3072], P(('dp', 'fsdp'))
- down_grad: float32 [3072, 768], P(('dp', 'fsdp'))
The draws below stay inside these ranges and needn't reach their ends.
Inputs may be any that keep to these rules, and one draw needn't show every extreme that they name: `doc_ids`: the tokens of one device, 512 in a row from a multiple of 512, form 1, 2 or 4 documents of equal length, numbered 4 b to 4 b + 3 within the b-th such block; the first block holds one document and the last four.
All inputs are finite; a program needn't handle non-finite values.
Results may differ from the reference program's by a relative error of at most 0.014.
Values may be sent and summed in bfloat16 or wider, within the bound.
A program may use at most 256 MiB of HBM per device.

```python
import jax
import jax.numpy as jnp
from jax import lax

D = 768
HEADS = 12
HEAD_DIM = 64
FF = 3072
TOK_DEV = 512
TOKENS = 16384


def draw_doc_ids(key, part):
    key = jax.random.fold_in(key, 11)
    blocks = TOKENS // TOK_DEV
    splits = 2 ** jax.random.randint(key, (blocks,), 0, 3)
    splits = splits.at[0].set(1).at[blocks - 1].set(4)
    places = jnp.arange(TOK_DEV, dtype=jnp.int32)
    row_index = places[None, :] * splits[:, None] // TOK_DEV
    idents = jnp.arange(blocks, dtype=jnp.int32)[:, None] * 4 + row_index
    return idents.reshape(TOKENS).astype(jnp.int32)


def steps_of(own_key, extent, cuts, least, largest):
    level = 1.0
    for axis_at, parts in cuts:
        steps = jax.random.uniform(jax.random.fold_in(jax.random.fold_in(own_key, 6), axis_at), (parts,), jnp.float32, least / len(cuts), largest / len(cuts))
        level = level * jnp.repeat(jnp.exp(steps), extent[axis_at] // parts).reshape((-1,) + (1,) * (len(extent) - 1 - axis_at))
    return level


def gaussian(rng, shape, width, most, split=(), kind=jnp.bfloat16):
    entries = width * jax.random.normal(rng, shape, jnp.float32)
    if split:
        entries = entries * steps_of(rng, shape, split, -0.22, 0.18)
    return jnp.clip(entries, -most, most).astype(kind)


def setup_inputs(seed: int = 0) -> dict:
    arg_keys = jax.random.split(jax.random.key(seed), 11)
    return {
        "tokens": gaussian(arg_keys[0], (TOKENS, D), 1.0, 6.0, ((0, 32),)),
        "doc_ids": draw_doc_ids(jax.random.fold_in(arg_keys[10], 71), 0),
        "pass_embed": gaussian(arg_keys[2], (D,), 1.0, 6.0, ((0, 32),)),
        "ln1_gain": jnp.clip(1.0 + 0.1 * jax.random.normal(arg_keys[3], (D,), jnp.float32), 0.5, 1.5).astype(jnp.bfloat16),
        "w_qkv": gaussian(arg_keys[4], (D, 3 * D), D ** -0.5, 0.21875, ((0, 32),)),
        "w_out": gaussian(arg_keys[5], (D, D), HEAD_DIM ** -0.5, 0.75, ((0, 32),)),
        "ln2_gain": jnp.clip(1.0 + 0.1 * jax.random.normal(arg_keys[6], (D,), jnp.float32), 0.5, 1.5).astype(jnp.bfloat16),
        "w_up": gaussian(arg_keys[7], (D, FF), D ** -0.5, 0.21875, ((0, 32),)),
        "w_down": gaussian(arg_keys[8], (FF, D), FF ** -0.5, 0.109375, ((0, 32),)),
        "cotangent": gaussian(arg_keys[9], (TOKENS, D), 1.0, 6.0, ((0, 32),)),
    }


@jax.custom_vjp
def low(v):
    return lax.optimization_barrier(v.astype(jnp.bfloat16)).astype(jnp.float32)

@jax.custom_vjp
def low_back(v):
    return v

def low_keep(v):
    return (low(v), None)

def low_pass(kept, grad):
    return (grad,)

def back_keep(v):
    return (v, None)

def back_low(kept, grad):
    return (low(grad),)
low.defvjp(low_keep, low_pass)
low_back.defvjp(back_keep, back_low)
EPS = 1e-05

def layer_norm(values, gain):
    center = values - lax.optimization_barrier(jnp.mean(values, -1, keepdims=True))
    spread = lax.optimization_barrier(jnp.mean(center * center, -1, keepdims=True))
    return center * lax.rsqrt(spread + EPS) * gain

def hi_dot(left, right):
    return jnp.dot(left, right, precision=lax.Precision.HIGHEST, preferred_element_type=jnp.float32)

def attend(queries, key_rows, value_rows, allowed):
    scores = jnp.einsum('qhd,khd->hqk', queries, key_rows, precision=lax.Precision.HIGHEST) * HEAD_DIM ** (-0.5)
    scores = low_back(scores)
    scores = jnp.where(allowed[None], scores, -1e+30)
    probs = jax.nn.softmax(scores, -1)
    return jnp.einsum('hqk,khd->qhd', low(probs), value_rows, precision=lax.Precision.HIGHEST)

def one_pass(inputs, earlier, allowed, weights):
    ln1_w, qkv_w, out_w, ln2_w, up_w, down_w = weights
    length = inputs.shape[0]
    normed = low(layer_norm(inputs, ln1_w))
    qkv = low(low_back(hi_dot(normed, qkv_w))).reshape(length, 3, HEADS, HEAD_DIM)
    queries, own_keys, own_values = (qkv[:, 0], qkv[:, 1], qkv[:, 2])
    if earlier is None:
        key_rows, value_rows, mask_rows = (own_keys, own_values, allowed)
    else:
        key_rows = jnp.concatenate([earlier[0], own_keys], 0)
        value_rows = jnp.concatenate([earlier[1], own_values], 0)
        mask_rows = jnp.concatenate([allowed, allowed], 1)
    attn = low(low_back(attend(queries, key_rows, value_rows, mask_rows))).reshape(length, D)
    middle = inputs + low_back(hi_dot(attn, out_w))
    second = low(layer_norm(middle, ln2_w))
    hidden = low_back(hi_dot(second, up_w))
    active = low(jax.nn.gelu(hidden, approximate=False))
    return (middle + low_back(hi_dot(active, down_w)), (own_keys, own_values))

def forward(inputs, embed, ln1_w, qkv_w, out_w, ln2_w, up_w, down_w, allowed):
    weights = (ln1_w, qkv_w, out_w, ln2_w, up_w, down_w)
    first, kept = one_pass(inputs, None, allowed, weights)
    result, unused = one_pass(first + embed, kept, allowed, weights)
    return result

def reference(tokens, doc_ids, pass_embed, ln1_gain, w_qkv, w_out, ln2_gain, w_up, w_down, cotangent):
    params = tuple((w.astype(jnp.float32) for w in (pass_embed, ln1_gain, w_qkv, w_out, ln2_gain, w_up, w_down)))
    blocks = TOKENS // TOK_DEV
    inputs = tokens.astype(jnp.float32).reshape(blocks, TOK_DEV, D)
    idents = doc_ids.reshape(blocks, TOK_DEV)
    cotans = cotangent.astype(jnp.float32).reshape(blocks, TOK_DEV, D)
    places = jnp.arange(TOK_DEV, dtype=jnp.int32)

    def step(totals, item):
        block_in, block_ids, block_cot = item
        allowed = (block_ids[:, None] == block_ids[None, :]) & (places[None, :] <= places[:, None])

        def local(values, *weights):
            return forward(values, *weights, allowed)
        result, pull = jax.vjp(local, block_in, *params)
        grads = pull(block_cot)
        totals = tuple((a + g for a, g in zip(totals, grads[1:])))
        return (totals, (result, grads[0]))
    start = tuple((jnp.zeros(w.shape, jnp.float32) for w in params))
    totals, (results, input_grads) = lax.scan(step, start, (inputs, idents, cotans))
    return (results.reshape(TOKENS, D).astype(jnp.bfloat16), input_grads.reshape(TOKENS, D), totals[0], totals[1], totals[2], totals[3], totals[4], totals[5], totals[6])
```

```python
import functools

import jax
import jax.numpy as jnp
from jax import lax
from jax.experimental import pallas as pl
from jax.experimental.pallas import tpu as pltpu
from jax.sharding import PartitionSpec as P

HEAD_DIM = 64


EPS = 1e-05


def layer_norm(values, gain):
    center = values - jnp.mean(values, -1, keepdims=True)
    spread = jnp.mean(center * center, -1, keepdims=True)
    return center * lax.rsqrt(spread + EPS) * gain


def exact_gelu(values):
    return jax.nn.gelu(values, approximate=False)


MESH = pl.DeviceIdType.MESH


def places():
    d, z = lax.axis_index("dp"), lax.axis_index("fsdp")
    y, x, c = d // 4, lax.rem(d // 2, 2), lax.rem(d, 2)
    return d, y, x, c, z


def greet(peers):
    barrier = pltpu.get_barrier_semaphore()
    for peer in peers:
        pl.semaphore_signal(barrier, inc=1, device_id=peer, device_id_type=MESH)
    pl.semaphore_wait(barrier, len(peers))


def peers_of(d, y, x, c, z):
    sideways = (y * 4 + (1 - x) * 2 + c, z)
    upward = ((1 - y) * 4 + x * 2 + c, z)
    sibling = (y * 4 + x * 2 + 1 - c, z)
    along = [(d, lax.rem(z + k, 4)) for k in (1, 2, 3)]
    return sideways, upward, sibling, along


class Gather:
    def __init__(self, shards, wholes, sems):
        self.shards, self.wholes = shards, wholes
        self.z_send, self.z_recv, self.p_send, self.p_recv, self.d_send, self.d_recv, self.own = sems
        self.d, self.y, self.x, self.c, self.z = places()
        self.sideways, self.upward, self.sibling, self.along = peers_of(self.d, self.y, self.x, self.c, self.z)
        self.started = []

    def halves(self, a):
        width = self.shards[a].shape[2]
        if width == 128:
            return ((0, 128),)
        return ((0, width // 2), (width // 2, width // 2))

    def group(self, a, y, x, cols=None):
        rows = self.shards[a].shape[0]
        at = (y * 4 + x * 2 + self.c) * 4 * rows
        whole = self.wholes[a]
        if cols is None:
            return whole.at[pl.ds(at, 4 * rows)]
        return whole.at[pl.ds(at, 4 * rows), :, pl.ds(*cols)]

    def send(self, src, dst, send, recv, peer):
        copy = pltpu.make_async_remote_copy(
            src_ref=src, dst_ref=dst, send_sem=send, recv_sem=recv, device_id=peer, device_id_type=MESH
        )
        copy.start()
        self.started.append(copy)
        return copy

    def begin(self, a):
        rows = self.shards[a].shape[0]
        at = (self.d * 4 + self.z) * rows
        shard, mine = self.shards[a], self.wholes[a].at[pl.ds(at, rows)]
        own = pltpu.make_async_copy(shard, mine, self.own.at[a])
        own.start()
        along = []
        for k in range(3):
            along.append(self.send(shard, mine, self.z_send.at[a, k], self.z_recv.at[a, k], self.along[k]))
        return own, along

    def to_sibling(self, a, g, y, x):
        block = self.group(a, y, x)
        return self.send(block, block, self.d_send.at[a, g], self.d_recv.at[a, g], self.sibling)

    def first(self, a, begun):
        own, along = begun
        own.wait()
        for copy in along:
            copy.wait_recv()
        sent = []
        for h, cols in enumerate(self.halves(a)):
            block = self.group(a, self.y, self.x, cols)
            one, two = (self.sideways, self.upward) if h == 0 else (self.upward, self.sideways)
            sent.append((
                self.send(block, block, self.p_send.at[a, h, 0], self.p_recv.at[a, h, 0], one),
                self.send(block, block, self.p_send.at[a, h, 1], self.p_recv.at[a, h, 1], two),
            ))
        shared = [self.to_sibling(a, 0, self.y, self.x)]
        return sent, shared

    def second(self, a, state):
        sent, shared = state
        last = []
        for h, cols in enumerate(self.halves(a)):
            sent[h][0].wait_recv()
            y, x = (self.y, 1 - self.x) if h == 0 else (1 - self.y, self.x)
            block = self.group(a, y, x, cols)
            two = self.upward if h == 0 else self.sideways
            last.append(self.send(block, block, self.p_send.at[a, h, 2], self.p_recv.at[a, h, 2], two))
        return sent, shared, last

    def third(self, a, state):
        sent, shared, last = state
        for copies in sent:
            copies[1].wait_recv()
        shared.append(self.to_sibling(a, 1, self.y, 1 - self.x))
        shared.append(self.to_sibling(a, 2, 1 - self.y, self.x))
        return shared, last

    def fourth(self, a, state):
        shared, last = state
        for copy in last:
            copy.wait_recv()
        shared.append(self.to_sibling(a, 3, 1 - self.y, 1 - self.x))
        return shared

    def finish(self, a, shared):
        for copy in shared:
            copy.wait_recv()

    def close(self):
        for copy in self.started:
            copy.wait_send()


def gather_kernel(*refs):
    shards, wholes, sems = refs[:5], refs[5:10], refs[10:]
    g = Gather(shards, wholes, sems)
    greet([g.sideways, g.upward, g.sibling, *g.along])
    order = (0, 1, 2, 3, 4)
    state = {a: g.begin(a) for a in order}
    steps = (g.first, g.second, g.third, g.fourth)
    for tick in range(len(order) + len(steps) - 1):
        for late, step in enumerate(steps):
            if 0 <= tick - late < len(order):
                a = order[tick - late]
                state[a] = step(a, state[a])
    for a in order:
        g.finish(a, state[a])
    g.close()


def gather_all(shards):
    count = len(shards)
    dma = pltpu.SemaphoreType.DMA
    return pl.pallas_call(
        gather_kernel,
        out_shape=[jax.ShapeDtypeStruct((32 * s.shape[0],) + s.shape[1:], s.dtype) for s in shards],
        in_specs=[pl.BlockSpec(memory_space=pl.ANY)] * count,
        out_specs=[pl.BlockSpec(memory_space=pl.ANY)] * count,
        scratch_shapes=[
            dma((count, 3)), dma((count, 3)), dma((count, 2, 3)), dma((count, 2, 3)), dma((count, 4)), dma((count, 4)), dma((count,)),
        ],
        name="gather",
        compiler_params=pltpu.CompilerParams(collective_id=0, has_side_effects=True),
    )(*shards)


class Reduce:
    def __init__(self, parts, r0, r1, r2, r3, outs, sems):
        self.parts, self.r0, self.r1, self.r2, self.r3, self.outs = parts, r0, r1, r2, r3, outs
        self.d_send, self.d_recv, self.p_send, self.p_recv, self.z_send, self.z_recv = sems
        self.d, self.y, self.x, self.c, self.z = places()
        self.sideways, self.upward, self.sibling, self.along = peers_of(self.d, self.y, self.x, self.c, self.z)
        self.started = []

    send = Gather.send

    def halves(self, a):
        width = self.outs[a].shape[2]
        if width == 128:
            return ((0, 128),)
        return ((0, width // 2), (width // 2, width // 2))

    def add(self, count, into, into_at, other, other_at, cols):
        cols = pl.ds(*cols)

        def one(i, carry):
            into[into_at + i, :, cols] = (
                into[into_at + i, :, cols].astype(jnp.float32) + other[other_at + i, :, cols].astype(jnp.float32)
            ).astype(into.dtype)
            return carry

        lax.fori_loop(0, count, one, 0)

    def begin(self, a):
        rows = self.outs[a].shape[0]
        copies = []
        for g in range(4):
            src = self.parts[a].at[pl.ds((g * 2 + 1 - self.c) * 4 * rows, 4 * rows)]
            dst = self.r0[a].at[pl.ds(g * 4 * rows, 4 * rows)]
            copies.append(self.send(src, dst, self.d_send.at[a, g], self.d_recv.at[a, g], self.sibling))
        return copies

    def first(self, a, copies):
        rows = self.outs[a].shape[0]
        width = self.outs[a].shape[2]
        for g in range(4):
            copies[g].wait_recv()
            self.add(4 * rows, self.r0[a], g * 4 * rows, self.parts[a], (g * 2 + self.c) * 4 * rows, (0, width))
        sent = []
        for h, cols in enumerate(self.halves(a)):
            pair = []
            for i in range(2):
                g = (1 - self.y) * 2 + i if h == 0 else i * 2 + 1 - self.x
                src = self.r0[a].at[pl.ds(g * 4 * rows, 4 * rows), :, pl.ds(*cols)]
                dst = self.r1[a].at[pl.ds(i * 4 * rows, 4 * rows), :, pl.ds(*cols)]
                peer = self.upward if h == 0 else self.sideways
                pair.append(self.send(src, dst, self.p_send.at[a, h, i], self.p_recv.at[a, h, i], peer))
            sent.append(pair)
        return sent

    def second(self, a, sent):
        rows = self.outs[a].shape[0]
        onward = []
        for h, cols in enumerate(self.halves(a)):
            for i in range(2):
                sent[h][i].wait_recv()
                g = self.y * 2 + i if h == 0 else i * 2 + self.x
                self.add(4 * rows, self.r1[a], i * 4 * rows, self.r0[a], g * 4 * rows, cols)
            far = 1 - self.x if h == 0 else 1 - self.y
            peer = self.sideways if h == 0 else self.upward
            src = self.r1[a].at[pl.ds(far * 4 * rows, 4 * rows), :, pl.ds(*cols)]
            dst = self.r2[a].at[:, :, pl.ds(*cols)]
            onward.append(self.send(src, dst, self.p_send.at[a, h, 2], self.p_recv.at[a, h, 2], peer))
        return onward

    def third(self, a, onward):
        rows = self.outs[a].shape[0]
        for h, cols in enumerate(self.halves(a)):
            onward[h].wait_recv()
            near = self.x if h == 0 else self.y
            self.add(4 * rows, self.r2[a], 0, self.r1[a], near * 4 * rows, cols)
        along = []
        for k in range(3):
            to = lax.rem(self.z + k + 1, 4)
            src = self.r2[a].at[pl.ds(to * rows, rows)]
            dst = self.r3[a].at[pl.ds(k * rows, rows)]
            along.append(self.send(src, dst, self.z_send.at[a, k], self.z_recv.at[a, k], self.along[k]))
        return along

    def finish(self, a, along):
        rows = self.outs[a].shape[0]
        for copy in along:
            copy.wait_recv()

        def one(i, carry):
            total = self.r2[a][self.z * rows + i].astype(jnp.float32)
            for k in range(3):
                total = total + self.r3[a][k * rows + i].astype(jnp.float32)
            self.outs[a][i] = total
            return carry

        lax.fori_loop(0, rows, one, 0)

    def close(self):
        for copy in self.started:
            copy.wait_send()


def reduce_kernel(count, *refs):
    parts, outs = refs[:count], refs[count : 2 * count]
    r0, r1, r2, r3 = (refs[(2 + k) * count : (3 + k) * count] for k in range(4))
    g = Reduce(parts, r0, r1, r2, r3, outs, refs[6 * count :])
    greet([g.sideways, g.upward, g.sibling, *g.along])
    order = range(count)
    state = {a: g.begin(a) for a in order}
    steps = (g.first, g.second, g.third, g.finish)
    for tick in range(len(order) + len(steps) - 1):
        for late, step in enumerate(steps):
            if 0 <= tick - late < len(order):
                a = order[tick - late]
                state[a] = step(a, state[a])
    g.close()


def reduce_all(parts):
    count = len(parts)
    dma = pltpu.SemaphoreType.DMA
    scratch = []
    for blocks in (16, 8, 4, 3):
        scratch += [pltpu.VMEM((p.shape[0] // 32 * blocks,) + p.shape[1:], p.dtype) for p in parts]
    return pl.pallas_call(
        functools.partial(reduce_kernel, count),
        out_shape=[jax.ShapeDtypeStruct((p.shape[0] // 32,) + p.shape[1:], jnp.float32) for p in parts],
        in_specs=[pl.BlockSpec(memory_space=pltpu.VMEM)] * count,
        out_specs=[pl.BlockSpec(memory_space=pltpu.VMEM)] * count,
        scratch_shapes=scratch + [
            dma((count, 4)), dma((count, 4)), dma((count, 2, 3)), dma((count, 2, 3)), dma((count, 3)), dma((count, 3)),
        ],
        name="reduce",
        compiler_params=pltpu.CompilerParams(collective_id=1, has_side_effects=True, vmem_limit_bytes=56 << 20),
    )(*parts)


def run_block(inputs, earlier, allowed, weights):
    embed, ln1_w, qkv_w, out_w, ln2_w, up_w, down_w = weights
    length, model_width = inputs.shape
    head_count = model_width // HEAD_DIM
    scale = HEAD_DIM ** (-0.5)
    normed = layer_norm(inputs, ln1_w.astype(jnp.float32)).astype(jnp.bfloat16)
    qkv = jnp.dot(normed, qkv_w, preferred_element_type=jnp.float32).astype(jnp.bfloat16)
    qkv = qkv.reshape(length, 3, head_count, HEAD_DIM)
    queries, own_keys, own_values = (qkv[:, 0], qkv[:, 1], qkv[:, 2])
    if earlier is None:
        key_rows, value_rows = (own_keys, own_values)
    else:
        key_rows = jnp.concatenate([earlier[0], own_keys], 0)
        value_rows = jnp.concatenate([earlier[1], own_values], 0)
    scores = (
        jnp.einsum("qhd,khd->hqk", queries, key_rows, preferred_element_type=jnp.float32) * scale
    )
    scores = jnp.where(allowed[None], scores, -1e30)
    peak = jnp.max(scores, -1, keepdims=True)
    expos = jnp.exp(scores - peak)
    probs = expos / jnp.sum(expos, -1, keepdims=True)
    attn = jnp.einsum(
        "hqk,khd->qhd", probs.astype(jnp.bfloat16), value_rows, preferred_element_type=jnp.float32
    )
    attn = attn.astype(jnp.bfloat16).reshape(length, model_width)
    middle = inputs + jnp.dot(attn, out_w, preferred_element_type=jnp.float32)
    second = layer_norm(middle, ln2_w.astype(jnp.float32)).astype(jnp.bfloat16)
    hidden = jnp.dot(second, up_w, preferred_element_type=jnp.float32)
    active = exact_gelu(hidden).astype(jnp.bfloat16)
    result = middle + jnp.dot(active, down_w, preferred_element_type=jnp.float32)
    kept = {
        "normed": normed,
        "queries": queries,
        "key_rows": key_rows,
        "value_rows": value_rows,
        "probs": probs,
        "attn": attn,
        "middle": middle,
        "second": second,
        "hidden": hidden,
        "active": active,
        "own_kv": (own_keys, own_values),
    }
    return (result, kept)


def run_back(inputs, earlier, allowed, weights, upstream, extra):
    embed, ln1_w, qkv_w, out_w, ln2_w, up_w, down_w = weights
    length, model_width = inputs.shape
    head_count = model_width // HEAD_DIM
    scale = HEAD_DIM ** (-0.5)
    unused, kept = run_block(inputs, earlier, allowed, weights)
    down_rounded = upstream.astype(jnp.bfloat16)
    down_g = jnp.dot(kept["active"].T, down_rounded, preferred_element_type=jnp.float32)
    active_g = jnp.dot(down_rounded, down_w.T, preferred_element_type=jnp.float32)
    unused_gelu, gelu_pull = jax.vjp(exact_gelu, kept["hidden"])
    hidden_g = gelu_pull(active_g)[0].astype(jnp.bfloat16)
    up_g = jnp.dot(kept["second"].T, hidden_g, preferred_element_type=jnp.float32)
    second_g = jnp.dot(hidden_g, up_w.T, preferred_element_type=jnp.float32)
    unused_norm, norm_pull = jax.vjp(layer_norm, kept["middle"], ln2_w.astype(jnp.float32))
    middle_part, ln2_g = norm_pull(second_g)
    middle_g = upstream + middle_part
    attn_rounded = middle_g.astype(jnp.bfloat16)
    wout_g = jnp.dot(kept["attn"].T, attn_rounded, preferred_element_type=jnp.float32)
    attn_g = jnp.dot(attn_rounded, out_w.T, preferred_element_type=jnp.float32)
    attn_g = attn_g.astype(jnp.bfloat16).reshape(length, head_count, HEAD_DIM)
    probs = kept["probs"]
    value_g = jnp.einsum(
        "hqk,qhd->khd", probs.astype(jnp.bfloat16), attn_g, preferred_element_type=jnp.float32
    )
    probs_g = jnp.einsum(
        "qhd,khd->hqk", attn_g, kept["value_rows"], preferred_element_type=jnp.float32
    )
    scores_g = probs * (probs_g - jnp.sum(probs * probs_g, -1, keepdims=True))
    scores_g = scores_g.astype(jnp.bfloat16)
    query_g = (
        jnp.einsum("hqk,khd->qhd", scores_g, kept["key_rows"], preferred_element_type=jnp.float32)
        * scale
    )
    key_g = (
        jnp.einsum("hqk,qhd->khd", scores_g, kept["queries"], preferred_element_type=jnp.float32)
        * scale
    )
    if earlier is None:
        earlier_g = None
        own_key_g, own_value_g = (key_g, value_g)
    else:
        earlier_g = (key_g[:length], value_g[:length])
        own_key_g, own_value_g = (key_g[length:], value_g[length:])
    if extra is not None:
        own_key_g = own_key_g + extra[0]
        own_value_g = own_value_g + extra[1]
    qkv_rounded = jnp.stack([query_g, own_key_g, own_value_g], 1).astype(jnp.bfloat16)
    qkv_rounded = qkv_rounded.reshape(length, 3 * model_width)
    qkv_g = jnp.dot(kept["normed"].T, qkv_rounded, preferred_element_type=jnp.float32)
    normed_g = jnp.dot(qkv_rounded, qkv_w.T, preferred_element_type=jnp.float32)
    unused_first, first_pull = jax.vjp(layer_norm, inputs, ln1_w.astype(jnp.float32))
    input_part, ln1_g = first_pull(normed_g)
    input_g = middle_g + input_part
    return ((ln1_g, qkv_g, wout_g, ln2_g, up_g, down_g), input_g, earlier_g)


AXES = ("dp", "fsdp")


def gather_weights(near, shards):
    if not near:
        return tuple(lax.all_gather(s, AXES, axis=0, tiled=True) for s in shards)
    embed, ln1, qkv, out, ln2, up, down = shards
    rows = embed.shape[0]
    small = jnp.zeros((1, 8, 128), jnp.bfloat16)
    small = small.at[0, :3, :rows].set(jnp.stack([embed, ln1, ln2]))
    cut = lambda w: w.reshape(w.shape[0] // 8, 8, w.shape[1])
    small, out, qkv, up, down = gather_all([small, cut(out), cut(qkv), cut(up), cut(down)])
    vectors = small[:, :3, :rows].transpose(1, 0, 2).reshape(3, 32 * rows)
    join = lambda w: w.reshape(w.shape[0] * 8, w.shape[2])
    return (vectors[0], vectors[1], join(qkv), join(out), vectors[2], join(up), join(down))


def reduce_grads(near, totals):
    if not near:
        return lax.psum_scatter(totals, AXES, scatter_dimension=0, tiled=True)
    embed, ln1, qkv, out, ln2, up, down = totals
    rows = embed.shape[0] // 32
    small = jnp.stack([embed, ln1, ln2]).reshape(3, 32, rows).transpose(1, 0, 2)
    small = jnp.zeros((32, 8, 128), jnp.bfloat16).at[:, :3, :rows].set(small.astype(jnp.bfloat16))
    cut = lambda w: w.astype(jnp.bfloat16).reshape(w.shape[0] // 8, 8, w.shape[1])
    down, up, out, qkv, small = reduce_all([cut(down), cut(up), cut(out), cut(qkv), small])
    join = lambda w: w.reshape(w.shape[0] * 8, w.shape[2])
    return (small[0, 0, :rows], small[0, 1, :rows], join(qkv), join(out), small[0, 2, :rows], join(up), join(down))


def body(near, tokens, doc_ids, pass_embed, ln1_gain, w_qkv, w_out, ln2_gain, w_up, w_down, cotangent):
    weights = gather_weights(near, (pass_embed, ln1_gain, w_qkv, w_out, ln2_gain, w_up, w_down))
    length = tokens.shape[0]
    places = jnp.arange(length, dtype=jnp.int32)
    allowed = (doc_ids[:, None] == doc_ids[None, :]) & (places[None, :] <= places[:, None])
    doubled = jnp.concatenate([allowed, allowed], 1)
    inputs = tokens.astype(jnp.float32)
    first_out, first_kept = run_block(inputs, None, allowed, weights)
    earlier = first_kept["own_kv"]
    second_in = first_out + weights[0].astype(jnp.float32)
    second_out, unused = run_block(second_in, earlier, doubled, weights)
    layer_out = second_out.astype(jnp.bfloat16)
    late_grads, second_in_g, earlier_g = run_back(
        second_in, earlier, doubled, weights, cotangent.astype(jnp.float32), None
    )
    embed_g = jnp.sum(second_in_g, 0)
    early_grads, tokens_grad, unused_g = run_back(
        inputs, None, allowed, weights, second_in_g, earlier_g
    )
    totals = (embed_g,) + tuple((a + b for a, b in zip(late_grads, early_grads)))
    return (layer_out, tokens_grad, *reduce_grads(near, totals))


def solution(mesh):
    near = dict(mesh.shape) == {"dp": 8, "fsdp": 4}
    placed = (
        P(("dp", "fsdp"), None),
        P(("dp", "fsdp")),
        P(("dp", "fsdp")),
        P(("dp", "fsdp")),
        P(("dp", "fsdp"), None),
        P(("dp", "fsdp"), None),
        P(("dp", "fsdp")),
        P(("dp", "fsdp"), None),
        P(("dp", "fsdp"), None),
        P(("dp", "fsdp"), None),
    )
    return jax.shard_map(
        functools.partial(body, near),
        mesh=mesh,
        in_specs=placed,
        out_specs=(
            P(("dp", "fsdp"), None),
            P(("dp", "fsdp"), None),
            P(("dp", "fsdp")),
            P(("dp", "fsdp")),
            P(("dp", "fsdp"), None),
            P(("dp", "fsdp"), None),
            P(("dp", "fsdp")),
            P(("dp", "fsdp"), None),
            P(("dp", "fsdp"), None),
        ),
        check_vma=False,
    )
```

```python
import functools
import math

import jax
import jax.numpy as jnp
from jax import lax
from jax.experimental import pallas as pl
from jax.experimental.pallas import tpu as pltpu
from jax.sharding import PartitionSpec as P

HEAD_DIM = 64


MESH = pl.DeviceIdType.MESH


def places():
    d, z = lax.axis_index("dp"), lax.axis_index("fsdp")
    y, x, c = d // 4, lax.rem(d // 2, 2), lax.rem(d, 2)
    return d, y, x, c, z


def greet(peers):
    barrier = pltpu.get_barrier_semaphore()
    for peer in peers:
        pl.semaphore_signal(barrier, inc=1, device_id=peer, device_id_type=MESH)
    pl.semaphore_wait(barrier, len(peers))


def peers_of(d, y, x, c, z):
    sideways = (y * 4 + (1 - x) * 2 + c, z)
    upward = ((1 - y) * 4 + x * 2 + c, z)
    sibling = (y * 4 + x * 2 + 1 - c, z)
    along = [(d, lax.rem(z + k, 4)) for k in (1, 2, 3)]
    return sideways, upward, sibling, along


class Gather:
    def __init__(self, shards, wholes, sems):
        self.shards, self.wholes = shards, wholes
        self.z_send, self.z_recv, self.p_send, self.p_recv, self.d_send, self.d_recv, self.own = sems
        self.d, self.y, self.x, self.c, self.z = places()
        self.sideways, self.upward, self.sibling, self.along = peers_of(self.d, self.y, self.x, self.c, self.z)
        self.started = []

    def halves(self, a):
        width = self.shards[a].shape[2]
        if width == 128:
            return ((0, 128),)
        return ((0, width // 2), (width // 2, width // 2))

    def group(self, a, y, x, cols=None):
        rows = self.shards[a].shape[0]
        at = (y * 4 + x * 2 + self.c) * 4 * rows
        whole = self.wholes[a]
        if cols is None:
            return whole.at[pl.ds(at, 4 * rows)]
        return whole.at[pl.ds(at, 4 * rows), :, pl.ds(*cols)]

    def send(self, src, dst, send, recv, peer):
        copy = pltpu.make_async_remote_copy(
            src_ref=src, dst_ref=dst, send_sem=send, recv_sem=recv, device_id=peer, device_id_type=MESH
        )
        copy.start()
        self.started.append(copy)
        return copy

    def begin(self, a):
        rows = self.shards[a].shape[0]
        at = (self.d * 4 + self.z) * rows
        shard, mine = self.shards[a], self.wholes[a].at[pl.ds(at, rows)]
        own = pltpu.make_async_copy(shard, mine, self.own.at[a])
        own.start()
        along = []
        for k in range(3):
            along.append(self.send(shard, mine, self.z_send.at[a, k], self.z_recv.at[a, k], self.along[k]))
        return own, along

    def to_sibling(self, a, g, y, x):
        block = self.group(a, y, x)
        return self.send(block, block, self.d_send.at[a, g], self.d_recv.at[a, g], self.sibling)

    def first(self, a, begun):
        own, along = begun
        own.wait()
        for copy in along:
            copy.wait_recv()
        sent = []
        for h, cols in enumerate(self.halves(a)):
            block = self.group(a, self.y, self.x, cols)
            one, two = (self.sideways, self.upward) if h == 0 else (self.upward, self.sideways)
            sent.append((
                self.send(block, block, self.p_send.at[a, h, 0], self.p_recv.at[a, h, 0], one),
                self.send(block, block, self.p_send.at[a, h, 1], self.p_recv.at[a, h, 1], two),
            ))
        shared = [self.to_sibling(a, 0, self.y, self.x)]
        return sent, shared

    def second(self, a, state):
        sent, shared = state
        last = []
        for h, cols in enumerate(self.halves(a)):
            sent[h][0].wait_recv()
            y, x = (self.y, 1 - self.x) if h == 0 else (1 - self.y, self.x)
            block = self.group(a, y, x, cols)
            two = self.upward if h == 0 else self.sideways
            last.append(self.send(block, block, self.p_send.at[a, h, 2], self.p_recv.at[a, h, 2], two))
        return sent, shared, last

    def third(self, a, state):
        sent, shared, last = state
        for copies in sent:
            copies[1].wait_recv()
        shared.append(self.to_sibling(a, 1, self.y, 1 - self.x))
        shared.append(self.to_sibling(a, 2, 1 - self.y, self.x))
        return shared, last

    def fourth(self, a, state):
        shared, last = state
        for copy in last:
            copy.wait_recv()
        shared.append(self.to_sibling(a, 3, 1 - self.y, 1 - self.x))
        return shared

    def finish(self, a, shared):
        for copy in shared:
            copy.wait_recv()

    def close(self):
        for copy in self.started:
            copy.wait_send()


def gather_kernel(*refs):
    shards, wholes, sems = refs[:5], refs[5:10], refs[10:]
    g = Gather(shards, wholes, sems)
    greet([g.sideways, g.upward, g.sibling, *g.along])
    order = (0, 1, 2, 3, 4)
    state = {a: g.begin(a) for a in order}
    steps = (g.first, g.second, g.third, g.fourth)
    for tick in range(len(order) + len(steps) - 1):
        for late, step in enumerate(steps):
            if 0 <= tick - late < len(order):
                a = order[tick - late]
                state[a] = step(a, state[a])
    for a in order:
        g.finish(a, state[a])
    g.close()


def gather_all(shards):
    count = len(shards)
    dma = pltpu.SemaphoreType.DMA
    return pl.pallas_call(
        gather_kernel,
        out_shape=[jax.ShapeDtypeStruct((32 * s.shape[0],) + s.shape[1:], s.dtype) for s in shards],
        in_specs=[pl.BlockSpec(memory_space=pl.ANY)] * count,
        out_specs=[pl.BlockSpec(memory_space=pl.ANY)] * count,
        scratch_shapes=[
            dma((count, 3)), dma((count, 3)), dma((count, 2, 3)), dma((count, 2, 3)), dma((count, 4)), dma((count, 4)), dma((count,)),
        ],
        name="gather",
        compiler_params=pltpu.CompilerParams(collective_id=0, has_side_effects=True),
    )(*shards)


class Reduce:
    def __init__(self, parts, r0, r1, r2, r3, outs, sems):
        self.parts, self.r0, self.r1, self.r2, self.r3, self.outs = parts, r0, r1, r2, r3, outs
        self.d_send, self.d_recv, self.p_send, self.p_recv, self.z_send, self.z_recv = sems
        self.d, self.y, self.x, self.c, self.z = places()
        self.sideways, self.upward, self.sibling, self.along = peers_of(self.d, self.y, self.x, self.c, self.z)
        self.started = []

    send = Gather.send

    def halves(self, a):
        width = self.outs[a].shape[2]
        if width == 128:
            return ((0, 128),)
        return ((0, width // 2), (width // 2, width // 2))

    def add(self, count, into, into_at, other, other_at, cols):
        cols = pl.ds(*cols)

        def one(i, carry):
            into[into_at + i, :, cols] = (
                into[into_at + i, :, cols].astype(jnp.float32) + other[other_at + i, :, cols].astype(jnp.float32)
            ).astype(into.dtype)
            return carry

        lax.fori_loop(0, count, one, 0)

    def begin(self, a):
        rows = self.outs[a].shape[0]
        copies = []
        for g in range(4):
            src = self.parts[a].at[pl.ds((g * 2 + 1 - self.c) * 4 * rows, 4 * rows)]
            dst = self.r0[a].at[pl.ds(g * 4 * rows, 4 * rows)]
            copies.append(self.send(src, dst, self.d_send.at[a, g], self.d_recv.at[a, g], self.sibling))
        return copies

    def first(self, a, copies):
        rows = self.outs[a].shape[0]
        width = self.outs[a].shape[2]
        for g in range(4):
            copies[g].wait_recv()
            self.add(4 * rows, self.r0[a], g * 4 * rows, self.parts[a], (g * 2 + self.c) * 4 * rows, (0, width))
        sent = []
        for h, cols in enumerate(self.halves(a)):
            pair = []
            for i in range(2):
                g = (1 - self.y) * 2 + i if h == 0 else i * 2 + 1 - self.x
                src = self.r0[a].at[pl.ds(g * 4 * rows, 4 * rows), :, pl.ds(*cols)]
                dst = self.r1[a].at[pl.ds(i * 4 * rows, 4 * rows), :, pl.ds(*cols)]
                peer = self.upward if h == 0 else self.sideways
                pair.append(self.send(src, dst, self.p_send.at[a, h, i], self.p_recv.at[a, h, i], peer))
            sent.append(pair)
        return sent

    def second(self, a, sent):
        rows = self.outs[a].shape[0]
        onward = []
        for h, cols in enumerate(self.halves(a)):
            for i in range(2):
                sent[h][i].wait_recv()
                g = self.y * 2 + i if h == 0 else i * 2 + self.x
                self.add(4 * rows, self.r1[a], i * 4 * rows, self.r0[a], g * 4 * rows, cols)
            far = 1 - self.x if h == 0 else 1 - self.y
            peer = self.sideways if h == 0 else self.upward
            src = self.r1[a].at[pl.ds(far * 4 * rows, 4 * rows), :, pl.ds(*cols)]
            dst = self.r2[a].at[:, :, pl.ds(*cols)]
            onward.append(self.send(src, dst, self.p_send.at[a, h, 2], self.p_recv.at[a, h, 2], peer))
        return onward

    def third(self, a, onward):
        rows = self.outs[a].shape[0]
        for h, cols in enumerate(self.halves(a)):
            onward[h].wait_recv()
            near = self.x if h == 0 else self.y
            self.add(4 * rows, self.r2[a], 0, self.r1[a], near * 4 * rows, cols)
        along = []
        for k in range(3):
            to = lax.rem(self.z + k + 1, 4)
            src = self.r2[a].at[pl.ds(to * rows, rows)]
            dst = self.r3[a].at[pl.ds(k * rows, rows)]
            along.append(self.send(src, dst, self.z_send.at[a, k], self.z_recv.at[a, k], self.along[k]))
        return along

    def finish(self, a, along):
        rows = self.outs[a].shape[0]
        for copy in along:
            copy.wait_recv()

        def one(i, carry):
            total = self.r2[a][self.z * rows + i].astype(jnp.float32)
            for k in range(3):
                total = total + self.r3[a][k * rows + i].astype(jnp.float32)
            self.outs[a][i] = total
            return carry

        lax.fori_loop(0, rows, one, 0)

    def close(self):
        for copy in self.started:
            copy.wait_send()


def reduce_kernel(count, *refs):
    parts, outs = refs[:count], refs[count : 2 * count]
    r0, r1, r2, r3 = (refs[(2 + k) * count : (3 + k) * count] for k in range(4))
    g = Reduce(parts, r0, r1, r2, r3, outs, refs[6 * count :])
    greet([g.sideways, g.upward, g.sibling, *g.along])
    order = range(count)
    state = {a: g.begin(a) for a in order}
    steps = (g.first, g.second, g.third, g.finish)
    for tick in range(len(order) + len(steps) - 1):
        for late, step in enumerate(steps):
            if 0 <= tick - late < len(order):
                a = order[tick - late]
                state[a] = step(a, state[a])
    g.close()


def reduce_all(parts):
    count = len(parts)
    dma = pltpu.SemaphoreType.DMA
    scratch = []
    for blocks in (16, 8, 4, 3):
        scratch += [pltpu.VMEM((p.shape[0] // 32 * blocks,) + p.shape[1:], p.dtype) for p in parts]
    return pl.pallas_call(
        functools.partial(reduce_kernel, count),
        out_shape=[jax.ShapeDtypeStruct((p.shape[0] // 32,) + p.shape[1:], jnp.float32) for p in parts],
        in_specs=[pl.BlockSpec(memory_space=pltpu.VMEM)] * count,
        out_specs=[pl.BlockSpec(memory_space=pltpu.VMEM)] * count,
        scratch_shapes=scratch + [
            dma((count, 4)), dma((count, 4)), dma((count, 2, 3)), dma((count, 2, 3)), dma((count, 3)), dma((count, 3)),
        ],
        name="reduce",
        compiler_params=pltpu.CompilerParams(collective_id=1, has_side_effects=True, vmem_limit_bytes=56 << 20),
    )(*parts)


EPS = 1e-05
QB = 256
SCALE = HEAD_DIM ** (-0.5)
NT = (((1,), (1,)), ((), ()))


def dot(left, right):
    return jnp.dot(left, right, preferred_element_type=jnp.float32)


def dot_nt(left, right):
    return lax.dot_general(left, right, NT, preferred_element_type=jnp.float32)


def tiles(count, step):
    def one(i, carry):
        step(i)
        return carry

    lax.fori_loop(0, count, one, 0)


def at(i, size):
    return pl.ds(pl.multiple_of(i * size, size), size)


def weight_columns(w, i, size):
    block = w[:, :, at(i, size)]
    return block.reshape(block.shape[0] * 8, size)


def weight_rows(w, i, size):
    block = w[pl.ds(i * (size // 8), size // 8)]
    return block.reshape(size, block.shape[2])


def normal(u):
    center = u - jnp.mean(u, -1, keepdims=True)
    spread = lax.rsqrt(jnp.mean(center * center, -1, keepdims=True) + EPS)
    return center * spread, spread


def norm_rows(u_ref, gain, out_ref):
    def step(i):
        hat, spread = normal(u_ref[at(i, 128)].astype(jnp.float32))
        out_ref[at(i, 128)] = (hat * gain).astype(jnp.bfloat16)

    tiles(u_ref.shape[0] // 128, step)


def gelu_both(x):
    e = jnp.exp(x * x * -0.5)
    t = 1.0 / (1.0 + jnp.abs(x) * (0.3275911 * 0.5**0.5))
    poly = 0.5 * 1.061405429
    for term in (-1.453152027, 1.421413741, -0.284496736, 0.254829592):
        poly = poly * t + 0.5 * term
    tail = poly * t * e
    cdf = jnp.where(x >= 0, 1.0 - tail, tail)
    return x * cdf, cdf + x * e * (0.5 / math.pi) ** 0.5


def split_heads(block, axis):
    half = lax.broadcasted_iota(jnp.int32, block.shape, axis) < HEAD_DIM
    zero = jnp.zeros_like(block)
    return jnp.where(half, block, zero), jnp.where(half, zero, block)


def attend(qkvs, bias_ref, p_refs, rl_ref, o_ref, ot_ref):
    model = o_ref.shape[1]
    own = qkvs[-1]

    def step(pair):
        lanes = at(pair, 128)
        keys, values = [], []
        for ref in qkvs:
            keys.append(ref[:, pl.ds(pl.multiple_of(model + pair * 128, 128), 128)])
            values.append(ref[:, pl.ds(pl.multiple_of(2 * model + pair * 128, 128), 128)].T)
        for b in range(own.shape[0] // QB):
            span = (b + 1) * QB
            queries = split_heads(own[b * QB : span, lanes] * SCALE, 1)
            bias = bias_ref[:span, b * QB : span]
            halves = []
            for h in range(2):
                scores = [dot_nt(k[:span], queries[h]) + bias for k in keys]
                peak = jnp.max(scores[0], 0, keepdims=True)
                for s in scores[1:]:
                    peak = jnp.maximum(peak, jnp.max(s, 0, keepdims=True))
                total, out = None, None
                for n, s in enumerate(scores):
                    p = jnp.exp(s - peak)
                    part = jnp.sum(p, 0, keepdims=True)
                    p = p.astype(jnp.bfloat16)
                    p_refs[b][pair, h, n * span : (n + 1) * span] = p
                    product = dot(values[n][h * HEAD_DIM : (h + 1) * HEAD_DIM, :span], p)
                    total = part if total is None else total + part
                    out = product if out is None else out + product
                scale = 1.0 / total
                rl_ref[pair, h : h + 1, b * QB : span] = scale
                halves.append(out * scale)
            both = jnp.concatenate(halves, 0)
            ot_ref[at(pair, 128), b * QB : span] = both
            o_ref[b * QB : span, lanes] = both.astype(jnp.bfloat16).T

    tiles(model // 128, step)


def attend_back(qkvs, p_refs, do_ref, ot_ref, dqkv_ref, dkv_refs):
    model = do_ref.shape[0]
    own = qkvs[-1]

    def step(pair):
        lanes = at(pair, 128)
        rows = at(pair, 128)
        right = [pl.ds(pl.multiple_of(n * model + pair * 128, 128), 128) for n in range(3)]
        keys = [ref[:, right[1]] for ref in qkvs]
        values = [ref[:, right[2]] for ref in qkvs]
        turned = [k.T for k in keys]
        dk, dv = [None] * len(qkvs), [None] * len(qkvs)
        for b in reversed(range(own.shape[0] // QB)):
            span = (b + 1) * QB
            block = slice(b * QB, span)
            queries = split_heads(own[block, lanes] * SCALE, 1)
            do = do_ref[rows, block]
            do_down = split_heads(do, 0)
            do_across = split_heads(do.T, 1)
            product = do.astype(jnp.float32) * ot_ref[rows, block]
            dq = []
            for h in range(2):
                delta = jnp.sum(product[h * HEAD_DIM : (h + 1) * HEAD_DIM], 0, keepdims=True)
                dq_head = None
                for n in range(len(qkvs)):
                    p = p_refs[b][pair, h, n * span : (n + 1) * span]
                    ds = dot(values[n][:span], do_down[h]) - delta
                    ds = (p.astype(jnp.float32) * ds).astype(jnp.bfloat16)
                    more_dv, more_dk = dot(p, do_across[h]), dot(ds, queries[h])
                    more_dq = dot(turned[n][h * HEAD_DIM : (h + 1) * HEAD_DIM, :span], ds)
                    dq_head = more_dq if dq_head is None else dq_head + more_dq
                    if dk[n] is None:
                        dk[n], dv[n] = more_dk, more_dv
                    elif dk[n].shape[0] == span:
                        dk[n], dv[n] = dk[n] + more_dk, dv[n] + more_dv
                    else:
                        dk[n] = jnp.concatenate([dk[n][:span] + more_dk, dk[n][span:]], 0)
                        dv[n] = jnp.concatenate([dv[n][:span] + more_dv, dv[n][span:]], 0)
                dq.append(dq_head)
            dq = (jnp.concatenate(dq, 0) * SCALE).astype(jnp.bfloat16)
            dqkv_ref[block, lanes] = dq.T
        for n, ref in enumerate(dkv_refs):
            if ref is not None and n < len(qkvs) - 1:
                ref[:, lanes] = dk[n]
                ref[:, right[1]] = dv[n]
        extra = dkv_refs[-1]
        dk, dv = dk[-1], dv[-1]
        if extra is not None:
            dk, dv = dk + extra[:, lanes], dv + extra[:, right[1]]
        dqkv_ref[:, right[1]] = dk.astype(jnp.bfloat16)
        dqkv_ref[:, right[2]] = dv.astype(jnp.bfloat16)

    tiles(model // 128, step)


def project(left_ref, w, add_ref, out_ref, shift=None, size=256):
    def step(i):
        value = dot(left_ref[...], weight_columns(w, i, size))
        if add_ref is not None:
            value = add_ref[:, at(i, size)].astype(jnp.float32) + value
        if shift is not None:
            value = value + shift[:, at(i, size)]
        out_ref[:, at(i, size)] = value.astype(out_ref.dtype)

    tiles(w.shape[2] // size, step)


def project_back(left_ref, w, out_ref, size=256):
    def step(i):
        out_ref[:, at(i, size)] = dot_nt(left_ref[...], weight_rows(w, i, size)).astype(out_ref.dtype)

    tiles(w.shape[0] * 8 // size, step)


def forward_pass(u_ref, qkv_before, bias_ref, gains, w, keep, out_ref, shift, ready):
    norm_rows(u_ref, gains[0], keep["a"])
    turn(keep["a"], keep["at"])
    ready("qkv")
    project(keep["a"], w["qkv"], None, keep["qkv"])
    qkvs = [keep["qkv"]] if qkv_before is None else [qkv_before, keep["qkv"]]
    attend(qkvs, bias_ref, keep["p"], keep["rl"], keep["o"], keep["ot"])
    ready("out")
    project(keep["o"], w["out"], u_ref, keep["m"])
    norm_rows(keep["m"], gains[1], keep["b"])
    turn(keep["b"], keep["bt"])
    ready("up")

    def step(i):
        hidden = dot(keep["b"][...], weight_columns(w["up"], i, 256))
        active, slope = gelu_both(hidden)
        active = active.astype(jnp.bfloat16)
        keep["f"][:, at(i, 256)] = active
        keep["ft"][at(i, 256)] = active.T
        keep["gp"][:, at(i, 256)] = slope.astype(jnp.bfloat16)

    tiles(w["up"].shape[2] // 256, step)
    ready("down")
    project(keep["f"], w["down"], keep["m"], out_ref, shift)


def norm_back(u_ref, gain, dy_ref, add_ref, out_ref, rounded_ref, gain_grad_ref, sum_ref=None):
    def step(i, totals):
        total, whole = totals
        hat, spread = normal(u_ref[at(i, 128)].astype(jnp.float32))
        dy = dy_ref[at(i, 128)]
        total = total + jnp.sum((dy * hat).reshape(16, 8, dy.shape[1]), 0)
        dy = dy * gain
        down = dy - jnp.mean(dy, -1, keepdims=True) - hat * jnp.mean(dy * hat, -1, keepdims=True)
        value = add_ref[at(i, 128)].astype(jnp.float32) + spread * down
        out_ref[at(i, 128)] = value
        if rounded_ref is not None:
            rounded_ref[at(i, 128)] = value.astype(jnp.bfloat16)
        if sum_ref is not None:
            whole = whole + jnp.sum(value.reshape(16, 8, dy.shape[1]), 0)
        return total, whole

    zero = jnp.zeros((8, u_ref.shape[1]), jnp.float32)
    total, whole = lax.fori_loop(0, u_ref.shape[0] // 128, step, (zero, zero))
    gain_grad_ref[...] = jnp.broadcast_to(jnp.sum(total, 0, keepdims=True), gain_grad_ref.shape)
    if sum_ref is not None:
        sum_ref[...] = jnp.broadcast_to(jnp.sum(whole, 0, keepdims=True), sum_ref.shape)


def staged(before, count, piece, stage, sems):
    def copy(i):
        slot = lax.rem(i, 2)
        return pltpu.make_async_copy(piece(before, i), stage.at[slot], sems.at[slot])

    copy(0).start()

    def take(i):
        @pl.when(i + 1 < count)
        def _():
            copy(i + 1).start()

        copy(i).wait()
        return stage[lax.rem(i, 2)].astype(jnp.float32)

    return take


def weight_grad(turned_ref, right_ref, out_ref, before, stages, size=256):
    count = right_ref.shape[1] // size
    if before is not None:
        take = staged(before, count, lambda ref, i: ref.at[:, :, at(i, size)], stages[0], stages[2])

    def step(i):
        value = dot(turned_ref[...].astype(jnp.bfloat16), right_ref[:, at(i, size)])
        value = value.reshape(value.shape[0] // 8, 8, size)
        if before is not None:
            value = value + take(i)
        out_ref[:, :, at(i, size)] = value.astype(out_ref.dtype)

    tiles(count, step)


def turn(ref, out_ref):
    def step(i):
        out_ref[at(i, 256)] = ref[:, at(i, 256)].T

    tiles(ref.shape[1] // 256, step)


def down_grad(ft_ref, dz_ref, out_ref, before, stages, size=256):
    count = ft_ref.shape[0] // size
    if before is not None:
        take = staged(before, count, lambda ref, i: ref.at[pl.ds(i * (size // 8), size // 8)], stages[1], stages[2])

    def step(i):
        value = dot(ft_ref[at(i, size)], dz_ref[...])
        value = value.reshape(size // 8, 8, value.shape[1])
        if before is not None:
            value = value + take(i)
        out_ref[pl.ds(i * (size // 8), size // 8)] = value.astype(out_ref.dtype)

    tiles(count, step)


def backward_pass(up_ref, u_ref, qkvs, dkv_refs, gains, w, keep, work, before, stages, du_ref, gain_grads, sum_ref, ready, done):
    before = before or dict.fromkeys(NAMES)
    dz = up_ref
    if up_ref.dtype != jnp.bfloat16:
        dz = work["dz"]

        def cast(i):
            dz[at(i, 128)] = up_ref[at(i, 128)].astype(jnp.bfloat16)

        tiles(up_ref.shape[0] // 128, cast)
    ready("down")
    dhid = work["dhid"]

    def step(i):
        value = dot_nt(dz[...], weight_rows(w["down"], i, 256)) * keep["gp"][:, at(i, 256)].astype(jnp.float32)
        dhid[:, at(i, 256)] = value.astype(jnp.bfloat16)

    tiles(w["down"].shape[0] * 8 // 256, step)
    down_grad(keep["ft"], dz, w["down"], before["down"], stages)
    done("down")
    ready("up")
    project_back(dhid, w["up"], work["dm"])
    weight_grad(keep["bt"], dhid, w["up"], before["up"], stages)
    done("up")
    norm_back(keep["m"], gains[1], work["dm"], up_ref, work["dm"], work["da"], gain_grads[1])
    ready("out")

    def head_grads(i):
        value = dot_nt(weight_rows(w["out"], i, 256), work["da"][...])
        scale = [jnp.broadcast_to(keep["rl"][2 * i + n // 2, n % 2 : n % 2 + 1], (HEAD_DIM, value.shape[1])) for n in range(4)]
        work["do"][at(i, 256)] = (value * jnp.concatenate(scale, 0)).astype(jnp.bfloat16)

    tiles(w["out"].shape[0] * 8 // 256, head_grads)
    weight_grad(keep["ot"], work["da"], w["out"], before["out"], stages)
    done("out")
    attend_back(qkvs, keep["p"], work["do"], keep["ot"], work["dqkv"], dkv_refs)
    ready("qkv")
    project_back(work["dqkv"], w["qkv"], du_ref)
    weight_grad(keep["at"], work["dqkv"], w["qkv"], before["qkv"], stages)
    done("qkv")
    norm_back(u_ref, gains[0], du_ref, work["dm"], du_ref, None, gain_grads[0], sum_ref)


NAMES = ("qkv", "out", "up", "down")
KEPT = ("at", "qkv", "rl", "ot", "m", "bt", "ft", "gp")
LOCAL = ("a", "o", "b", "f")
WORK = ("dz", "da", "do", "dm", "dhid", "dqkv")


def shapes_of(length, model, hidden, passes):
    f32, bf16 = jnp.float32, jnp.bfloat16
    shape = jax.ShapeDtypeStruct
    pairs = model // 128
    table = {
        "a": shape((length, model), bf16),
        "at": shape((model, length), bf16),
        "qkv": shape((length, 3 * model), bf16),
        "rl": shape((pairs, 2, length), f32),
        "o": shape((length, model), bf16),
        "ot": shape((model, length), f32),
        "m": shape((length, model), f32),
        "b": shape((length, model), bf16),
        "bt": shape((model, length), bf16),
        "f": shape((length, hidden), bf16),
        "ft": shape((hidden, length), bf16),
        "gp": shape((length, hidden), bf16),
        "dz": shape((length, model), bf16),
        "da": shape((length, model), bf16),
        "do": shape((model, length), bf16),
        "dm": shape((length, model), f32),
        "dhid": shape((length, hidden), bf16),
        "dqkv": shape((length, 3 * model), bf16),
    }
    p = [shape((pairs, 2, passes * (b + 1) * QB, QB), bf16) for b in range(length // QB)]
    return table, p


def scratch_of(shapes):
    return [pltpu.VMEM(s.shape, s.dtype) for s in shapes]


def weight_copies(hbm, vmem, sems, back=False):
    ends = lambda n: (vmem[n], hbm[n]) if back else (hbm[n], vmem[n])
    return {n: pltpu.make_async_copy(*ends(n), sems.at[i]) for i, n in enumerate(NAMES)}


def forward_kernel(passes, blocks, *refs):
    it = iter(refs)
    u = next(it)
    before = next(it) if passes == 2 else None
    bias, vectors = next(it), next(it)
    hbm = {n: next(it) for n in NAMES}
    out = next(it)
    keep = {n: next(it) for n in KEPT}
    keep["p"] = [next(it) for _ in range(blocks)]
    keep.update({n: next(it) for n in LOCAL})
    w = {n: next(it) for n in NAMES}
    copies = weight_copies(hbm, w, next(it))
    for n in NAMES:
        copies[n].start()
    gains = [vectors[n : n + 1] for n in (1, 2)]
    shift = vectors.at[0:1] if passes == 1 else None
    forward_pass(u, before, bias, gains, w, keep, out, shift, lambda n: copies[n].wait())


VMEM_LIMIT = 62 << 20


def run_forward(u, before, bias, vectors, weights, out_dtype):
    length, model = u.shape
    passes = 1 if before is None else 2
    table, p = shapes_of(length, model, weights["up"].shape[2], passes)
    vmem, anywhere = pl.BlockSpec(memory_space=pltpu.VMEM), pl.BlockSpec(memory_space=pl.ANY)
    inputs = [u] + ([] if before is None else [before]) + [bias, vectors]
    out_shape = [jax.ShapeDtypeStruct((length, model), out_dtype)] + [table[n] for n in KEPT] + p
    outs = pl.pallas_call(
        functools.partial(forward_kernel, passes, len(p)),
        out_shape=out_shape,
        in_specs=[vmem] * len(inputs) + [anywhere] * 4,
        out_specs=[vmem] * len(out_shape),
        scratch_shapes=scratch_of([table[n] for n in LOCAL] + [weights[n] for n in NAMES]) + [pltpu.SemaphoreType.DMA((4,))],
        name="forward%d" % passes,
        compiler_params=pltpu.CompilerParams(vmem_limit_bytes=VMEM_LIMIT),
    )(*inputs, *(weights[n] for n in NAMES))
    keep = dict(zip(KEPT, outs[1:]))
    keep["p"] = list(outs[1 + len(KEPT) :])
    return outs[0], keep


def backward_kernel(passes, blocks, with_before, *refs):
    it = iter(refs)
    up, u = next(it), next(it)
    other = next(it)
    vectors = next(it)
    keep = {n: next(it) for n in KEPT}
    keep["p"] = [next(it) for _ in range(blocks)]
    hbm = {n: next(it) for n in NAMES}
    before = {n: next(it) for n in NAMES} if with_before else None
    du, ln1, ln2, whole = next(it), next(it), next(it), next(it)
    dkv = next(it) if passes == 2 else None
    grads = {n: next(it) for n in NAMES}
    w = {n: next(it) for n in NAMES}
    work = {n: next(it) for n in WORK}
    loads, stores = weight_copies(hbm, w, next(it)), weight_copies(grads, w, next(it), back=True)
    stages = [next(it), next(it), next(it)] if with_before else None
    for n in reversed(NAMES):
        loads[n].start()
    gains = [vectors[n : n + 1] for n in (1, 2)]
    qkvs, dkvs = ([keep["qkv"]], [other]) if passes == 1 else ([other, keep["qkv"]], [dkv, None])
    backward_pass(
        up, u, qkvs, dkvs, gains, w, keep, work, before, stages, du, (ln1, ln2), whole,
        lambda n: loads[n].wait(), lambda n: stores[n].start(),
    )
    for n in NAMES:
        stores[n].wait()


def run_backward(up, u, other, vectors, keep, weights, before, passes):
    length, model = u.shape
    f32, bf16 = jnp.float32, jnp.bfloat16
    shape = jax.ShapeDtypeStruct
    table, p = shapes_of(length, model, weights["up"].shape[2], passes)
    vmem, anywhere = pl.BlockSpec(memory_space=pltpu.VMEM), pl.BlockSpec(memory_space=pl.ANY)
    inputs = [up, u, other, vectors] + [keep[n] for n in KEPT] + keep["p"]
    far = [weights[n] for n in NAMES] + ([] if before is None else [before[n] for n in NAMES])
    out_shape = [shape((length, model), f32)] + [shape((8, model), f32)] * 3
    if passes == 2:
        out_shape.append(shape((length, 2 * model), f32))
    near = len(out_shape)
    out_shape += [shape(weights[n].shape, bf16) for n in NAMES]
    scratch = scratch_of([weights[n] for n in NAMES] + [table[n] for n in WORK])
    scratch += [pltpu.SemaphoreType.DMA((4,)), pltpu.SemaphoreType.DMA((4,))]
    if before is not None:
        scratch += [
            pltpu.VMEM((2, model // 8, 8, 256), bf16),
            pltpu.VMEM((2, 32, 8, model), bf16),
            pltpu.SemaphoreType.DMA((2,)),
        ]
    outs = pl.pallas_call(
        functools.partial(backward_kernel, passes, len(p), before is not None),
        out_shape=out_shape,
        in_specs=[vmem] * len(inputs) + [anywhere] * len(far),
        out_specs=[vmem] * near + [anywhere] * 4,
        scratch_shapes=scratch,
        name="backward%d" % passes,
        compiler_params=pltpu.CompilerParams(vmem_limit_bytes=VMEM_LIMIT),
    )(*inputs, *far)
    return outs[:near], dict(zip(NAMES, outs[near:]))


AXES = ("dp", "fsdp")


def cut(w):
    return w.reshape(w.shape[0] // 8, 8, w.shape[1])


def join(w):
    return w.reshape(w.shape[0] * 8, w.shape[2])


def gather_weights(near, vectors, shards):
    if not near:
        vectors = [lax.all_gather(v, AXES, axis=0, tiled=True) for v in vectors]
        weights = {n: cut(lax.all_gather(shards[n], AXES, axis=0, tiled=True)) for n in NAMES}
        return jnp.stack(vectors).astype(jnp.float32), weights
    rows = vectors[0].shape[0]
    small = jnp.zeros((1, 8, 128), jnp.bfloat16).at[0, :3, :rows].set(jnp.stack(vectors))
    small, *wholes = gather_all([small] + [cut(shards[n]) for n in ("out", "qkv", "up", "down")])
    vectors = small[:, :3, :rows].transpose(1, 0, 2).reshape(3, 32 * rows)
    return vectors.astype(jnp.float32), dict(zip(("out", "qkv", "up", "down"), wholes))


def reduce_grads(near, vectors, grads):
    if not near:
        vectors = [lax.psum_scatter(v, AXES, scatter_dimension=0, tiled=True) for v in vectors]
        return vectors, {n: lax.psum_scatter(join(grads[n]).astype(jnp.float32), AXES, scatter_dimension=0, tiled=True) for n in NAMES}
    rows = vectors[0].shape[0] // 32
    small = jnp.stack(vectors).reshape(3, 32, rows).transpose(1, 0, 2)
    small = jnp.zeros((32, 8, 128), jnp.bfloat16).at[:, :3, :rows].set(small.astype(jnp.bfloat16))
    order = ("down", "up", "out", "qkv")
    *sums, small = reduce_all([grads[n] for n in order] + [small])
    return [small[0, n, :rows] for n in range(3)], {n: join(s) for n, s in zip(order, sums)}


def body(near, tokens, doc_ids, pass_embed, ln1_gain, w_qkv, w_out, ln2_gain, w_up, w_down, cotangent):
    shards = {"qkv": w_qkv, "out": w_out, "up": w_up, "down": w_down}
    vectors, weights = gather_weights(near, (pass_embed, ln1_gain, ln2_gain), shards)
    vectors = jnp.pad(vectors, ((0, 5), (0, 0)))
    length = tokens.shape[0]
    at_ = jnp.arange(length, dtype=jnp.int32)
    allowed = (doc_ids[:, None] == doc_ids[None, :]) & (at_[:, None] <= at_[None, :])
    bias = jnp.where(allowed, 0.0, -1e30).astype(jnp.float32)
    second_in, kept1 = run_forward(tokens, None, bias, vectors, weights, jnp.float32)
    layer_out, kept2 = run_forward(second_in, kept1["qkv"], bias, vectors, weights, jnp.bfloat16)
    (second_g, late1, late2, embed_g, dkv), late = run_backward(
        cotangent, second_in, kept1["qkv"], vectors, kept2, weights, None, 2
    )
    (tokens_grad, early1, early2, _), grads = run_backward(second_g, tokens, dkv, vectors, kept1, weights, late, 1)
    small, sums = reduce_grads(near, (embed_g[0], late1[0] + early1[0], late2[0] + early2[0]), grads)
    return (layer_out, tokens_grad, small[0], small[1], sums["qkv"], sums["out"], small[2], sums["up"], sums["down"])


def solution(mesh):
    near = dict(mesh.shape) == {"dp": 8, "fsdp": 4}
    placed = (
        P(("dp", "fsdp"), None),
        P(("dp", "fsdp")),
        P(("dp", "fsdp")),
        P(("dp", "fsdp")),
        P(("dp", "fsdp"), None),
        P(("dp", "fsdp"), None),
        P(("dp", "fsdp")),
        P(("dp", "fsdp"), None),
        P(("dp", "fsdp"), None),
        P(("dp", "fsdp"), None),
    )
    return jax.shard_map(
        functools.partial(body, near),
        mesh=mesh,
        in_specs=placed,
        out_specs=(
            P(("dp", "fsdp"), None),
            P(("dp", "fsdp"), None),
            P(("dp", "fsdp")),
            P(("dp", "fsdp")),
            P(("dp", "fsdp"), None),
            P(("dp", "fsdp"), None),
            P(("dp", "fsdp")),
            P(("dp", "fsdp"), None),
            P(("dp", "fsdp"), None),
        ),
        check_vma=False,
    )
```

```python
import functools
import math

import jax
import jax.numpy as jnp
from jax import lax
from jax.experimental import pallas as pl
from jax.experimental.pallas import tpu as pltpu
from jax.sharding import PartitionSpec as P

HEAD_DIM = 64


MESH = pl.DeviceIdType.MESH
NAMES = ("qkv", "out", "up", "down")


def pieces(width, parts):
    count = width // 128 // parts
    result = []
    for n in range(parts):
        first = (count + 1 - n % 2) // 2
        start = n * count * 128
        result.append(((start, first * 128), (start + first * 128, (count - first) * 128)))
    return result


class Links:
    def __init__(self, chunks, depth):
        d, z = lax.axis_index("dp"), lax.axis_index("fsdp")
        y, x, c = d // 4, lax.rem(d // 2, 2), lax.rem(d, 2)
        self.d, self.z, self.y, self.x, self.c = d, z, y, x, c
        self.sideways = (y * 4 + (1 - x) * 2 + c, z)
        self.upward = ((1 - y) * 4 + x * 2 + c, z)
        self.sibling = (y * 4 + x * 2 + 1 - c, z)
        self.along = [(d, lax.rem(z + k, 4)) for k in (1, 2, 3)]
        self.chunks, self.depth = chunks, depth

    def greet(self):
        peers = [self.sideways, self.upward, self.sibling, *self.along]
        barrier = pltpu.get_barrier_semaphore()
        for peer in peers:
            pl.semaphore_signal(barrier, inc=1, device_id=peer, device_id_type=MESH)
        pl.semaphore_wait(barrier, len(peers))

    def columns(self, n):
        halves = self.chunks[n][1]
        return pl.ds(halves[0][0], sum(size for _, size in halves))

    def rows(self, n):
        return self.depth[self.chunks[n][0]]

    def hops(self, h):
        return (self.sideways, self.upward) if h == 0 else (self.upward, self.sideways)


def remote(src, dst, send, recv, peer):
    return pltpu.make_async_remote_copy(
        src_ref=src, dst_ref=dst, send_sem=send, recv_sem=recv, device_id=peer, device_id_type=MESH
    )


def link_semaphores(count):
    dma = pltpu.SemaphoreType.DMA
    return [dma((count, 3)), dma((count, 3)), dma((count, 2, 3)), dma((count, 2, 3)), dma((count, 4)), dma((count, 4)), dma((count,))]


class Gather:
    def __init__(self, chunks, shards, wholes, sems):
        self.links = Links(chunks, {n: s.shape[0] for n, s in shards.items()})
        self.chunks, self.shards, self.wholes = chunks, shards, wholes
        self.z_send, self.z_recv, self.p_send, self.p_recv, self.d_send, self.d_recv, self.own_sem = sems

    def group(self, n, y, x, cols):
        rows = self.links.rows(n)
        return self.wholes[self.chunks[n][0]].at[pl.ds((y * 4 + x * 2 + self.links.c) * 4 * rows, 4 * rows), :, cols]

    def near(self, n):
        rows, cols = self.links.rows(n), self.links.columns(n)
        name = self.chunks[n][0]
        at = (self.links.d * 4 + self.links.z) * rows
        return self.shards[name].at[:, :, cols], self.wholes[name].at[pl.ds(at, rows), :, cols]

    def own(self, n):
        return pltpu.make_async_copy(*self.near(n), self.own_sem.at[n])

    def ahead(self, n, k):
        return remote(*self.near(n), self.z_send.at[n, k], self.z_recv.at[n, k], self.links.along[k])

    def hop(self, n, h, i):
        at = self.links
        one, two = at.hops(h)
        y, x = at.y, at.x
        if i == 2:
            y, x = (y, 1 - x) if h == 0 else (1 - y, x)
        block = self.group(n, y, x, pl.ds(*self.chunks[n][1][h]))
        return remote(block, block, self.p_send.at[n, h, i], self.p_recv.at[n, h, i], one if i == 0 else two)

    def share(self, n, g):
        at = self.links
        y, x = at.y, at.x
        block = self.group(n, 1 - y if g >= 2 else y, 1 - x if g % 2 else x, at.columns(n))
        return remote(block, block, self.d_send.at[n, g], self.d_recv.at[n, g], at.sibling)

    def halves(self, n):
        return range(len(self.chunks[n][1]))

    def step(self, what, n):
        if what == "begin":
            self.own(n).start()
            for k in range(3):
                self.ahead(n, k).start()
        elif what == "first":
            self.own(n).wait()
            for k in range(3):
                self.ahead(n, k).wait_recv()
            for h in self.halves(n):
                self.hop(n, h, 0).start()
                self.hop(n, h, 1).start()
            self.share(n, 0).start()
        elif what == "second":
            for h in self.halves(n):
                self.hop(n, h, 0).wait_recv()
                self.hop(n, h, 2).start()
        elif what == "third":
            for h in self.halves(n):
                self.hop(n, h, 1).wait_recv()
            self.share(n, 1).start()
            self.share(n, 2).start()
        elif what == "fourth":
            for h in self.halves(n):
                self.hop(n, h, 2).wait_recv()
            self.share(n, 3).start()
        elif what == "finish":
            for g in range(4):
                self.share(n, g).wait_recv()
        elif what == "close":
            for k in range(3):
                self.ahead(n, k).wait_send()
            for h in self.halves(n):
                for i in range(3):
                    self.hop(n, h, i).wait_send()
            for g in range(4):
                self.share(n, g).wait_send()


def staggered(count, ahead, stages):
    events = [("begin", n) for n in range(min(ahead, count))]
    for tick in range(count + len(stages) - 1):
        for late, what in enumerate(stages):
            if 0 <= tick - late < count:
                events.append((what, tick - late))
                if late == 0 and tick + ahead < count:
                    events.append(("begin", tick + ahead))
    return events


class Pump:
    def __init__(self, step, events):
        self.run, self.events, self.next = step, events, 0

    def take(self, count):
        taken = self.events[self.next : self.next + count]
        self.next += len(taken)
        return taken

    def until(self, *event):
        if event in self.events[self.next :]:
            for one in self.take(self.events.index(event) + 1 - self.next):
                self.run(*one)

    def rest(self):
        for one in self.take(len(self.events)):
            self.run(*one)

    def hook(self, loops, count):
        plan = [self.take(count * (i + 1) // loops - count * i // loops) for i in range(loops)]

        def at_step(i):
            for k, events in enumerate(plan):
                if events:

                    @pl.when(i == k)
                    def _(events=events):
                        for one in events:
                            self.run(*one)

        return at_step


class Reduce:
    def __init__(self, chunks, parts, r0, r1, r2, r3, outs, sems):
        self.links = Links(chunks, {n: s.shape[0] for n, s in outs.items()})
        self.chunks, self.parts, self.outs = chunks, parts, outs
        self.r0, self.r1, self.r2, self.r3 = r0, r1, r2, r3
        self.z_send, self.z_recv, self.p_send, self.p_recv, self.d_send, self.d_recv, _ = sems

    def share(self, n, g):
        at, name = self.links, self.chunks[n][0]
        span, cols = 4 * at.rows(n), at.columns(n)
        src = self.parts[name].at[pl.ds((g * 2 + 1 - at.c) * span, span), :, cols]
        dst = self.r0[name].at[pl.ds(g * span, span), :, cols]
        return remote(src, dst, self.d_send.at[n, g], self.d_recv.at[n, g], at.sibling)

    def hop(self, n, h, i):
        at, name = self.links, self.chunks[n][0]
        span, cols = 4 * at.rows(n), pl.ds(*self.chunks[n][1][h])
        two, one = at.hops(h)
        if i < 2:
            g = (1 - at.y) * 2 + i if h == 0 else i * 2 + 1 - at.x
            src = self.r0[name].at[pl.ds(g * span, span), :, cols]
            dst = self.r1[name].at[pl.ds(i * span, span), :, cols]
        else:
            far = 1 - at.x if h == 0 else 1 - at.y
            src = self.r1[name].at[pl.ds(far * span, span), :, cols]
            dst = self.r2[name].at[:, :, cols]
        return remote(src, dst, self.p_send.at[n, h, i], self.p_recv.at[n, h, i], one if i < 2 else two)

    def ahead(self, n, k):
        at, name = self.links, self.chunks[n][0]
        rows, cols = at.rows(n), at.columns(n)
        src = self.r2[name].at[pl.ds(lax.rem(at.z + k + 1, 4) * rows, rows), :, cols]
        dst = self.r3[name].at[pl.ds(k * rows, rows), :, cols]
        return remote(src, dst, self.z_send.at[n, k], self.z_recv.at[n, k], at.along[k])

    def add(self, count, into, into_at, other, other_at, cols):
        def one(i, carry):
            into[into_at + i, :, cols] = (
                into[into_at + i, :, cols].astype(jnp.float32) + other[other_at + i, :, cols].astype(jnp.float32)
            ).astype(into.dtype)
            return carry

        lax.fori_loop(0, count, one, 0)

    def halves(self, n):
        return range(len(self.chunks[n][1]))

    def step(self, what, n):
        at, name = self.links, self.chunks[n][0]
        rows = at.rows(n)
        span = 4 * rows
        if what == "begin":
            for g in range(4):
                self.share(n, g).start()
        elif what == "first":
            for g in range(4):
                self.share(n, g).wait_recv()
                self.add(span, self.r0[name], g * span, self.parts[name], (g * 2 + at.c) * span, at.columns(n))
            for h in self.halves(n):
                self.hop(n, h, 0).start()
                self.hop(n, h, 1).start()
        elif what == "second":
            for h in self.halves(n):
                cols = pl.ds(*self.chunks[n][1][h])
                for i in range(2):
                    self.hop(n, h, i).wait_recv()
                    g = at.y * 2 + i if h == 0 else i * 2 + at.x
                    self.add(span, self.r1[name], i * span, self.r0[name], g * span, cols)
                self.hop(n, h, 2).start()
        elif what == "third":
            for h in self.halves(n):
                cols = pl.ds(*self.chunks[n][1][h])
                self.hop(n, h, 2).wait_recv()
                self.add(span, self.r2[name], 0, self.r1[name], (at.x if h == 0 else at.y) * span, cols)
            for k in range(3):
                self.ahead(n, k).start()
        elif what == "finish":
            cols = at.columns(n)
            for k in range(3):
                self.ahead(n, k).wait_recv()

            def one(i, carry):
                total = self.r2[name][at.z * rows + i, :, cols].astype(jnp.float32)
                for k in range(3):
                    total = total + self.r3[name][k * rows + i, :, cols].astype(jnp.float32)
                self.outs[name][i, :, cols] = total
                return carry

            lax.fori_loop(0, rows, one, 0)
        elif what == "close":
            for g in range(4):
                self.share(n, g).wait_send()
            for h in self.halves(n):
                for i in range(3):
                    self.hop(n, h, i).wait_send()
            for k in range(3):
                self.ahead(n, k).wait_send()


EPS = 1e-05
QB = 256
SCALE = HEAD_DIM ** (-0.5)
NT = (((1,), (1,)), ((), ()))


def dot(left, right):
    return jnp.dot(left, right, preferred_element_type=jnp.float32)


def dot_nt(left, right):
    return lax.dot_general(left, right, NT, preferred_element_type=jnp.float32)


def tiles(count, step):
    def one(i, carry):
        step(i)
        return carry

    lax.fori_loop(0, count, one, 0)


def at(i, size):
    return pl.ds(pl.multiple_of(i * size, size), size)


def weight_columns(w, i, size):
    block = w[:, :, at(i, size)]
    return block.reshape(block.shape[0] * 8, size)


def weight_rows(w, i, size):
    block = w[pl.ds(i * (size // 8), size // 8)]
    return block.reshape(size, block.shape[2])


def normal(u):
    center = u - jnp.mean(u, -1, keepdims=True)
    spread = lax.rsqrt(jnp.mean(center * center, -1, keepdims=True) + EPS)
    return center * spread, spread


def norm_rows(u_ref, gain, out_ref):
    def step(i):
        hat, spread = normal(u_ref[at(i, 128)].astype(jnp.float32))
        out_ref[at(i, 128)] = (hat * gain).astype(jnp.bfloat16)

    tiles(u_ref.shape[0] // 128, step)


def gelu_both(x):
    e = jnp.exp(x * x * -0.5)
    t = 1.0 / (1.0 + jnp.abs(x) * (0.3275911 * 0.5**0.5))
    poly = 0.5 * 1.061405429
    for term in (-1.453152027, 1.421413741, -0.284496736, 0.254829592):
        poly = poly * t + 0.5 * term
    tail = poly * t * e
    cdf = jnp.where(x >= 0, 1.0 - tail, tail)
    return x * cdf, cdf + x * e * (0.5 / math.pi) ** 0.5


def split_heads(block, axis):
    half = lax.broadcasted_iota(jnp.int32, block.shape, axis) < HEAD_DIM
    zero = jnp.zeros_like(block)
    return jnp.where(half, block, zero), jnp.where(half, zero, block)


def attend(qkvs, bias_ref, p_refs, rl_ref, o_ref, ot_ref, hook=None):
    model = o_ref.shape[1]
    own = qkvs[-1]

    def step(pair):
        if hook is not None:
            hook(pair)
        lanes = at(pair, 128)
        keys, values = [], []
        for ref in qkvs:
            keys.append(ref[:, pl.ds(pl.multiple_of(model + pair * 128, 128), 128)])
            values.append(ref[:, pl.ds(pl.multiple_of(2 * model + pair * 128, 128), 128)].T)
        for b in range(own.shape[0] // QB):
            span = (b + 1) * QB
            queries = split_heads(own[b * QB : span, lanes] * SCALE, 1)
            bias = bias_ref[:span, b * QB : span]
            halves = []
            for h in range(2):
                scores = [dot_nt(k[:span], queries[h]) + bias for k in keys]
                peak = jnp.max(scores[0], 0, keepdims=True)
                for s in scores[1:]:
                    peak = jnp.maximum(peak, jnp.max(s, 0, keepdims=True))
                total, out = None, None
                for n, s in enumerate(scores):
                    p = jnp.exp(s - peak)
                    part = jnp.sum(p, 0, keepdims=True)
                    p = p.astype(jnp.bfloat16)
                    p_refs[b][pair, h, n * span : (n + 1) * span] = p
                    product = dot(values[n][h * HEAD_DIM : (h + 1) * HEAD_DIM, :span], p)
                    total = part if total is None else total + part
                    out = product if out is None else out + product
                scale = 1.0 / total
                rl_ref[pair, h : h + 1, b * QB : span] = scale
                halves.append(out * scale)
            both = jnp.concatenate(halves, 0)
            ot_ref[at(pair, 128), b * QB : span] = both
            o_ref[b * QB : span, lanes] = both.astype(jnp.bfloat16).T

    tiles(model // 128, step)


def attend_back(qkvs, p_refs, do_ref, ot_ref, dqkv_ref, dkv_refs, hook=None):
    model = do_ref.shape[0]
    own = qkvs[-1]

    def step(pair):
        if hook is not None:
            hook(pair)
        lanes = at(pair, 128)
        rows = at(pair, 128)
        right = [pl.ds(pl.multiple_of(n * model + pair * 128, 128), 128) for n in range(3)]
        keys = [ref[:, right[1]] for ref in qkvs]
        values = [ref[:, right[2]] for ref in qkvs]
        turned = [k.T for k in keys]
        dk, dv = [None] * len(qkvs), [None] * len(qkvs)
        for b in reversed(range(own.shape[0] // QB)):
            span = (b + 1) * QB
            block = slice(b * QB, span)
            queries = split_heads(own[block, lanes] * SCALE, 1)
            do = do_ref[rows, block]
            do_down = split_heads(do, 0)
            do_across = split_heads(do.T, 1)
            product = do.astype(jnp.float32) * ot_ref[rows, block]
            dq = []
            for h in range(2):
                delta = jnp.sum(product[h * HEAD_DIM : (h + 1) * HEAD_DIM], 0, keepdims=True)
                dq_head = None
                for n in range(len(qkvs)):
                    p = p_refs[b][pair, h, n * span : (n + 1) * span]
                    ds = dot(values[n][:span], do_down[h]) - delta
                    ds = (p.astype(jnp.float32) * ds).astype(jnp.bfloat16)
                    more_dv, more_dk = dot(p, do_across[h]), dot(ds, queries[h])
                    more_dq = dot(turned[n][h * HEAD_DIM : (h + 1) * HEAD_DIM, :span], ds)
                    dq_head = more_dq if dq_head is None else dq_head + more_dq
                    if dk[n] is None:
                        dk[n], dv[n] = more_dk, more_dv
                    elif dk[n].shape[0] == span:
                        dk[n], dv[n] = dk[n] + more_dk, dv[n] + more_dv
                    else:
                        dk[n] = jnp.concatenate([dk[n][:span] + more_dk, dk[n][span:]], 0)
                        dv[n] = jnp.concatenate([dv[n][:span] + more_dv, dv[n][span:]], 0)
                dq.append(dq_head)
            dq = (jnp.concatenate(dq, 0) * SCALE).astype(jnp.bfloat16)
            dqkv_ref[block, lanes] = dq.T
        for n, ref in enumerate(dkv_refs):
            if ref is not None and n < len(qkvs) - 1:
                ref[:, lanes] = dk[n]
                ref[:, right[1]] = dv[n]
        extra = dkv_refs[-1]
        dk, dv = dk[-1], dv[-1]
        if extra is not None:
            dk, dv = dk + extra[:, lanes], dv + extra[:, right[1]]
        dqkv_ref[:, right[1]] = dk.astype(jnp.bfloat16)
        dqkv_ref[:, right[2]] = dv.astype(jnp.bfloat16)

    tiles(model // 128, step)


def project(left_ref, w, add_ref, out_ref, shift=None, size=256):
    def step(i):
        value = dot(left_ref[...], weight_columns(w, i, size))
        if add_ref is not None:
            value = add_ref[:, at(i, size)].astype(jnp.float32) + value
        if shift is not None:
            value = value + shift[:, at(i, size)]
        out_ref[:, at(i, size)] = value.astype(out_ref.dtype)

    tiles(w.shape[2] // size, step)


def project_back(left_ref, w, out_ref, size=256):
    def step(i):
        out_ref[:, at(i, size)] = dot_nt(left_ref[...], weight_rows(w, i, size)).astype(out_ref.dtype)

    tiles(w.shape[0] * 8 // size, step)


def forward_pass(u_ref, qkv_before, bias_ref, gains, w, keep, out_ref, shift, ready, done=None, hook=None):
    done = done or (lambda *names: None)
    hook = hook or (lambda loops, count: None)
    norm_rows(u_ref, gains[0], keep["a"])
    turn(keep["a"], keep["at"])
    done("at")
    ready("qkv")
    project(keep["a"], w["qkv"], None, keep["qkv"])
    done("qkv")
    qkvs = [keep["qkv"]] if qkv_before is None else [qkv_before, keep["qkv"]]
    attend(qkvs, bias_ref, [keep["p0"], keep["p1"]], keep["rl"], keep["o"], keep["ot"], hook(6, 9))
    done("p0", "p1", "rl", "ot")
    ready("out")
    project(keep["o"], w["out"], u_ref, keep["m"])
    norm_rows(keep["m"], gains[1], keep["b"])
    turn(keep["b"], keep["bt"])
    done("m", "bt")
    ready("up")
    between = hook(12, 6)

    def step(i):
        if between is not None:
            between(i)
        hidden = dot(keep["b"][...], weight_columns(w["up"], i, 256))
        active, slope = gelu_both(hidden)
        active = active.astype(jnp.bfloat16)
        keep["f"][:, at(i, 256)] = active
        keep["ft"][at(i, 256)] = active.T
        keep["gp"][:, at(i, 256)] = slope.astype(jnp.bfloat16)

    tiles(w["up"].shape[2] // 256, step)
    done("ft", "gp")
    ready("down")
    project(keep["f"], w["down"], keep["m"], out_ref, shift)


def norm_back(u_ref, gain, dy_ref, add_ref, out_ref, rounded_ref, gain_grad_ref, sum_ref=None):
    def step(i, totals):
        total, whole = totals
        hat, spread = normal(u_ref[at(i, 128)].astype(jnp.float32))
        dy = dy_ref[at(i, 128)]
        total = total + jnp.sum((dy * hat).reshape(16, 8, dy.shape[1]), 0)
        dy = dy * gain
        down = dy - jnp.mean(dy, -1, keepdims=True) - hat * jnp.mean(dy * hat, -1, keepdims=True)
        value = add_ref[at(i, 128)].astype(jnp.float32) + spread * down
        out_ref[at(i, 128)] = value
        if rounded_ref is not None:
            rounded_ref[at(i, 128)] = value.astype(jnp.bfloat16)
        if sum_ref is not None:
            whole = whole + jnp.sum(value.reshape(16, 8, dy.shape[1]), 0)
        return total, whole

    zero = jnp.zeros((8, u_ref.shape[1]), jnp.float32)
    total, whole = lax.fori_loop(0, u_ref.shape[0] // 128, step, (zero, zero))
    gain_grad_ref[...] = jnp.broadcast_to(jnp.sum(total, 0, keepdims=True), gain_grad_ref.shape)
    if sum_ref is not None:
        sum_ref[...] = jnp.broadcast_to(jnp.sum(whole, 0, keepdims=True), sum_ref.shape)


def staged(before, count, piece, stage, sems):
    def copy(i):
        slot = lax.rem(i, 2)
        return pltpu.make_async_copy(piece(before, i), stage.at[slot], sems.at[slot])

    copy(0).start()

    def take(i):
        @pl.when(i + 1 < count)
        def _():
            copy(i + 1).start()

        copy(i).wait()
        return stage[lax.rem(i, 2)].astype(jnp.float32)

    return take


def weight_grad(turned_ref, right_ref, out_ref, before, stages, size=256):
    count = right_ref.shape[1] // size
    if before is not None:
        take = staged(before, count, lambda ref, i: ref.at[:, :, at(i, size)], stages[0], stages[2])

    def step(i):
        value = dot(turned_ref[...].astype(jnp.bfloat16), right_ref[:, at(i, size)])
        value = value.reshape(value.shape[0] // 8, 8, size)
        if before is not None:
            value = value + take(i)
        out_ref[:, :, at(i, size)] = value.astype(out_ref.dtype)

    tiles(count, step)


def turn(ref, out_ref):
    def step(i):
        out_ref[at(i, 256)] = ref[:, at(i, 256)].T

    tiles(ref.shape[1] // 256, step)


def down_grad(ft_ref, dz_ref, out_ref, before, stages, size=256):
    count = ft_ref.shape[0] // size
    if before is not None:
        take = staged(before, count, lambda ref, i: ref.at[pl.ds(i * (size // 8), size // 8)], stages[1], stages[2])

    def step(i):
        value = dot(ft_ref[at(i, size)], dz_ref[...])
        value = value.reshape(size // 8, 8, value.shape[1])
        if before is not None:
            value = value + take(i)
        out_ref[pl.ds(i * (size // 8), size // 8)] = value.astype(out_ref.dtype)

    tiles(count, step)


def backward_pass(up_ref, u_ref, qkvs, dkv_refs, gains, w, keep, work, before, stages, du_ref, gain_grads, sum_ref, ready, done, hook=None):
    before = before or dict.fromkeys(NAMES)
    dz = up_ref
    if up_ref.dtype != jnp.bfloat16:
        dz = work["dz"]

        def cast(i):
            dz[at(i, 128)] = up_ref[at(i, 128)].astype(jnp.bfloat16)

        ready("upstream")
        tiles(up_ref.shape[0] // 128, cast)
    ready("down")
    dhid = work["dhid"]

    def step(i):
        value = dot_nt(dz[...], weight_rows(w["down"], i, 256)) * keep["gp"][:, at(i, 256)].astype(jnp.float32)
        dhid[:, at(i, 256)] = value.astype(jnp.bfloat16)

    tiles(w["down"].shape[0] * 8 // 256, step)
    ready("ft")
    down_grad(keep["ft"], dz, w["down"], before["down"], stages)
    done("down")
    ready("up")
    project_back(dhid, w["up"], work["dm"])
    done("hidden")
    weight_grad(keep["bt"], dhid, w["up"], before["up"], stages)
    done("up")
    norm_back(keep["m"], gains[1], work["dm"], up_ref, work["dm"], work["da"], gain_grads[1])
    done("norm")
    ready("out")

    def head_grads(i):
        value = dot_nt(weight_rows(w["out"], i, 256), work["da"][...])
        scale = [jnp.broadcast_to(keep["rl"][2 * i + n // 2, n % 2 : n % 2 + 1], (HEAD_DIM, value.shape[1])) for n in range(4)]
        work["do"][at(i, 256)] = (value * jnp.concatenate(scale, 0)).astype(jnp.bfloat16)

    tiles(w["out"].shape[0] * 8 // 256, head_grads)
    weight_grad(keep["ot"], work["da"], w["out"], before["out"], stages)
    done("out")
    ready("attention")
    attend_back(qkvs, [keep["p0"], keep["p1"]], work["do"], keep["ot"], work["dqkv"], dkv_refs, hook)
    done("dkv")
    ready("qkv")
    project_back(work["dqkv"], w["qkv"], du_ref)
    weight_grad(keep["at"], work["dqkv"], w["qkv"], before["qkv"], stages)
    done("qkv")
    norm_back(u_ref, gains[0], du_ref, work["dm"], du_ref, None, gain_grads[0], sum_ref)


KEPT = ("at", "qkv", "rl", "ot", "m", "bt", "ft", "gp", "p0", "p1")
LOCAL = ("a", "o", "b", "f")
VMEM_LIMIT = 63 << 20
VMEM = pl.BlockSpec(memory_space=pltpu.VMEM)
FAR = pl.BlockSpec(memory_space=pl.ANY)


def shapes_of(length, model, hidden, passes):
    f32, bf16 = jnp.float32, jnp.bfloat16
    shape = jax.ShapeDtypeStruct
    pairs = model // 128
    table = {
        "a": shape((length, model), bf16),
        "at": shape((model, length), bf16),
        "qkv": shape((length, 3 * model), bf16),
        "rl": shape((pairs, 2, length), f32),
        "o": shape((length, model), bf16),
        "ot": shape((model, length), f32),
        "m": shape((length, model), f32),
        "b": shape((length, model), bf16),
        "bt": shape((model, length), bf16),
        "f": shape((length, hidden), bf16),
        "ft": shape((hidden, length), bf16),
        "gp": shape((length, hidden), bf16),
        "dz": shape((length, model), bf16),
        "do": shape((model, length), bf16),
        "dm": shape((length, model), f32),
        "dqkv": shape((length, 3 * model), bf16),
        "dkv": shape((length, 2 * model), f32),
        "bias": shape((length, length), f32),
        "u": shape((length, model), f32),
        "vectors": shape((8, model), f32),
    }
    for b in range(length // QB):
        table["p%d" % b] = shape((pairs, 2, passes * (b + 1) * QB, QB), bf16)
    return table


class Room:
    def __init__(self):
        self.names, self.shapes, self.moves = [], [], []

    def scratch(self, **shapes):
        for name, s in shapes.items():
            self.names.append(name)
            self.shapes.append(pltpu.VMEM(s.shape, s.dtype))

    def bind(self, refs):
        return dict(zip(self.names, refs))


class Mover:
    def __init__(self, sems):
        self.sems, self.open, self.used = sems, {}, 0

    def start(self, src, dst, key):
        copy = pltpu.make_async_copy(src, dst, self.sems.at[self.used])
        self.used += 1
        copy.start()
        self.open[key] = copy

    def wait(self, *keys):
        for key in keys:
            if key in self.open:
                self.open.pop(key).wait()

    def close(self):
        self.wait(*list(self.open))


def make_bias(docs, bias_ref):
    length = bias_ref.shape[0]
    down = jnp.broadcast_to(docs[...], (128, length)).T

    def step(i):
        place_down = lax.broadcasted_iota(jnp.int32, (length, 128), 0)
        place_across = lax.broadcasted_iota(jnp.int32, (length, 128), 1) + i * 128
        seen = (down == docs[:, at(i, 128)]) & (place_down <= place_across)
        bias_ref[:, at(i, 128)] = jnp.where(seen, 0.0, -1e30)

    tiles(length // 128, step)


def spread_vectors(small, vectors_ref, rows):
    count, model = small.shape[0], vectors_ref.shape[1]
    lane = lax.broadcasted_iota(jnp.int32, (128, model), 1)
    place = lax.broadcasted_iota(jnp.int32, (128, model), 0)
    block = (lane * 2731) >> 16
    pick = jnp.where(lane - block * rows == place, 1.0, 0.0).astype(jnp.bfloat16)
    wide = dot(small[...].reshape(count * 8, 128), pick)
    row = lax.broadcasted_iota(jnp.int32, wide.shape, 0)
    owner = (lax.broadcasted_iota(jnp.int32, wide.shape, 1) * 2731) >> 16
    wide = jnp.where((row >> 3) == owner, wide, 0.0)
    vectors_ref[...] = jnp.sum(wide.reshape(count, 8, model), 0)


def gather_chunks(weights):
    chunks = [("small", ((0, 128),))]
    for name, parts in (("out", 1), ("qkv", 3), ("up", 2), ("down", 2)):
        chunks += [(name, halves) for halves in pieces(weights[name].shape[2], parts)]
    return chunks


def first_kernel(near, table, room, chunks, *refs):
    it = iter(refs)
    tokens, docs = next(it), next(it)
    shards = {n: next(it) for n in NAMES}
    if near:
        shards["small"] = next(it)
    else:
        vectors = next(it)
    far = {n: next(it) for n in ("u",) + KEPT}
    if near:
        whole = {n: next(it) for n in NAMES}
        vectors = next(it)
    refs = list(it)
    v = room.bind(refs)
    sems = refs[len(room.names) :]
    mover = Mover(sems[0])
    w = {n: v["w_" + n] for n in NAMES}
    pump = None
    if near:
        gather = Gather(chunks, shards, {**w, "small": v["small"]}, sems[1:])
        pump = Pump(gather.step, staggered(len(chunks), 2, ("first", "second", "third", "fourth", "finish")))
        gather.links.greet()
        for one in pump.take(2):
            pump.run(*one)
    else:
        for n in NAMES:
            mover.start(shards[n], w[n], "w_" + n)
    make_bias(docs, v["bias"])
    if near:
        pump.until("finish", 0)
        spread_vectors(v["small"], vectors, 24)
    last = {name: n for n, (name, _) in enumerate(chunks)}

    def ready(name):
        if near:
            pump.until("finish", last[name])
            mover.start(w[name], whole[name], "whole_" + name)
        else:
            mover.wait("w_" + name)

    def hook(loops, count):
        return pump.hook(loops, count) if near else None

    def done(*names):
        for n in names:
            mover.start(v[n], far[n], "far_" + n)

    gains = [vectors[n : n + 1] for n in (1, 2)]
    forward_pass(tokens, None, v["bias"], gains, w, v, v["u"], vectors.at[0:1], ready, done, hook)
    mover.start(v["u"], far["u"], "far_u")
    if near:
        pump.rest()
        for n in range(len(chunks)):
            gather.step("close", n)
    mover.close()


def run_first(near, tokens, docs, small, vectors, shards):
    length, model = tokens.shape
    devices = 32 if near else 1
    weights = {n: jax.ShapeDtypeStruct((devices * s.shape[0],) + s.shape[1:], s.dtype) for n, s in shards.items()}
    table = shapes_of(length, model, weights["up"].shape[2], 1)
    room = Room()
    room.scratch(**{n: table[n] for n in KEPT + LOCAL + ("bias", "u")}, **{"w_" + n: weights[n] for n in NAMES})
    chunks = gather_chunks(weights) if near else []
    out_shape = [table[n] for n in ("u",) + KEPT]
    semaphores = [pltpu.SemaphoreType.DMA((24,))]
    params = dict(vmem_limit_bytes=VMEM_LIMIT)
    out_specs = [FAR] * len(out_shape)
    inputs = [tokens, docs] + [shards[n] for n in NAMES]
    if near:
        room.scratch(small=jax.ShapeDtypeStruct((32, 8, 128), jnp.bfloat16))
        out_shape += [weights[n] for n in NAMES] + [table["vectors"]]
        out_specs += [FAR] * 4 + [VMEM]
        semaphores += link_semaphores(len(chunks))
        params.update(collective_id=0, has_side_effects=True)
        inputs, in_specs = inputs + [small], [VMEM] * 2 + [FAR] * 5
    else:
        inputs, in_specs = inputs + [vectors], [VMEM] * 2 + [FAR] * 4 + [VMEM]
    outs = pl.pallas_call(
        functools.partial(first_kernel, near, table, room, chunks),
        out_shape=out_shape,
        in_specs=in_specs,
        out_specs=out_specs,
        scratch_shapes=room.shapes + semaphores,
        name="first",
        compiler_params=pltpu.CompilerParams(**params),
    )(*inputs)
    kept = dict(zip(("u",) + KEPT, outs))
    if near:
        return kept, outs[-1], dict(zip(NAMES, outs[1 + len(KEPT) :]))
    return kept, vectors, shards


def middle_kernel(table, room, *refs):
    it = iter(refs)
    u, docs, vectors = next(it), next(it), next(it)
    cotangent, qkv_before = next(it), next(it)
    weights = {n: next(it) for n in NAMES}
    ln1, ln2, whole = next(it), next(it), next(it)
    layer_out, du, dkv = next(it), next(it), next(it)
    grads = {n: next(it) for n in NAMES}
    refs = list(it)
    v = room.bind(refs)
    mover = Mover(refs[len(room.names)])
    w = {n: v["w_" + n] for n in NAMES}
    mover.start(weights["qkv"], w["qkv"], "w_qkv")
    mover.start(qkv_before, v["before"], "before")
    for n in NAMES[1:]:
        mover.start(weights[n], w[n], "w_" + n)
    mover.start(cotangent, v["dz"], "dz")
    make_bias(docs, v["bias"])
    gains = [vectors[n : n + 1] for n in (1, 2)]

    def ready(name):
        if name == "qkv":
            mover.wait("before")
        mover.wait("w_" + name)

    forward_pass(u, v["before"], v["bias"], gains, w, v, v["b"], None, ready)
    mover.start(v["b"], layer_out, "layer_out")
    mover.wait("dz")
    work = dict(dz=v["dz"], da=v["a"], do=v["do"], dm=v["dm"], dhid=v["f"], dqkv=v["dqkv"], du=v["m"])

    def done(name):
        if name == "dkv":
            mover.start(v["dkv"], dkv, "dkv")
        elif name in NAMES:
            mover.start(w[name], grads[name], "g_" + name)

    backward_pass(
        v["dz"], u, [v["before"], v["qkv"]], [v["dkv"], None], gains, w, v, work, None, None, v["m"], (ln1, ln2), whole, no_wait, done
    )
    mover.start(v["m"], du, "du")
    mover.close()


def no_wait(name):
    pass


def run_middle(u, docs, vectors, cotangent, qkv_before, weights):
    length, model = u.shape
    table = shapes_of(length, model, weights["up"].shape[2], 2)
    room = Room()
    room.scratch(**{n: table[n] for n in KEPT + LOCAL + ("bias", "dz", "do", "dm", "dqkv", "dkv")}, before=table["qkv"])
    room.scratch(**{"w_" + n: weights[n] for n in NAMES})
    out_shape = [table["vectors"]] * 3 + [table["b"], table["u"], table["dkv"]] + [weights[n] for n in NAMES]
    outs = pl.pallas_call(
        functools.partial(middle_kernel, table, room),
        out_shape=out_shape,
        in_specs=[VMEM] * 3 + [FAR] * 6,
        out_specs=[VMEM] * 3 + [FAR] * 7,
        scratch_shapes=room.shapes + [pltpu.SemaphoreType.DMA((16,))],
        name="middle",
        compiler_params=pltpu.CompilerParams(vmem_limit_bytes=VMEM_LIMIT),
    )(u, docs, vectors, cotangent, qkv_before, *(weights[n] for n in NAMES))
    return outs[:3], outs[3], outs[4], outs[5], dict(zip(NAMES, outs[6:]))


LATE = {
    "down": [("begin", 0), ("begin", 1)],
    "hidden": [("first", 0)],
    "up": [("begin", 2), ("begin", 3), ("first", 1)],
    "norm": [("second", 0), ("first", 2)],
    "out": [("begin", 4), ("second", 1), ("first", 3)],
}
INSIDE = [
    [("third", 0), ("second", 2)],
    [("third", 1), ("first", 4)],
    [("finish", 0), ("second", 3)],
    [("third", 2), ("finish", 1)],
    [("second", 4), ("third", 3)],
    [("finish", 2)],
]
AFTER = [("begin", 5), ("begin", 6), ("begin", 7), ("third", 4), ("finish", 3), ("first", 5)]
TAIL = [
    ("begin", 8), ("first", 6), ("second", 5), ("first", 7), ("second", 6), ("third", 5), ("finish", 4), ("first", 8), ("second", 7),
    ("third", 6), ("second", 8), ("finish", 5), ("third", 7), ("third", 8), ("finish", 6), ("finish", 7), ("finish", 8),
]


def reduce_chunks(weights):
    chunks = []
    for name, parts in (("down", 2), ("up", 2), ("out", 1), ("qkv", 3)):
        chunks += [(name, halves) for halves in pieces(weights[name].shape[2], parts)]
    return chunks + [("small", ((0, 128),))]


def fold_vectors(vector, small, rows):
    count, model = small.shape[0], vector.shape[1]
    lane = lax.broadcasted_iota(jnp.int32, (128, model), 1)
    place = lax.broadcasted_iota(jnp.int32, (128, model), 0)
    block = (lane * 2731) >> 16
    pick = jnp.where(lane - block * rows == place, 1.0, 0.0).astype(jnp.bfloat16)
    wide = jnp.broadcast_to(vector[None], (count, 8, model)).reshape(count * 8, model)
    row = lax.broadcasted_iota(jnp.int32, wide.shape, 0)
    owner = (lax.broadcasted_iota(jnp.int32, wide.shape, 1) * 2731) >> 16
    wide = jnp.where((row >> 3) == owner, wide, 0.0).astype(jnp.bfloat16)
    small[...] = dot_nt(wide, pick).astype(jnp.bfloat16).reshape(small.shape)


def last_kernel(near, room, chunks, *refs):
    it = iter(refs)
    tokens, vectors, late1, late2, embed = next(it), next(it), next(it), next(it), next(it)
    far = {n: next(it) for n in ("upstream", "dkv") + KEPT}
    weights = {n: next(it) for n in NAMES}
    before = {n: next(it) for n in NAMES}
    du = next(it)
    outs = {n: next(it) for n in NAMES + ("small",)}
    refs = list(it)
    v = room.bind(refs)
    sems = refs[len(room.names) :]
    mover = Mover(sems[0])
    w = {n: v["w_" + n] for n in NAMES}
    mover.start(far["upstream"], v["upstream"], "upstream")
    mover.start(weights["down"], w["down"], "w_down")
    for n in ("gp", "ft"):
        mover.start(far[n], v[n], n)
    mover.start(weights["up"], w["up"], "w_up")
    for n in ("bt", "m"):
        mover.start(far[n], v[n], n)
    mover.start(weights["out"], w["out"], "w_out")
    for n in ("rl", "ot", "qkv", "p0", "p1", "dkv"):
        mover.start(far[n], v[n], n)
    mover.start(weights["qkv"], w["qkv"], "w_qkv")
    mover.start(far["at"], v["at"], "at")
    needs = {
        "upstream": ("upstream",),
        "down": ("w_down", "gp"),
        "ft": ("ft",),
        "up": ("w_up", "bt", "m"),
        "out": ("w_out", "rl", "ot"),
        "attention": ("qkv", "p0", "p1", "dkv"),
        "qkv": ("w_qkv", "at"),
    }

    def ready(name):
        mover.wait(*needs[name])

    hook = None
    if near:
        reduce = Reduce(
            chunks, {**w, "small": v["small"]}, *({n: v["r%d_%s" % (k, n)] for n in NAMES + ("small",)} for k in range(4)), outs, sems[2:]
        )
        reduce.links.greet()

        def run(events):
            for what, n in events:
                reduce.step(what, n)

        def hook(pair):
            for k, events in enumerate(INSIDE):

                @pl.when(pair == k)
                def _(events=events):
                    run(events)

    def done(name):
        if near:
            run(LATE.get(name, ()))
            if name == "qkv":
                run(AFTER)
        elif name in NAMES:
            mover.start(w[name], outs[name], "g_" + name)

    work = dict(dz=v["dz"], da=v["dz"], do=v["do"], dm=v["dm"], dhid=v["gp"], dqkv=v["dqkv"])
    gains = [vectors[n : n + 1] for n in (1, 2)]
    backward_pass(
        v["upstream"], tokens, [v["qkv"]], [v["dkv"]], gains, w, v, work, before, (v["stage0"], v["stage1"], sems[1]),
        v["m"], (v["ln1"], v["ln2"]), None, ready, done, hook,
    )
    mover.start(v["m"], du, "du")
    row = lax.broadcasted_iota(jnp.int32, embed.shape, 0)
    vector = jnp.where(row == 0, embed[...], jnp.where(row == 1, late1[...] + v["ln1"][...], jnp.where(row == 2, late2[...] + v["ln2"][...], 0.0)))
    if near:
        fold_vectors(vector, v["small"], 24)
        run(TAIL)
        for n in range(len(chunks)):
            reduce.step("close", n)
    else:
        outs["small"][...] = vector
    mover.close()


def run_last(near, tokens, vectors, late1, late2, embed, upstream, dkv, kept, weights, before):
    length, model = tokens.shape
    bf16 = jnp.bfloat16
    shape = jax.ShapeDtypeStruct
    table = shapes_of(length, model, weights["up"].shape[2], 1)
    room = Room()
    room.scratch(**{n: table[n] for n in KEPT + ("dz", "do", "dm", "dqkv", "dkv")}, upstream=table["u"])
    room.scratch(ln1=table["vectors"], ln2=table["vectors"])
    room.scratch(**{"w_" + n: weights[n] for n in NAMES})
    room.scratch(stage0=shape((2, model // 8, 8, 256), bf16), stage1=shape((2, 32, 8, model), bf16))
    chunks = reduce_chunks(weights) if near else []
    semaphores = [pltpu.SemaphoreType.DMA((24,)), pltpu.SemaphoreType.DMA((2,))]
    params = dict(vmem_limit_bytes=VMEM_LIMIT)
    if near:
        parts = {**weights, "small": shape((32, 8, 128), bf16)}
        room.scratch(small=parts["small"])
        for k, blocks in enumerate((16, 8, 4, 3)):
            room.scratch(**{"r%d_%s" % (k, n): shape((p.shape[0] // 32 * blocks,) + p.shape[1:], bf16) for n, p in parts.items()})
        out_shape = [shape((parts[n].shape[0] // 32,) + parts[n].shape[1:], jnp.float32) for n in NAMES + ("small",)]
        out_specs = [VMEM] * 5
        semaphores += link_semaphores(len(chunks))
        params.update(collective_id=1, has_side_effects=True)
    else:
        out_shape = [weights[n] for n in NAMES] + [table["vectors"]]
        out_specs = [FAR] * 4 + [VMEM]
    outs = pl.pallas_call(
        functools.partial(last_kernel, near, room, chunks),
        out_shape=[table["u"]] + out_shape,
        in_specs=[VMEM] * 5 + [FAR] * (2 + len(KEPT) + 8),
        out_specs=[FAR] + out_specs,
        scratch_shapes=room.shapes + semaphores,
        name="last",
        compiler_params=pltpu.CompilerParams(**params),
    )(tokens, vectors, late1, late2, embed, upstream, dkv, *(kept[n] for n in KEPT), *(weights[n] for n in NAMES), *(before[n] for n in NAMES))
    return outs[0], dict(zip(NAMES, outs[1:])), outs[5]


AXES = ("dp", "fsdp")


def cut(w):
    return w.reshape(w.shape[0] // 8, 8, w.shape[1])


def join(w):
    return w.reshape(w.shape[0] * 8, w.shape[2])


def body(near, tokens, doc_ids, pass_embed, ln1_gain, w_qkv, w_out, ln2_gain, w_up, w_down, cotangent):
    shards = {"qkv": w_qkv, "out": w_out, "up": w_up, "down": w_down}
    docs = doc_ids.astype(jnp.float32).reshape(1, -1)
    rows = pass_embed.shape[0]
    small = vectors = None
    if near:
        small = jnp.zeros((1, 8, 128), jnp.bfloat16).at[0, :3, :rows].set(jnp.stack([pass_embed, ln1_gain, ln2_gain]))
        shards = {n: cut(s) for n, s in shards.items()}
    else:
        vectors = jnp.stack([lax.all_gather(v, AXES, axis=0, tiled=True) for v in (pass_embed, ln1_gain, ln2_gain)])
        vectors = jnp.pad(vectors.astype(jnp.float32), ((0, 5), (0, 0)))
        shards = {n: cut(lax.all_gather(s, AXES, axis=0, tiled=True)) for n, s in shards.items()}
    kept, vectors, weights = run_first(near, tokens, docs, small, vectors, shards)
    (late1, late2, embed), layer_out, second_g, dkv, late = run_middle(kept["u"], docs, vectors, cotangent, kept["qkv"], weights)
    tokens_grad, sums, small = run_last(near, tokens, vectors, late1, late2, embed, second_g, dkv, kept, weights, late)
    if near:
        sums = {n: join(s) for n, s in sums.items()}
        small = [small[0, n, :rows] for n in range(3)]
    else:
        scatter = lambda v: lax.psum_scatter(v, AXES, scatter_dimension=0, tiled=True)
        sums = {n: scatter(join(s).astype(jnp.float32)) for n, s in sums.items()}
        small = [scatter(small[n]) for n in range(3)]
    return (layer_out, tokens_grad, small[0], small[1], sums["qkv"], sums["out"], small[2], sums["up"], sums["down"])


def solution(mesh):
    near = dict(mesh.shape) == {"dp": 8, "fsdp": 4}
    placed = (
        P(("dp", "fsdp"), None),
        P(("dp", "fsdp")),
        P(("dp", "fsdp")),
        P(("dp", "fsdp")),
        P(("dp", "fsdp"), None),
        P(("dp", "fsdp"), None),
        P(("dp", "fsdp")),
        P(("dp", "fsdp"), None),
        P(("dp", "fsdp"), None),
        P(("dp", "fsdp"), None),
    )
    return jax.shard_map(
        functools.partial(body, near),
        mesh=mesh,
        in_specs=placed,
        out_specs=(
            P(("dp", "fsdp"), None),
            P(("dp", "fsdp"), None),
            P(("dp", "fsdp")),
            P(("dp", "fsdp")),
            P(("dp", "fsdp"), None),
            P(("dp", "fsdp"), None),
            P(("dp", "fsdp")),
            P(("dp", "fsdp"), None),
            P(("dp", "fsdp"), None),
        ),
        check_vma=False,
    )
```

```python
import functools
import math

import jax
import jax.numpy as jnp
from jax import lax
from jax.experimental import pallas as pl
from jax.experimental.pallas import tpu as pltpu
from jax.sharding import PartitionSpec as P

HEAD_DIM = 64


MESH = pl.DeviceIdType.MESH
NAMES = ("qkv", "out", "up", "down")


def pieces(width, parts):
    count = width // 128 // parts
    result = []
    for n in range(parts):
        first = (count + 1 - n % 2) // 2
        start = n * count * 128
        result.append(((start, first * 128), (start + first * 128, (count - first) * 128)))
    return result


class Links:
    def __init__(self, chunks, depth):
        d, z = lax.axis_index("dp"), lax.axis_index("fsdp")
        y, x, c = d // 4, lax.rem(d // 2, 2), lax.rem(d, 2)
        self.d, self.z, self.y, self.x, self.c = d, z, y, x, c
        self.sideways = (y * 4 + (1 - x) * 2 + c, z)
        self.upward = ((1 - y) * 4 + x * 2 + c, z)
        self.sibling = (y * 4 + x * 2 + 1 - c, z)
        self.along = [(d, lax.rem(z + k, 4)) for k in (1, 2, 3)]
        self.chunks, self.depth = chunks, depth

    def greet(self):
        peers = [self.sideways, self.upward, self.sibling, *self.along]
        barrier = pltpu.get_barrier_semaphore()
        for peer in peers:
            pl.semaphore_signal(barrier, inc=1, device_id=peer, device_id_type=MESH)
        pl.semaphore_wait(barrier, len(peers))

    def columns(self, n):
        halves = self.chunks[n][1]
        return pl.ds(halves[0][0], sum(size for _, size in halves))

    def rows(self, n):
        return self.depth[self.chunks[n][0]]

    def hops(self, h):
        return (self.sideways, self.upward) if h == 0 else (self.upward, self.sideways)


def remote(src, dst, send, recv, peer):
    return pltpu.make_async_remote_copy(
        src_ref=src, dst_ref=dst, send_sem=send, recv_sem=recv, device_id=peer, device_id_type=MESH
    )


def link_semaphores(count):
    dma = pltpu.SemaphoreType.DMA
    return [dma((count, 3)), dma((count, 3)), dma((count, 2, 3)), dma((count, 2, 3)), dma((count, 4)), dma((count, 4)), dma((count,))]


class Gather:
    def __init__(self, chunks, shards, wholes, sems):
        self.links = Links(chunks, {n: s.shape[0] for n, s in shards.items()})
        self.chunks, self.shards, self.wholes = chunks, shards, wholes
        self.z_send, self.z_recv, self.p_send, self.p_recv, self.d_send, self.d_recv, self.own_sem = sems

    def group(self, n, y, x, cols):
        rows = self.links.rows(n)
        return self.wholes[self.chunks[n][0]].at[pl.ds((y * 4 + x * 2 + self.links.c) * 4 * rows, 4 * rows), :, cols]

    def near(self, n):
        rows, cols = self.links.rows(n), self.links.columns(n)
        name = self.chunks[n][0]
        at = (self.links.d * 4 + self.links.z) * rows
        return self.shards[name].at[:, :, cols], self.wholes[name].at[pl.ds(at, rows), :, cols]

    def own(self, n):
        return pltpu.make_async_copy(*self.near(n), self.own_sem.at[n])

    def ahead(self, n, k):
        return remote(*self.near(n), self.z_send.at[n, k], self.z_recv.at[n, k], self.links.along[k])

    def hop(self, n, h, i):
        at = self.links
        one, two = at.hops(h)
        y, x = at.y, at.x
        if i == 2:
            y, x = (y, 1 - x) if h == 0 else (1 - y, x)
        block = self.group(n, y, x, pl.ds(*self.chunks[n][1][h]))
        return remote(block, block, self.p_send.at[n, h, i], self.p_recv.at[n, h, i], one if i == 0 else two)

    def share(self, n, g):
        at = self.links
        y, x = at.y, at.x
        block = self.group(n, 1 - y if g >= 2 else y, 1 - x if g % 2 else x, at.columns(n))
        return remote(block, block, self.d_send.at[n, g], self.d_recv.at[n, g], at.sibling)

    def halves(self, n):
        return range(len(self.chunks[n][1]))

    def step(self, what, n):
        if what == "begin":
            self.own(n).start()
            for k in range(3):
                self.ahead(n, k).start()
        elif what == "first":
            self.own(n).wait()
            for k in range(3):
                self.ahead(n, k).wait_recv()
            for h in self.halves(n):
                self.hop(n, h, 0).start()
                self.hop(n, h, 1).start()
            self.share(n, 0).start()
        elif what == "second":
            for h in self.halves(n):
                self.hop(n, h, 0).wait_recv()
                self.hop(n, h, 2).start()
        elif what == "third":
            for h in self.halves(n):
                self.hop(n, h, 1).wait_recv()
            self.share(n, 1).start()
            self.share(n, 2).start()
        elif what == "fourth":
            for h in self.halves(n):
                self.hop(n, h, 2).wait_recv()
            self.share(n, 3).start()
        elif what == "finish":
            for g in range(4):
                self.share(n, g).wait_recv()
        elif what == "close":
            for k in range(3):
                self.ahead(n, k).wait_send()
            for h in self.halves(n):
                for i in range(3):
                    self.hop(n, h, i).wait_send()
            for g in range(4):
                self.share(n, g).wait_send()


def staggered(count, ahead, stages):
    events = [("begin", n) for n in range(min(ahead, count))]
    for tick in range(count + len(stages) - 1):
        for late, what in enumerate(stages):
            if 0 <= tick - late < count:
                events.append((what, tick - late))
                if late == 0 and tick + ahead < count:
                    events.append(("begin", tick + ahead))
    return events


class Pump:
    def __init__(self, step, events):
        self.run, self.events, self.next = step, events, 0

    def take(self, count):
        taken = self.events[self.next : self.next + count]
        self.next += len(taken)
        return taken

    def until(self, *event):
        if event in self.events[self.next :]:
            for one in self.take(self.events.index(event) + 1 - self.next):
                self.run(*one)

    def rest(self):
        for one in self.take(len(self.events)):
            self.run(*one)

    def hook(self, loops, count):
        return at_steps(self.run, [self.take(count * (i + 1) // loops - count * i // loops) for i in range(loops)])


def at_steps(run, plan):
    def at_step(i):
        for k, events in enumerate(plan):
            if not isinstance(i, int):

                @pl.when(i == k)
                def _(events=events):
                    for one in events:
                        run(*one)

            elif i == k:
                for one in events:
                    run(*one)

    return at_step


class Reduce:
    def __init__(self, chunks, parts, r0, r1, r2, r3, outs, sems):
        self.links = Links(chunks, {n: s.shape[0] for n, s in outs.items()})
        self.chunks, self.parts, self.outs = chunks, parts, outs
        self.r0, self.r1, self.r2, self.r3 = r0, r1, r2, r3
        self.z_send, self.z_recv, self.p_send, self.p_recv, self.d_send, self.d_recv, _ = sems

    def share(self, n, g):
        at, name = self.links, self.chunks[n][0]
        span, cols = 4 * at.rows(n), at.columns(n)
        src = self.parts[name].at[pl.ds((g * 2 + 1 - at.c) * span, span), :, cols]
        dst = self.r0[name].at[pl.ds(g * span, span), :, cols]
        return remote(src, dst, self.d_send.at[n, g], self.d_recv.at[n, g], at.sibling)

    def hop(self, n, h, i):
        at, name = self.links, self.chunks[n][0]
        span, cols = 4 * at.rows(n), pl.ds(*self.chunks[n][1][h])
        two, one = at.hops(h)
        if i < 2:
            g = (1 - at.y) * 2 + i if h == 0 else i * 2 + 1 - at.x
            src = self.r0[name].at[pl.ds(g * span, span), :, cols]
            dst = self.r1[name].at[pl.ds(i * span, span), :, cols]
        else:
            far = 1 - at.x if h == 0 else 1 - at.y
            src = self.r1[name].at[pl.ds(far * span, span), :, cols]
            dst = self.r2[name].at[:, :, cols]
        return remote(src, dst, self.p_send.at[n, h, i], self.p_recv.at[n, h, i], one if i < 2 else two)

    def ahead(self, n, k):
        at, name = self.links, self.chunks[n][0]
        rows, cols = at.rows(n), at.columns(n)
        src = self.r2[name].at[pl.ds(lax.rem(at.z + k + 1, 4) * rows, rows), :, cols]
        dst = self.r3[name].at[pl.ds(k * rows, rows), :, cols]
        return remote(src, dst, self.z_send.at[n, k], self.z_recv.at[n, k], at.along[k])

    def add(self, count, into, into_at, other, other_at, cols):
        def one(i, carry):
            into[into_at + i, :, cols] = into[into_at + i, :, cols] + other[other_at + i, :, cols]
            return carry

        lax.fori_loop(0, count, one, 0, unroll=4)

    def halves(self, n):
        return range(len(self.chunks[n][1]))

    def step(self, what, n):
        at, name = self.links, self.chunks[n][0]
        rows = at.rows(n)
        span = 4 * rows
        if what == "begin":
            for g in range(4):
                self.share(n, g).start()
        elif what == "first":
            for g in range(4):
                self.share(n, g).wait_recv()
                self.add(span, self.r0[name], g * span, self.parts[name], (g * 2 + at.c) * span, at.columns(n))
            for h in self.halves(n):
                self.hop(n, h, 0).start()
                self.hop(n, h, 1).start()
        elif what == "second":
            for h in self.halves(n):
                cols = pl.ds(*self.chunks[n][1][h])
                for i in range(2):
                    self.hop(n, h, i).wait_recv()
                    g = at.y * 2 + i if h == 0 else i * 2 + at.x
                    self.add(span, self.r1[name], i * span, self.r0[name], g * span, cols)
                self.hop(n, h, 2).start()
        elif what == "third":
            for h in self.halves(n):
                cols = pl.ds(*self.chunks[n][1][h])
                self.hop(n, h, 2).wait_recv()
                self.add(span, self.r2[name], 0, self.r1[name], (at.x if h == 0 else at.y) * span, cols)
            for k in range(3):
                self.ahead(n, k).start()
        elif what == "finish":
            cols = at.columns(n)
            for k in range(3):
                self.ahead(n, k).wait_recv()

            def one(i, carry):
                total = self.r2[name][at.z * rows + i, :, cols].astype(jnp.float32)
                for k in range(3):
                    total = total + self.r3[name][k * rows + i, :, cols].astype(jnp.float32)
                self.outs[name][i, :, cols] = total
                return carry

            lax.fori_loop(0, rows, one, 0)
        elif what == "close":
            for g in range(4):
                self.share(n, g).wait_send()
            for h in self.halves(n):
                for i in range(3):
                    self.hop(n, h, i).wait_send()
            for k in range(3):
                self.ahead(n, k).wait_send()


EPS = 1e-05
QB = 256
SCALE = HEAD_DIM ** (-0.5)
NT = (((1,), (1,)), ((), ()))


def dot(left, right):
    return jnp.dot(left, right, preferred_element_type=jnp.float32)


def dot_nt(left, right):
    return lax.dot_general(left, right, NT, preferred_element_type=jnp.float32)


def tiles(count, step, by=1):
    def go(i, carry):
        for k in range(by):
            step(i * by + k)
        return carry

    if by >= count:
        for k in range(count):
            step(k)
    else:
        lax.fori_loop(0, count // by, go, 0)


def at(i, size, start=0):
    if isinstance(i, int):
        return pl.ds(start + i * size, size)
    return pl.ds(pl.multiple_of(start + i * size, 128 if size % 128 == 0 else size), size)


def weight_columns(w, i, size):
    block = w[:, :, at(i, size)]
    return block.reshape(block.shape[0] * 8, size)


def weight_rows(w, i, size):
    block = w[pl.ds(i * (size // 8), size // 8)]
    return block.reshape(size, block.shape[2])


def normal(u):
    center = u - jnp.mean(u, -1, keepdims=True)
    spread = lax.rsqrt(jnp.mean(center * center, -1, keepdims=True) + EPS)
    return center * spread, spread


def norm_rows(u_ref, gain, out_ref):
    def step(i):
        hat, spread = normal(u_ref[at(i, 128)].astype(jnp.float32))
        out_ref[at(i, 128)] = (hat * gain).astype(jnp.bfloat16)

    tiles(u_ref.shape[0] // 128, step)


def gelu_both(x):
    e = jnp.exp(x * x * -0.5)
    t = 1.0 / (1.0 + jnp.abs(x) * (0.3275911 * 0.5**0.5))
    poly = 0.5 * 1.061405429
    for term in (-1.453152027, 1.421413741, -0.284496736, 0.254829592):
        poly = poly * t + 0.5 * term
    tail = poly * t * e
    cdf = jnp.where(x >= 0, 1.0 - tail, tail)
    return x * cdf, cdf + x * e * (0.5 / math.pi) ** 0.5


def both_heads(block, axis):
    half = lax.broadcasted_iota(jnp.int32, block.shape, axis) < HEAD_DIM
    zero = jnp.zeros_like(block)
    return jnp.concatenate([jnp.where(half, block, zero), jnp.where(half, zero, block)], 1 - axis)


def own_heads(wide):
    count = wide.shape[1] // 2
    return jnp.concatenate([wide[:HEAD_DIM, :count], wide[HEAD_DIM:, count:]], 0)


def right(model, n, pair):
    return at(pair, 128, n * model)


def attend(qkvs, bias_ref, p_refs, rl_ref, o_ref, ot_ref, between=None, by=6, depth=2):
    model = o_ref.shape[1]
    own = qkvs[-1]

    def score(pair, b):
        span = (b + 1) * QB
        queries = both_heads(own[b * QB : span, at(pair, 128)] * SCALE, 1)
        bias = bias_ref[:span, b * QB : span]
        bias = jnp.concatenate([bias, bias], 1)
        return [dot_nt(ref[:span, right(model, 1, pair)], queries) + bias for ref in qkvs]

    def finish(pair, b, scores):
        span = (b + 1) * QB
        lanes = at(pair, 128)
        peak = jnp.max(scores[0], 0, keepdims=True)
        for s in scores[1:]:
            peak = jnp.maximum(peak, jnp.max(s, 0, keepdims=True))
        total, out = None, None
        for n, s in enumerate(scores):
            p = jnp.exp(s - peak)
            part = jnp.sum(p, 0, keepdims=True)
            p = p.astype(jnp.bfloat16)
            p_refs[b][pair, n * span : (n + 1) * span] = p
            product = dot(qkvs[n][:span, right(model, 2, pair)].T, p)
            total = part if total is None else total + part
            out = product if out is None else out + product
        scale = 1.0 / total
        rl_ref[pair, 0:1, b * QB : span] = scale[:, :QB]
        rl_ref[pair, 1:2, b * QB : span] = scale[:, QB:]
        out = own_heads(out * scale)
        ot_ref[at(pair, 128), b * QB : span] = out
        o_ref[b * QB : span, lanes] = out.astype(jnp.bfloat16).T

    def step(i):
        items = [(i * by + k, b) for k in range(by) for b in (1, 0)]
        waiting = []
        for n, item in enumerate(items):
            if between is not None and n % 2 == 0:
                between(item[0])
            waiting.append((item, score(*item)))
            if len(waiting) > depth:
                item, s = waiting.pop(0)
                finish(*item, s)
        for item, s in waiting:
            finish(*item, s)

    tiles(model // 128 // by, step)


def attend_back(qkvs, p_refs, do_ref, ot_ref, dqkv_ref, dkv_refs, hook=None):
    model = do_ref.shape[0]
    own = qkvs[-1]

    def step(pair):
        if hook is not None:
            hook(pair)
        lanes = at(pair, 128)
        keys = [ref[:, right(model, 1, pair)] for ref in qkvs]
        values = [ref[:, right(model, 2, pair)] for ref in qkvs]
        turned = [k.T for k in keys]
        dk, dv = [None] * len(qkvs), [None] * len(qkvs)
        for b in reversed(range(own.shape[0] // QB)):
            span = (b + 1) * QB
            block = slice(b * QB, span)
            queries = both_heads(own[block, lanes] * SCALE, 1)
            do = do_ref[lanes, block]
            do_down, do_across = both_heads(do, 0), both_heads(do.T, 1)
            product = do.astype(jnp.float32) * ot_ref[lanes, block]
            delta = jnp.concatenate([jnp.sum(product[h * HEAD_DIM : (h + 1) * HEAD_DIM], 0, keepdims=True) for h in range(2)], 1)
            dq = None
            for n in range(len(qkvs)):
                p = p_refs[b][pair, n * span : (n + 1) * span]
                ds = dot(values[n][:span], do_down) - delta
                ds = (p.astype(jnp.float32) * ds).astype(jnp.bfloat16)
                more_dv, more_dk = dot(p, do_across), dot(ds, queries)
                more_dq = dot(turned[n][:, :span], ds)
                dq = more_dq if dq is None else dq + more_dq
                if dk[n] is None:
                    dk[n], dv[n] = more_dk, more_dv
                else:
                    dk[n] = jnp.concatenate([dk[n][:span] + more_dk, dk[n][span:]], 0)
                    dv[n] = jnp.concatenate([dv[n][:span] + more_dv, dv[n][span:]], 0)
            dqkv_ref[block, lanes] = (own_heads(dq) * SCALE).astype(jnp.bfloat16).T
        for n, ref in enumerate(dkv_refs):
            if ref is not None and n < len(qkvs) - 1:
                ref[:, lanes] = dk[n]
                ref[:, right(model, 1, pair)] = dv[n]
        extra = dkv_refs[-1]
        dk, dv = dk[-1], dv[-1]
        if extra is not None:
            dk, dv = dk + extra[:, lanes], dv + extra[:, right(model, 1, pair)]
        dqkv_ref[:, right(model, 1, pair)] = dk.astype(jnp.bfloat16)
        dqkv_ref[:, right(model, 2, pair)] = dv.astype(jnp.bfloat16)

    tiles(model // 128, step, 3)


def project(left_ref, w, add_ref, out_ref, shift=None, size=256, by=9):
    def step(i):
        value = dot(left_ref[...], weight_columns(w, i, size))
        if add_ref is not None:
            value = add_ref[:, at(i, size)].astype(jnp.float32) + value
        if shift is not None:
            value = value + shift[:, at(i, size)]
        out_ref[:, at(i, size)] = value.astype(out_ref.dtype)

    tiles(w.shape[2] // size, step, by)


def project_back(left_ref, w, out_ref, size=768):
    def step(i):
        out_ref[:, at(i, size)] = dot_nt(left_ref[...], weight_rows(w, i, size)).astype(out_ref.dtype)

    tiles(w.shape[0] * 8 // size, step)


def forward_pass(u_ref, qkv_before, bias_ref, gains, w, keep, out_ref, shift, ready, done=None, hook=None):
    done = done or (lambda *names: None)
    hook = hook or (lambda loops, count: None)
    norm_rows(u_ref, gains[0], keep["a"])
    turn(keep["a"], keep["at"])
    done("at")
    ready("qkv")
    project(keep["a"], w["qkv"], None, keep["qkv"])
    done("qkv")
    qkvs = [keep["qkv"]] if qkv_before is None else [qkv_before, keep["qkv"]]
    attend(qkvs, bias_ref, [keep["p0"], keep["p1"]], keep["rl"], keep["o"], keep["ot"], hook(6, 9))
    done("p0", "p1", "rl", "ot")
    ready("out")
    project(keep["o"], w["out"], u_ref, keep["m"])
    norm_rows(keep["m"], gains[1], keep["b"])
    turn(keep["b"], keep["bt"])
    done("m", "bt")
    ready("up")
    between = hook(4, 6)

    def step(i):
        if between is not None:
            between(i)
        hidden = dot(keep["b"][...], weight_columns(w["up"], i, 768))
        active, slope = gelu_both(hidden)
        active = active.astype(jnp.bfloat16)
        keep["f"][:, at(i, 768)] = active
        keep["ft"][at(i, 768)] = active.T
        keep["gp"][:, at(i, 768)] = slope.astype(jnp.bfloat16)

    tiles(w["up"].shape[2] // 768, step, 2)
    done("ft", "gp")
    ready("down")
    project(keep["f"], w["down"], keep["m"], out_ref, shift)


def norm_back(u_ref, gain, dy_ref, add_ref, out_ref, rounded_ref, gain_grad_ref, sum_ref=None):
    def step(i, totals):
        total, whole = totals
        hat, spread = normal(u_ref[at(i, 128)].astype(jnp.float32))
        dy = dy_ref[at(i, 128)]
        total = total + jnp.sum((dy * hat).reshape(16, 8, dy.shape[1]), 0)
        dy = dy * gain
        down = dy - jnp.mean(dy, -1, keepdims=True) - hat * jnp.mean(dy * hat, -1, keepdims=True)
        value = add_ref[at(i, 128)].astype(jnp.float32) + spread * down
        out_ref[at(i, 128)] = value
        if rounded_ref is not None:
            rounded_ref[at(i, 128)] = value.astype(jnp.bfloat16)
        if sum_ref is not None:
            whole = whole + jnp.sum(value.reshape(16, 8, dy.shape[1]), 0)
        return total, whole

    zero = jnp.zeros((8, u_ref.shape[1]), jnp.float32)
    total, whole = lax.fori_loop(0, u_ref.shape[0] // 128, step, (zero, zero))
    gain_grad_ref[...] = jnp.broadcast_to(jnp.sum(total, 0, keepdims=True), gain_grad_ref.shape)
    if sum_ref is not None:
        sum_ref[...] = jnp.broadcast_to(jnp.sum(whole, 0, keepdims=True), sum_ref.shape)


def weight_grad(turned_ref, right_ref, out_ref, add, size=768, by=2, each=None):
    def step(i):
        value = dot(turned_ref[...].astype(jnp.bfloat16), right_ref[:, at(i, size)])
        value = value.reshape(value.shape[0] // 8, 8, size)
        if add:
            value = value + out_ref[:, :, at(i, size)].astype(jnp.float32)
        out_ref[:, :, at(i, size)] = value.astype(out_ref.dtype)
        if each is not None:
            each(i)

    tiles(right_ref.shape[1] // size, step, by)


def turn(ref, out_ref):
    def step(i):
        out_ref[at(i, 256)] = ref[:, at(i, 256)].T

    tiles(ref.shape[1] // 256, step)


def backward_pass(up_ref, u_ref, qkvs, dkv_refs, gains, w, keep, work, late, du_ref, gain_grads, sum_ref, ready, done, hook=None, each=None):
    dz = up_ref
    if up_ref.dtype != jnp.bfloat16:
        dz = work["dz"]
        ready("upstream")

        def cast(i):
            dz[at(i, 128)] = up_ref[at(i, 128)].astype(jnp.bfloat16)

        tiles(up_ref.shape[0] // 128, cast)
    ready("down")
    dhid = work["dhid"]
    count = w["down"].shape[0] * 8 // 768

    def back(i):
        value = dot_nt(dz[...], weight_rows(w["down"], i, 768)) * keep["gp"][:, at(i, 768)].astype(jnp.float32)
        dhid[:, at(i, 768)] = value.astype(jnp.bfloat16)
        if late is not None:
            late("down", i)

    def down_grad(i):
        block = pl.ds(i * 96, 96)
        value = dot(keep["ft"][at(i, 768)], dz[...]).reshape(96, 8, dz.shape[1])
        if late is not None:
            ready("late_down%d" % i)
            value = value + w["down"][block].astype(jnp.float32)
        w["down"][block] = value.astype(jnp.bfloat16)

    for i in range(count + 1):
        if i < count:
            back(i)
        if i == 0:
            ready("ft")
        else:
            down_grad(i - 1)
    done("down")
    ready("up")
    project_back(dhid, w["up"], work["dm"])
    if late is not None:
        late("up")
    done("hidden")
    norm_back(keep["m"], gains[1], work["dm"], up_ref, work["dm"], work["da"], gain_grads[1])
    done("norm")
    ready("late_up")
    weight_grad(keep["bt"], dhid, w["up"], late is not None)
    done("up")
    ready("out")

    def head_grads(i):
        value = dot_nt(weight_rows(w["out"], i, 256), work["da"][...])
        scale = [jnp.broadcast_to(keep["rl"][2 * i + n // 2, n % 2 : n % 2 + 1], (HEAD_DIM, value.shape[1])) for n in range(4)]
        work["do"][at(i, 256)] = (value * jnp.concatenate(scale, 0)).astype(jnp.bfloat16)

    tiles(w["out"].shape[0] * 8 // 256, head_grads, 3)
    if late is not None:
        late("out")
    ready("attention")
    attend_back(qkvs, [keep["p0"], keep["p1"]], work["do"], keep["ot"], work["dqkv"], dkv_refs, hook)
    done("dkv")
    ready("late_out")
    weight_grad(keep["ot"], work["da"], w["out"], late is not None)
    done("out")
    ready("qkv")
    project_back(work["dqkv"], w["qkv"], du_ref)
    if late is not None:
        late("qkv")
    norm_back(u_ref, gains[0], du_ref, work["dm"], du_ref, None, gain_grads[0], sum_ref)
    done("inputs")
    ready("late_qkv")
    weight_grad(keep["at"], work["dqkv"], w["qkv"], late is not None, by=3, each=each)
    done("qkv")


KEPT = ("at", "qkv", "rl", "ot", "m", "bt", "ft", "gp", "p0", "p1")
LOCAL = ("a", "o", "b", "f")
VMEM_LIMIT = 63 << 20
VMEM = pl.BlockSpec(memory_space=pltpu.VMEM)
FAR = pl.BlockSpec(memory_space=pl.ANY)


def shapes_of(length, model, hidden, passes):
    f32, bf16 = jnp.float32, jnp.bfloat16
    shape = jax.ShapeDtypeStruct
    pairs = model // 128
    table = {
        "a": shape((length, model), bf16),
        "at": shape((model, length), bf16),
        "qkv": shape((length, 3 * model), bf16),
        "rl": shape((pairs, 2, length), f32),
        "o": shape((length, model), bf16),
        "ot": shape((model, length), f32),
        "m": shape((length, model), f32),
        "b": shape((length, model), bf16),
        "bt": shape((model, length), bf16),
        "f": shape((length, hidden), bf16),
        "ft": shape((hidden, length), bf16),
        "gp": shape((length, hidden), bf16),
        "dz": shape((length, model), bf16),
        "dm": shape((length, model), f32),
        "dqkv": shape((length, 3 * model), bf16),
        "dkv": shape((length, 2 * model), f32),
        "bias": shape((length, length), f32),
        "u": shape((length, model), f32),
        "vectors": shape((8, model), f32),
    }
    for b in range(length // QB):
        table["p%d" % b] = shape((pairs, passes * (b + 1) * QB, 2 * QB), bf16)
    return table


class Room:
    def __init__(self):
        self.names, self.shapes, self.moves = [], [], []

    def scratch(self, **shapes):
        for name, s in shapes.items():
            self.names.append(name)
            self.shapes.append(pltpu.VMEM(s.shape, s.dtype))

    def bind(self, refs):
        return dict(zip(self.names, refs))


class Mover:
    def __init__(self, sems):
        self.sems, self.open, self.used = sems, {}, 0

    def start(self, src, dst, key):
        copy = pltpu.make_async_copy(src, dst, self.sems.at[self.used])
        self.used += 1
        copy.start()
        self.open[key] = copy

    def wait(self, *keys):
        for key in keys:
            if key in self.open:
                self.open.pop(key).wait()

    def close(self):
        self.wait(*list(self.open))


def make_bias(docs, bias_ref):
    length = bias_ref.shape[0]
    down = jnp.broadcast_to(docs[...], (128, length)).T

    def step(i):
        place_down = lax.broadcasted_iota(jnp.int32, (length, 128), 0)
        place_across = lax.broadcasted_iota(jnp.int32, (length, 128), 1) + i * 128
        seen = (down == docs[:, at(i, 128)]) & (place_down <= place_across)
        bias_ref[:, at(i, 128)] = jnp.where(seen, 0.0, -1e30)

    tiles(length // 128, step)


def spread_vectors(small, vectors_ref, rows):
    count, model = small.shape[0], vectors_ref.shape[1]
    lane = lax.broadcasted_iota(jnp.int32, (128, model), 1)
    place = lax.broadcasted_iota(jnp.int32, (128, model), 0)
    block = (lane * 2731) >> 16
    pick = jnp.where(lane - block * rows == place, 1.0, 0.0).astype(jnp.bfloat16)
    wide = dot(small[...].reshape(count * 8, 128), pick)
    row = lax.broadcasted_iota(jnp.int32, wide.shape, 0)
    owner = (lax.broadcasted_iota(jnp.int32, wide.shape, 1) * 2731) >> 16
    wide = jnp.where((row >> 3) == owner, wide, 0.0)
    vectors_ref[...] = jnp.sum(wide.reshape(count, 8, model), 0)


def gather_chunks(weights):
    chunks = [("small", ((0, 128),))]
    for name, parts in (("out", 1), ("qkv", 3), ("up", 2), ("down", 2)):
        chunks += [(name, halves) for halves in pieces(weights[name].shape[2], parts)]
    return chunks


def first_kernel(near, table, room, chunks, *refs):
    it = iter(refs)
    tokens, docs = next(it), next(it)
    shards = {n: next(it) for n in NAMES}
    if near:
        shards["small"] = next(it)
    else:
        vectors = next(it)
    far = {n: next(it) for n in ("u",) + KEPT}
    if near:
        whole = {n: next(it) for n in NAMES}
        vectors = next(it)
    refs = list(it)
    v = room.bind(refs)
    sems = refs[len(room.names) :]
    mover = Mover(sems[0])
    w = {n: v["w_" + n] for n in NAMES}
    pump = None
    if near:
        gather = Gather(chunks, shards, {**w, "small": v["small"]}, sems[1:])
        pump = Pump(gather.step, staggered(len(chunks), 2, ("first", "second", "third", "fourth", "finish")))
        gather.links.greet()
        for one in pump.take(2):
            pump.run(*one)
    else:
        for n in NAMES:
            mover.start(shards[n], w[n], "w_" + n)
    make_bias(docs, v["bias"])
    if near:
        pump.until("finish", 0)
        spread_vectors(v["small"], vectors, 24)
    last = {name: n for n, (name, _) in enumerate(chunks)}

    def ready(name):
        if near:
            pump.until("finish", last[name])
            mover.start(w[name], whole[name], "whole_" + name)
        else:
            mover.wait("w_" + name)

    def hook(loops, count):
        return pump.hook(loops, count) if near else None

    def done(*names):
        for n in names:
            mover.start(v[n], far[n], "far_" + n)

    gains = [vectors[n : n + 1] for n in (1, 2)]
    forward_pass(tokens, None, v["bias"], gains, w, v, v["u"], vectors.at[0:1], ready, done, hook)
    mover.start(v["u"], far["u"], "far_u")
    if near:
        pump.rest()
        for n in range(len(chunks)):
            gather.step("close", n)
    mover.close()


def run_first(near, tokens, docs, small, vectors, shards):
    length, model = tokens.shape
    devices = 32 if near else 1
    weights = {n: jax.ShapeDtypeStruct((devices * s.shape[0],) + s.shape[1:], s.dtype) for n, s in shards.items()}
    table = shapes_of(length, model, weights["up"].shape[2], 1)
    room = Room()
    room.scratch(**{n: table[n] for n in KEPT + LOCAL + ("bias", "u")}, **{"w_" + n: weights[n] for n in NAMES})
    chunks = gather_chunks(weights) if near else []
    out_shape = [table[n] for n in ("u",) + KEPT]
    semaphores = [pltpu.SemaphoreType.DMA((24,))]
    params = dict(vmem_limit_bytes=VMEM_LIMIT)
    out_specs = [FAR] * len(out_shape)
    inputs = [tokens, docs] + [shards[n] for n in NAMES]
    if near:
        room.scratch(small=jax.ShapeDtypeStruct((32, 8, 128), jnp.bfloat16))
        out_shape += [weights[n] for n in NAMES] + [table["vectors"]]
        out_specs += [FAR] * 4 + [VMEM]
        semaphores += link_semaphores(len(chunks))
        params.update(collective_id=0, has_side_effects=True)
        inputs, in_specs = inputs + [small], [VMEM] * 2 + [FAR] * 5
    else:
        inputs, in_specs = inputs + [vectors], [VMEM] * 2 + [FAR] * 4 + [VMEM]
    outs = pl.pallas_call(
        functools.partial(first_kernel, near, table, room, chunks),
        out_shape=out_shape,
        in_specs=in_specs,
        out_specs=out_specs,
        scratch_shapes=room.shapes + semaphores,
        name="first",
        compiler_params=pltpu.CompilerParams(**params),
    )(*inputs)
    kept = dict(zip(("u",) + KEPT, outs))
    if near:
        return kept, outs[-1], dict(zip(NAMES, outs[1 + len(KEPT) :]))
    return kept, vectors, shards


def middle_kernel(table, room, *refs):
    it = iter(refs)
    u, docs, vectors = next(it), next(it), next(it)
    cotangent, qkv_before = next(it), next(it)
    weights = {n: next(it) for n in NAMES}
    ln1, ln2, whole = next(it), next(it), next(it)
    layer_out, du, dkv = next(it), next(it), next(it)
    grads = {n: next(it) for n in NAMES}
    refs = list(it)
    v = room.bind(refs)
    mover = Mover(refs[len(room.names)])
    w = {n: v["w_" + n] for n in NAMES}
    mover.start(weights["qkv"], w["qkv"], "w_qkv")
    mover.start(qkv_before, v["before"], "before")
    for n in NAMES[1:]:
        mover.start(weights[n], w[n], "w_" + n)
    mover.start(cotangent, v["dz"], "dz")
    make_bias(docs, v["bias"])
    gains = [vectors[n : n + 1] for n in (1, 2)]

    def ready(name):
        if name == "qkv":
            mover.wait("before")
        mover.wait("w_" + name)

    forward_pass(u, v["before"], v["bias"], gains, w, v, v["b"], None, ready)
    mover.start(v["b"], layer_out, "layer_out")
    mover.wait("dz")
    work = dict(dz=v["dz"], da=v["a"], do=v["bt"], dm=v["dm"], dhid=v["f"], dqkv=v["dqkv"], du=v["m"])

    def done(name):
        if name == "dkv":
            mover.start(v["dkv"], dkv, "dkv")
        elif name == "inputs":
            mover.start(v["m"], du, "du")
        elif name in NAMES:
            mover.start(w[name], grads[name], "g_" + name)

    backward_pass(
        v["dz"], u, [v["before"], v["qkv"]], [v["dkv"], None], gains, w, v, work, None, v["m"], (ln1, ln2), whole, no_wait, done
    )
    mover.close()


def no_wait(name):
    pass


def run_middle(u, docs, vectors, cotangent, qkv_before, weights):
    length, model = u.shape
    table = shapes_of(length, model, weights["up"].shape[2], 2)
    room = Room()
    room.scratch(**{n: table[n] for n in KEPT + LOCAL + ("bias", "dz", "dm", "dqkv", "dkv")}, before=table["qkv"])
    room.scratch(**{"w_" + n: weights[n] for n in NAMES})
    out_shape = [table["vectors"]] * 3 + [table["b"], table["u"], table["dkv"]] + [weights[n] for n in NAMES]
    outs = pl.pallas_call(
        functools.partial(middle_kernel, table, room),
        out_shape=out_shape,
        in_specs=[VMEM] * 3 + [FAR] * 6,
        out_specs=[VMEM] * 3 + [FAR] * 7,
        scratch_shapes=room.shapes + [pltpu.SemaphoreType.DMA((16,))],
        name="middle",
        compiler_params=pltpu.CompilerParams(vmem_limit_bytes=VMEM_LIMIT),
    )(u, docs, vectors, cotangent, qkv_before, *(weights[n] for n in NAMES))
    return outs[:3], outs[3], outs[4], outs[5], dict(zip(NAMES, outs[6:]))


LATE = {
    "down": [("begin", 0), ("begin", 1)],
    "hidden": [("first", 0)],
    "norm": [("first", 1)],
    "up": [("begin", 2), ("begin", 3), ("second", 0)],
    "out": [("begin", 4), ("second", 2)],
    "inputs": [("first", 4), ("third", 1)],
    "qkv": [("begin", 8), ("third", 2), ("first", 5), ("finish", 0)],
}
INSIDE = [[], [("first", 2)], [("second", 1)], [("first", 3)], [], [("third", 0)]]
TAIL = [
    ("second", 3), ("first", 6), ("finish", 1), ("second", 4), ("first", 7), ("third", 3), ("first", 8), ("second", 5), ("finish", 2),
    ("third", 4), ("second", 6), ("finish", 3), ("third", 5), ("second", 7), ("second", 8), ("finish", 4), ("third", 6), ("finish", 5),
    ("third", 7), ("third", 8), ("finish", 6), ("finish", 7), ("finish", 8),
]


def reduce_chunks(weights):
    chunks = []
    for name, parts in (("down", 2), ("up", 2), ("out", 1), ("qkv", 3)):
        chunks += [(name, halves) for halves in pieces(weights[name].shape[2], parts)]
    return chunks + [("small", ((0, 128),))]


def fold_vectors(vector, small, rows):
    count, model = small.shape[0], vector.shape[1]
    lane = lax.broadcasted_iota(jnp.int32, (128, model), 1)
    place = lax.broadcasted_iota(jnp.int32, (128, model), 0)
    block = (lane * 2731) >> 16
    pick = jnp.where(lane - block * rows == place, 1.0, 0.0).astype(jnp.bfloat16)
    wide = jnp.broadcast_to(vector[None], (count, 8, model)).reshape(count * 8, model)
    row = lax.broadcasted_iota(jnp.int32, wide.shape, 0)
    owner = (lax.broadcasted_iota(jnp.int32, wide.shape, 1) * 2731) >> 16
    wide = jnp.where((row >> 3) == owner, wide, 0.0).astype(jnp.bfloat16)
    small[...] = dot_nt(wide, pick).astype(jnp.bfloat16).reshape(small.shape)


def last_kernel(near, room, chunks, *refs):
    it = iter(refs)
    tokens, vectors, late1, late2, embed = next(it), next(it), next(it), next(it), next(it)
    far = {n: next(it) for n in ("upstream", "dkv") + KEPT}
    weights = {n: next(it) for n in NAMES}
    before = {n: next(it) for n in NAMES}
    du = next(it)
    outs = {n: next(it) for n in NAMES + ("small",)}
    refs = list(it)
    v = room.bind(refs)
    sems = refs[len(room.names) :]
    mover = Mover(sems[0])
    w = {n: v["w_" + n] for n in NAMES}
    mover.start(far["upstream"], v["upstream"], "upstream")
    mover.start(weights["down"], w["down"], "w_down")
    for n in ("gp", "ft"):
        mover.start(far[n], v[n], n)
    mover.start(weights["up"], w["up"], "w_up")
    for n in ("bt", "m"):
        mover.start(far[n], v[n], n)
    mover.start(weights["out"], w["out"], "w_out")
    for n in ("rl", "ot", "qkv", "p0", "p1", "dkv"):
        mover.start(far[n], v[n], n)
    mover.start(weights["qkv"], w["qkv"], "w_qkv")
    mover.start(far["at"], v["at"], "at")
    needs = {
        "upstream": ("upstream",),
        "down": ("w_down", "gp"),
        "ft": ("ft",),
        "up": ("w_up", "bt", "m"),
        "out": ("w_out", "rl", "ot"),
        "attention": ("qkv", "p0", "p1", "dkv"),
        "qkv": ("w_qkv", "at"),
    }

    def late(name, i=None):
        if i is None:
            mover.start(before[name], w[name], "late_" + name)
        else:
            block = pl.ds(i * 96, 96)
            mover.start(before[name].at[block], w[name].at[block], "late_%s%d" % (name, i))

    def ready(name):
        mover.wait(*needs.get(name, (name,)))

    hook = each = None
    if near:
        reduce = Reduce(
            chunks, {**w, "small": v["small"]}, *({n: v["r%d_%s" % (k, n)] for n in NAMES + ("small",)} for k in range(4)), outs, sems[1:]
        )
        reduce.links.greet()
        hook = at_steps(reduce.step, INSIDE)

        def each(i):
            reduce.step("begin", 5 + i)

    def run(events):
        for what, n in events:
            reduce.step(what, n)

    def done(name):
        if name == "inputs":
            mover.start(v["m"], du, "du")
            row = lax.broadcasted_iota(jnp.int32, embed.shape, 0)
            vector = jnp.where(row == 2, late2[...] + v["ln2"][...], 0.0)
            vector = jnp.where(row == 0, embed[...], jnp.where(row == 1, late1[...] + v["ln1"][...], vector))
            if near:
                fold_vectors(vector, v["small"], 24)
            else:
                outs["small"][...] = vector
        if near:
            run(LATE.get(name, ()))
        elif name in NAMES:
            mover.start(w[name], outs[name], "g_" + name)

    work = dict(dz=v["dz"], da=v["dz"], do=v["bt"], dm=v["dm"], dhid=v["gp"], dqkv=v["dqkv"])
    gains = [vectors[n : n + 1] for n in (1, 2)]
    backward_pass(
        v["upstream"], tokens, [v["qkv"]], [v["dkv"]], gains, w, v, work, late, v["m"], (v["ln1"], v["ln2"]), None, ready, done, hook, each
    )
    if near:
        run(TAIL)
        for n in range(len(chunks)):
            reduce.step("close", n)
    mover.close()


def run_last(near, tokens, vectors, late1, late2, embed, upstream, dkv, kept, weights, before):
    length, model = tokens.shape
    bf16 = jnp.bfloat16
    shape = jax.ShapeDtypeStruct
    table = shapes_of(length, model, weights["up"].shape[2], 1)
    room = Room()
    room.scratch(**{n: table[n] for n in KEPT + ("dz", "dm", "dqkv", "dkv")}, upstream=table["u"])
    room.scratch(ln1=table["vectors"], ln2=table["vectors"])
    room.scratch(**{"w_" + n: weights[n] for n in NAMES})
    chunks = reduce_chunks(weights) if near else []
    semaphores = [pltpu.SemaphoreType.DMA((32,))]
    params = dict(vmem_limit_bytes=VMEM_LIMIT)
    if near:
        parts = {**weights, "small": shape((32, 8, 128), bf16)}
        room.scratch(small=parts["small"])
        for k, blocks in enumerate((16, 8, 4, 3)):
            room.scratch(**{"r%d_%s" % (k, n): shape((p.shape[0] // 32 * blocks,) + p.shape[1:], bf16) for n, p in parts.items()})
        out_shape = [shape((parts[n].shape[0] // 32,) + parts[n].shape[1:], jnp.float32) for n in NAMES + ("small",)]
        out_specs = [VMEM] * 5
        semaphores += link_semaphores(len(chunks))
        params.update(collective_id=1, has_side_effects=True)
    else:
        out_shape = [weights[n] for n in NAMES] + [table["vectors"]]
        out_specs = [FAR] * 4 + [VMEM]
    outs = pl.pallas_call(
        functools.partial(last_kernel, near, room, chunks),
        out_shape=[table["u"]] + out_shape,
        in_specs=[VMEM] * 5 + [FAR] * (2 + len(KEPT) + 8),
        out_specs=[FAR] + out_specs,
        scratch_shapes=room.shapes + semaphores,
        name="last",
        compiler_params=pltpu.CompilerParams(**params),
    )(tokens, vectors, late1, late2, embed, upstream, dkv, *(kept[n] for n in KEPT), *(weights[n] for n in NAMES), *(before[n] for n in NAMES))
    return outs[0], dict(zip(NAMES, outs[1:])), outs[5]


AXES = ("dp", "fsdp")


def cut(w):
    return w.reshape(w.shape[0] // 8, 8, w.shape[1])


def join(w):
    return w.reshape(w.shape[0] * 8, w.shape[2])


def body(near, tokens, doc_ids, pass_embed, ln1_gain, w_qkv, w_out, ln2_gain, w_up, w_down, cotangent):
    shards = {"qkv": w_qkv, "out": w_out, "up": w_up, "down": w_down}
    docs = doc_ids.astype(jnp.float32).reshape(1, -1)
    rows = pass_embed.shape[0]
    small = vectors = None
    if near:
        small = jnp.zeros((1, 8, 128), jnp.bfloat16).at[0, :3, :rows].set(jnp.stack([pass_embed, ln1_gain, ln2_gain]))
        shards = {n: cut(s) for n, s in shards.items()}
    else:
        vectors = jnp.stack([lax.all_gather(v, AXES, axis=0, tiled=True) for v in (pass_embed, ln1_gain, ln2_gain)])
        vectors = jnp.pad(vectors.astype(jnp.float32), ((0, 5), (0, 0)))
        shards = {n: cut(lax.all_gather(s, AXES, axis=0, tiled=True)) for n, s in shards.items()}
    kept, vectors, weights = run_first(near, tokens, docs, small, vectors, shards)
    (late1, late2, embed), layer_out, second_g, dkv, late = run_middle(kept["u"], docs, vectors, cotangent, kept["qkv"], weights)
    tokens_grad, sums, small = run_last(near, tokens, vectors, late1, late2, embed, second_g, dkv, kept, weights, late)
    if near:
        sums = {n: join(s) for n, s in sums.items()}
        small = [small[0, n, :rows] for n in range(3)]
    else:
        scatter = lambda v: lax.psum_scatter(v, AXES, scatter_dimension=0, tiled=True)
        sums = {n: scatter(join(s).astype(jnp.float32)) for n, s in sums.items()}
        small = [scatter(small[n]) for n in range(3)]
    return (layer_out, tokens_grad, small[0], small[1], sums["qkv"], sums["out"], small[2], sums["up"], sums["down"])


def solution(mesh):
    near = dict(mesh.shape) == {"dp": 8, "fsdp": 4}
    placed = (
        P(("dp", "fsdp"), None),
        P(("dp", "fsdp")),
        P(("dp", "fsdp")),
        P(("dp", "fsdp")),
        P(("dp", "fsdp"), None),
        P(("dp", "fsdp"), None),
        P(("dp", "fsdp")),
        P(("dp", "fsdp"), None),
        P(("dp", "fsdp"), None),
        P(("dp", "fsdp"), None),
    )
    return jax.shard_map(
        functools.partial(body, near),
        mesh=mesh,
        in_specs=placed,
        out_specs=(
            P(("dp", "fsdp"), None),
            P(("dp", "fsdp"), None),
            P(("dp", "fsdp")),
            P(("dp", "fsdp")),
            P(("dp", "fsdp"), None),
            P(("dp", "fsdp"), None),
            P(("dp", "fsdp")),
            P(("dp", "fsdp"), None),
            P(("dp", "fsdp"), None),
        ),
        check_vma=False,
    )
```

```python
import functools
import math

import jax
import jax.numpy as jnp
from jax import lax
from jax.experimental import pallas as pl
from jax.experimental.pallas import tpu as pltpu
from jax.sharding import PartitionSpec as P

HEAD_DIM = 64


MESH = pl.DeviceIdType.MESH
NAMES = ("qkv", "out", "up", "down")


def pieces(width, parts):
    count = width // 128 // parts
    result = []
    for n in range(parts):
        first = (count + 1 - n % 2) // 2
        start = n * count * 128
        result.append(((start, first * 128), (start + first * 128, (count - first) * 128)))
    return result


class Links:
    def __init__(self, chunks):
        d, z = lax.axis_index("dp"), lax.axis_index("fsdp")
        y, x, c = d // 4, lax.rem(d // 2, 2), lax.rem(d, 2)
        self.z, self.y, self.x, self.c = z, y, x, c
        self.here = y * 2 + x
        self.sideways = (y * 4 + (1 - x) * 2 + c, z)
        self.upward = ((1 - y) * 4 + x * 2 + c, z)
        self.sibling = (y * 4 + x * 2 + 1 - c, z)
        self.along = [(d, lax.rem(z + k, 4)) for k in (1, 2, 3)]
        self.chunks = chunks

    def greet(self):
        peers = [self.sideways, self.upward, self.sibling, *self.along]
        barrier = pltpu.get_barrier_semaphore()
        for peer in peers:
            pl.semaphore_signal(barrier, inc=1, device_id=peer, device_id_type=MESH)
        pl.semaphore_wait(barrier, len(peers))

    def columns(self, n):
        halves = self.chunks[n][1]
        return pl.ds(halves[0][0], sum(size for _, size in halves))

    def hops(self, h):
        return (self.sideways, self.upward) if h == 0 else (self.upward, self.sideways)


def remote(src, dst, send, recv, peer):
    return pltpu.make_async_remote_copy(
        src_ref=src, dst_ref=dst, send_sem=send, recv_sem=recv, device_id=peer, device_id_type=MESH
    )


def link_semaphores(count):
    dma = pltpu.SemaphoreType.DMA
    return [dma((count, 3)), dma((count, 3)), dma((count, 2, 3)), dma((count, 2, 3)), dma((count, 4)), dma((count, 4)), dma((count,))]


class Gather:
    def __init__(self, chunks, shards, wholes, sems):
        self.links = Links(chunks)
        self.chunks, self.shards, self.wholes = chunks, shards, wholes
        self.z_send, self.z_recv, self.p_send, self.p_recv, self.d_send, self.d_recv, self.own_sem = sems

    def near(self, n, cols):
        name, at = self.chunks[n][0], self.links
        return self.shards[name].at[:, :, cols], self.wholes[name].at[at.here, at.c * 4 + at.z, :, :, cols]

    def line(self, n, chip, cols):
        return self.wholes[self.chunks[n][0]].at[chip, pl.ds(self.links.c * 4, 4), :, :, cols]

    def plane(self, n, z, cols):
        return self.wholes[self.chunks[n][0]].at[:, self.links.c * 4 + z, :, :, cols]

    def own(self, n):
        return pltpu.make_async_copy(*self.near(n, self.links.columns(n)), self.own_sem.at[n])

    def ahead(self, n, k):
        at, cols = self.links, self.links.columns(n)
        src, dst = self.near(n, cols)
        if self.chunks[n][2]:
            src = dst = self.plane(n, at.z, cols)
        return remote(src, dst, self.z_send.at[n, k], self.z_recv.at[n, k], at.along[k])

    def hop(self, n, h, i):
        at, cols = self.links, pl.ds(*self.chunks[n][1][h])
        one, two = at.hops(h)
        other = at.y * 2 + 1 - at.x if h == 0 else (1 - at.y) * 2 + at.x
        if self.chunks[n][2]:
            src, dst = self.near(n, cols)
            if i == 2:
                src = dst = self.wholes[self.chunks[n][0]].at[other, at.c * 4 + at.z, :, :, cols]
        else:
            src = dst = self.line(n, other if i == 2 else at.here, cols)
        return remote(src, dst, self.p_send.at[n, h, i], self.p_recv.at[n, h, i], one if i == 0 else two)

    def share(self, n, g):
        at, cols = self.links, self.links.columns(n)
        if self.chunks[n][2]:
            block = self.plane(n, lax.rem(at.z + 4 - g, 4), cols)
        else:
            y, x = (1 - at.y if g >= 2 else at.y), (1 - at.x if g % 2 else at.x)
            block = self.line(n, y * 2 + x, cols)
        return remote(block, block, self.d_send.at[n, g], self.d_recv.at[n, g], at.sibling)

    def halves(self, n):
        return range(len(self.chunks[n][1]))

    def step(self, what, n):
        if self.chunks[n][2]:
            self.plane_step(what, n)
        elif what == "begin":
            self.own(n).start()
            for k in range(3):
                self.ahead(n, k).start()
        elif what == "first":
            self.own(n).wait()
            for k in range(3):
                self.ahead(n, k).wait_recv()
            for h in self.halves(n):
                self.hop(n, h, 0).start()
                self.hop(n, h, 1).start()
            self.share(n, 0).start()
        elif what == "second":
            for h in self.halves(n):
                self.hop(n, h, 0).wait_recv()
                self.hop(n, h, 2).start()
        elif what == "third":
            for h in self.halves(n):
                self.hop(n, h, 1).wait_recv()
            self.share(n, 1).start()
            self.share(n, 2).start()
        elif what == "fourth":
            for h in self.halves(n):
                self.hop(n, h, 2).wait_recv()
            self.share(n, 3).start()
        if what == "finish":
            for g in range(4):
                self.share(n, g).wait_recv()
        elif what == "close":
            for k in range(3):
                self.ahead(n, k).wait_send()
            for h in self.halves(n):
                for i in range(3):
                    self.hop(n, h, i).wait_send()
            for g in range(4):
                self.share(n, g).wait_send()

    def plane_step(self, what, n):
        if what == "begin":
            self.own(n).start()
            for h in self.halves(n):
                self.hop(n, h, 0).start()
                self.hop(n, h, 1).start()
        elif what == "first":
            for h in self.halves(n):
                self.hop(n, h, 0).wait_recv()
                self.hop(n, h, 2).start()
        elif what == "second":
            self.own(n).wait()
            for h in self.halves(n):
                self.hop(n, h, 1).wait_recv()
                self.hop(n, h, 2).wait_recv()
            for k in range(3):
                self.ahead(n, k).start()
            self.share(n, 0).start()
        elif what == "third":
            for k in range(3):
                self.ahead(n, k).wait_recv()
                self.share(n, k + 1).start()


def in_turn(blocks, before, needs, after, step, mover):
    last = None
    for name in blocks:
        if last in after:
            after[last]()
        for event in before.get(name, ()):
            step(*event)
        mover.wait(*needs.get(name, ()))
        last = name


def events_before(order):
    stages = {"b": "begin", "1": "first", "2": "second", "3": "third", "4": "fourth", "f": "finish"}
    table, waiting = {}, []
    for word in order:
        if word[0] == "/":
            table[word[1:]], waiting = waiting, []
        else:
            waiting.append((stages[word[0]], int(word[1:])))
    table["end"] = table.get("end", []) + waiting
    return table


class Reduce:
    def __init__(self, chunks, parts, r0, r1, r2, r3, outs, sems):
        self.links = Links(chunks)
        self.chunks, self.parts, self.outs = chunks, parts, outs
        self.r0, self.r1, self.r2, self.r3 = r0, r1, r2, r3
        self.z_send, self.z_recv, self.p_send, self.p_recv, self.d_send, self.d_recv, _ = sems

    def share(self, n, g):
        at, name, cols = self.links, self.chunks[n][0], self.links.columns(n)
        src = self.parts[name].at[g, pl.ds((1 - at.c) * 4, 4), :, :, cols]
        return remote(src, self.r0[name].at[g, :, :, :, cols], self.d_send.at[n, g], self.d_recv.at[n, g], at.sibling)

    def hop(self, n, h, i):
        at, name, cols = self.links, self.chunks[n][0], pl.ds(*self.chunks[n][1][h])
        two, one = at.hops(h)
        far = 1 - at.x if h == 0 else 1 - at.y
        g = (1 - at.y) * 2 + i if h == 0 else i * 2 + 1 - at.x
        if self.chunks[n][2]:
            src = self.r3[name].at[far, :, :, cols] if i == 2 else self.r0[name].at[g, at.z, :, :, cols]
            dst = self.r3[name].at[i, :, :, cols]
        elif i == 2:
            src, dst = self.r1[name].at[far, :, :, :, cols], self.r2[name].at[:, :, :, cols]
        else:
            src, dst = self.r0[name].at[g, :, :, :, cols], self.r1[name].at[i, :, :, :, cols]
        return remote(src, dst, self.p_send.at[n, h, i], self.p_recv.at[n, h, i], one if i < 2 else two)

    def ahead(self, n, k):
        at, name, cols = self.links, self.chunks[n][0], self.links.columns(n)
        to = lax.rem(at.z + k + 1, 4)
        if self.chunks[n][2]:
            src = self.r0[name].at[:, to, :, :, cols]
            dst = self.r2[name].at[:, :, :, cols] if k == 2 else self.r1[name].at[k, :, :, :, cols]
        else:
            src, dst = self.r2[name].at[to, :, :, cols], self.r3[name].at[k, :, :, cols]
        return remote(src, dst, self.z_send.at[n, k], self.z_recv.at[n, k], at.along[k])

    def add(self, into, other, cols, steps):
        def one(i, carry):
            (ref, at), (source, place) = into(i), other(i)
            ref[*at, :, cols] = ref[*at, :, cols] + source[*place, :, cols]
            return carry

        lax.fori_loop(0, steps, one, 0, unroll=4 if steps % 4 == 0 else 3)

    def halves(self, n):
        return range(len(self.chunks[n][1]))

    def step(self, what, n):
        at, name = self.links, self.chunks[n][0]
        r0, r1, r2, r3, out = self.r0[name], self.r1[name], self.r2[name], self.r3[name], self.outs[name]
        rows = out.shape[0]
        cols = at.columns(n)
        by = lambda ref, *lead: lambda i: (ref, (*lead, i // rows, lax.rem(i, rows)))
        by_row = lambda ref, *lead: lambda i: (ref, (*lead, i))
        if what == "begin":
            for g in range(4):
                self.share(n, g).start()
        elif what == "first":
            for g in range(4):
                self.share(n, g).wait_recv()
                mine = lambda i, g=g: (self.parts[name], (g, at.c * 4 + i // rows, lax.rem(i, rows)))
                self.add(by(r0, g), mine, cols, 4 * rows)
            if self.chunks[n][2]:
                for k in range(3):
                    self.ahead(n, k).start()
            else:
                for h in self.halves(n):
                    self.hop(n, h, 0).start()
                    self.hop(n, h, 1).start()
        elif what == "close":
            for g in range(4):
                self.share(n, g).wait_send()
            for h in self.halves(n):
                for i in range(3):
                    self.hop(n, h, i).wait_send()
            for k in range(3):
                self.ahead(n, k).wait_send()
        elif self.chunks[n][2]:
            self.plane_step(what, n, rows, by_row)
        elif what == "second":
            for h in self.halves(n):
                half = pl.ds(*self.chunks[n][1][h])
                for i in range(2):
                    self.hop(n, h, i).wait_recv()
                    self.add(by(r1, i), by(r0, at.y * 2 + i if h == 0 else i * 2 + at.x), half, 4 * rows)
                self.hop(n, h, 2).start()
        elif what == "third":
            for h in self.halves(n):
                half = pl.ds(*self.chunks[n][1][h])
                self.hop(n, h, 2).wait_recv()
                self.add(by(r2), by(r1, at.x if h == 0 else at.y), half, 4 * rows)
            for k in range(3):
                self.ahead(n, k).start()
        elif what == "finish":
            for k in range(3):
                self.ahead(n, k).wait_recv()

            def one(i, carry):
                total = r2[at.z, i, :, cols].astype(jnp.float32)
                for k in range(3):
                    total = total + r3[k, i, :, cols].astype(jnp.float32)
                out[i, :, cols] = total
                return carry

            lax.fori_loop(0, rows, one, 0)

    def plane_step(self, what, n, rows, by_row):
        at, name = self.links, self.chunks[n][0]
        r0, r1, r2, r3, out = self.r0[name], self.r1[name], self.r2[name], self.r3[name], self.outs[name]
        cols = at.columns(n)
        if what == "second":
            for k in range(3):
                self.ahead(n, k).wait_recv()

            def one(i, carry):
                g, row = i // rows, lax.rem(i, rows)
                total = r0[g, at.z, row, :, cols].astype(jnp.float32)
                for part in (r1[0, g, row, :, cols], r1[1, g, row, :, cols], r2[g, row, :, cols]):
                    total = total + part.astype(jnp.float32)
                r0[g, at.z, row, :, cols] = total.astype(r0.dtype)
                return carry

            lax.fori_loop(0, 4 * rows, one, 0)
            for h in self.halves(n):
                self.hop(n, h, 0).start()
                self.hop(n, h, 1).start()
        elif what == "third":
            for h in self.halves(n):
                half = pl.ds(*self.chunks[n][1][h])
                for i in range(2):
                    self.hop(n, h, i).wait_recv()
                    g = at.y * 2 + i if h == 0 else i * 2 + at.x
                    self.add(by_row(r3, i), by_row(r0, g, at.z), half, rows)
                self.hop(n, h, 2).start()
        elif what == "finish":
            for h in self.halves(n):
                half = pl.ds(*self.chunks[n][1][h])
                self.hop(n, h, 2).wait_recv()
                near = at.x if h == 0 else at.y
                for row in range(rows):
                    out[row, :, half] = r3[near, row, :, half].astype(jnp.float32) + r3[2, row, :, half].astype(jnp.float32)


EPS = 1e-05
QB = 256
SCALE = HEAD_DIM ** (-0.5)
NT = (((1,), (1,)), ((), ()))


def dot(left, right):
    return jnp.dot(left, right, preferred_element_type=jnp.float32)


def dot_nt(left, right):
    return lax.dot_general(left, right, NT, preferred_element_type=jnp.float32)


def tiles(count, step, by=1):
    def go(i, carry):
        for k in range(by):
            step(i * by + k)
        return carry

    if by >= count:
        for k in range(count):
            step(k)
    else:
        lax.fori_loop(0, count // by, go, 0)


def at(i, size, start=0):
    if isinstance(i, int):
        return pl.ds(start + i * size, size)
    return pl.ds(pl.multiple_of(start + i * size, 128 if size % 128 == 0 else size), size)


def weight_columns(w, i, size):
    block = w[:, :, :, :, at(i, size)]
    return block.reshape(-1, size)


def weight_rows(w, i=None):
    block = w[...] if i is None else w[i]
    return block.reshape(-1, block.shape[-1])


def normal(u):
    center = u - jnp.mean(u, -1, keepdims=True)
    spread = lax.rsqrt(jnp.mean(center * center, -1, keepdims=True) + EPS)
    return center * spread, spread


def norm_rows(u_ref, gain, out_ref):
    def step(i):
        hat, spread = normal(u_ref[at(i, 128)].astype(jnp.float32))
        out_ref[at(i, 128)] = (hat * gain).astype(jnp.bfloat16)

    tiles(u_ref.shape[0] // 128, step)


def gelu_both(x):
    e = jnp.exp(x * x * -0.5)
    t = 1.0 / (1.0 + jnp.abs(x) * (0.3275911 * 0.5**0.5))
    poly = 0.5 * 1.061405429
    for term in (-1.453152027, 1.421413741, -0.284496736, 0.254829592):
        poly = poly * t + 0.5 * term
    tail = poly * t * e
    cdf = jnp.where(x >= 0, 1.0 - tail, tail)
    return x * cdf, cdf + x * e * (0.5 / math.pi) ** 0.5


def both_heads(block, axis):
    half = lax.broadcasted_iota(jnp.int32, block.shape, axis) < HEAD_DIM
    zero = jnp.zeros_like(block)
    return jnp.concatenate([jnp.where(half, block, zero), jnp.where(half, zero, block)], 1 - axis)


def own_heads(wide):
    count = wide.shape[1] // 2
    return jnp.concatenate([wide[:HEAD_DIM, :count], wide[HEAD_DIM:, count:]], 0)


def right(model, n, pair):
    return at(pair, 128, n * model)


def attend(qkvs, bias_ref, p_refs, rl_ref, o_ref, ot_ref, by=6, depth=2):
    model = o_ref.shape[1]
    own = qkvs[-1]

    def score(pair, b):
        span = (b + 1) * QB
        queries = both_heads(own[b * QB : span, at(pair, 128)] * SCALE, 1)
        bias = bias_ref[:span, b * QB : span]
        bias = jnp.concatenate([bias, bias], 1)
        return [dot_nt(ref[:span, right(model, 1, pair)], queries) + bias for ref in qkvs]

    def finish(pair, b, scores):
        span = (b + 1) * QB
        lanes = at(pair, 128)
        peak = jnp.max(scores[0], 0, keepdims=True)
        for s in scores[1:]:
            peak = jnp.maximum(peak, jnp.max(s, 0, keepdims=True))
        total, out = None, None
        for n, s in enumerate(scores):
            p = jnp.exp(s - peak)
            part = jnp.sum(p, 0, keepdims=True)
            p = p.astype(jnp.bfloat16)
            p_refs[b][pair, n * span : (n + 1) * span] = p
            product = dot(qkvs[n][:span, right(model, 2, pair)].T, p)
            total = part if total is None else total + part
            out = product if out is None else out + product
        scale = 1.0 / total
        rl_ref[pair, 0:1, b * QB : span] = scale[:, :QB]
        rl_ref[pair, 1:2, b * QB : span] = scale[:, QB:]
        out = own_heads(out * scale)
        ot_ref[at(pair, 128), b * QB : span] = out
        o_ref[b * QB : span, lanes] = out.astype(jnp.bfloat16).T

    def step(i):
        items = [(i * by + k, b) for k in range(by) for b in range(own.shape[0] // QB - 1, -1, -1)]
        waiting = []
        for n, item in enumerate(items):
            if n % (own.shape[0] // QB) == 0:
                yield "a%d" % item[0]
            waiting.append((item, score(*item)))
            if len(waiting) > depth:
                item, s = waiting.pop(0)
                finish(*item, s)
        for item, s in waiting:
            finish(*item, s)

    yield from step(0)


def attend_back(qkvs, p_refs, do_ref, ot_ref, dqkv_ref, dkv_refs):
    model = do_ref.shape[0]
    own = qkvs[-1]

    def step(pair):
        lanes = at(pair, 128)
        keys = [ref[:, right(model, 1, pair)] for ref in qkvs]
        values = [ref[:, right(model, 2, pair)] for ref in qkvs]
        turned = [k.T for k in keys]
        dk, dv = [None] * len(qkvs), [None] * len(qkvs)
        for b in reversed(range(own.shape[0] // QB)):
            span = (b + 1) * QB
            block = slice(b * QB, span)
            queries = both_heads(own[block, lanes] * SCALE, 1)
            do = do_ref[lanes, block]
            do_down, do_across = both_heads(do, 0), both_heads(do.T, 1)
            product = do.astype(jnp.float32) * ot_ref[lanes, block]
            delta = jnp.concatenate([jnp.sum(product[h * HEAD_DIM : (h + 1) * HEAD_DIM], 0, keepdims=True) for h in range(2)], 1)
            dq = None
            for n in range(len(qkvs)):
                p = p_refs[b][pair, n * span : (n + 1) * span]
                ds = dot(values[n][:span], do_down) - delta
                ds = (p.astype(jnp.float32) * ds).astype(jnp.bfloat16)
                more_dv, more_dk = dot(p, do_across), dot(ds, queries)
                more_dq = dot(turned[n][:, :span], ds)
                dq = more_dq if dq is None else dq + more_dq
                if dk[n] is None:
                    dk[n], dv[n] = more_dk, more_dv
                else:
                    dk[n] = jnp.concatenate([dk[n][:span] + more_dk, dk[n][span:]], 0)
                    dv[n] = jnp.concatenate([dv[n][:span] + more_dv, dv[n][span:]], 0)
            dqkv_ref[block, lanes] = (own_heads(dq) * SCALE).astype(jnp.bfloat16).T
        for n, ref in enumerate(dkv_refs):
            if ref is not None and n < len(qkvs) - 1:
                ref[:, lanes] = dk[n]
                ref[:, right(model, 1, pair)] = dv[n]
        extra = dkv_refs[-1]
        dk, dv = dk[-1], dv[-1]
        if extra is not None:
            dk, dv = dk + extra[:, lanes], dv + extra[:, right(model, 1, pair)]
        dqkv_ref[:, right(model, 1, pair)] = dk.astype(jnp.bfloat16)
        dqkv_ref[:, right(model, 2, pair)] = dv.astype(jnp.bfloat16)

    for pair in range(model // 128):
        yield "a%d" % pair
        step(pair)


def project(left_ref, w, add_ref, out_ref, shift, size, blocks):
    for i in blocks:
        value = dot(left_ref[...], weight_columns(w, i, size))
        if add_ref is not None:
            value = add_ref[:, at(i, size)].astype(jnp.float32) + value
        if shift is not None:
            value = value + shift[:, at(i, size)]
        out_ref[:, at(i, size)] = value.astype(out_ref.dtype)


def project_back(left_ref, w, out_ref):
    out_ref[...] = dot_nt(left_ref[...], weight_rows(w)).astype(out_ref.dtype)


def forward_pass(u_ref, qkv_before, bias_ref, gains, w, keep, out_ref, shift):
    yield "ln1"
    norm_rows(u_ref, gains[0], keep["a"])
    turn(keep["a"], keep["at"])
    for k in range(w["qkv"].shape[-1] // 768):
        yield "q%d" % k
        project(keep["a"], w["qkv"], None, keep["qkv"], None, 256, range(3 * k, 3 * k + 3))
    qkvs = [keep["qkv"]] if qkv_before is None else [qkv_before, keep["qkv"]]
    yield from attend(qkvs, bias_ref, [keep["p0"], keep["p1"]], keep["rl"], keep["o"], keep["ot"])
    yield "o"
    project(keep["o"], w["out"], u_ref, keep["m"], None, 256, range(3))
    yield "ln2"
    norm_rows(keep["m"], gains[1], keep["b"])
    turn(keep["b"], keep["bt"])
    for k in range(w["up"].shape[-1] // 768):
        yield "u%d" % k
        cols = at(k, 768)
        hidden = dot(keep["b"][...], weight_columns(w["up"], k, 768))
        active, slope = gelu_both(hidden)
        active = active.astype(jnp.bfloat16)
        keep["f"][:, cols] = active
        keep["ft"][cols] = active.T
        keep["gp"][:, cols] = slope.astype(jnp.bfloat16)
    for k in range(2):
        yield "d%d" % k
        project(keep["f"], w["down"], keep["m"], out_ref, shift, 384, (k,))
    yield "end"


def norm_back(u_ref, gain, dy_ref, add_ref, out_ref, rounded_ref, gain_grad_ref, sum_ref=None):
    def step(i, totals):
        total, whole = totals
        hat, spread = normal(u_ref[at(i, 128)].astype(jnp.float32))
        dy = dy_ref[at(i, 128)]
        total = total + jnp.sum((dy * hat).reshape(16, 8, dy.shape[1]), 0)
        dy = dy * gain
        down = dy - jnp.mean(dy, -1, keepdims=True) - hat * jnp.mean(dy * hat, -1, keepdims=True)
        value = add_ref[at(i, 128)].astype(jnp.float32) + spread * down
        out_ref[at(i, 128)] = value
        if rounded_ref is not None:
            rounded_ref[at(i, 128)] = value.astype(jnp.bfloat16)
        if sum_ref is not None:
            whole = whole + jnp.sum(value.reshape(16, 8, dy.shape[1]), 0)
        return total, whole

    zero = jnp.zeros((8, u_ref.shape[1]), jnp.float32)
    total, whole = lax.fori_loop(0, u_ref.shape[0] // 128, step, (zero, zero))
    gain_grad_ref[...] = jnp.broadcast_to(jnp.sum(total, 0, keepdims=True), gain_grad_ref.shape)
    if sum_ref is not None:
        sum_ref[...] = jnp.broadcast_to(jnp.sum(whole, 0, keepdims=True), sum_ref.shape)


def weight_grad(turned_ref, right_ref, out_ref, add, i, size=768):
    value = dot(turned_ref[...].astype(jnp.bfloat16), right_ref[:, at(i, size)])
    value = value.reshape(*out_ref.shape[:4], size)
    if add:
        value = value + out_ref[:, :, :, :, at(i, size)].astype(jnp.float32)
    out_ref[:, :, :, :, at(i, size)] = value.astype(out_ref.dtype)


def turn(ref, out_ref):
    def step(i):
        out_ref[at(i, 256)] = ref[:, at(i, 256)].T

    tiles(ref.shape[1] // 256, step)


def backward_pass(up_ref, u_ref, qkvs, dkv_refs, gains, w, keep, work, add, du_ref, gain_grads, sum_ref):
    yield "cast"
    dz = up_ref
    if up_ref.dtype != jnp.bfloat16:
        dz = work["dz"]

        def cast(i):
            dz[at(i, 128)] = up_ref[at(i, 128)].astype(jnp.bfloat16)

        tiles(up_ref.shape[0] // 128, cast)
    dhid = work["dhid"]
    for i in range(4):
        yield "b%d" % i
        value = dot_nt(dz[...], weight_rows(w["down"], i)) * keep["gp"][:, at(i, 768)].astype(jnp.float32)
        dhid[:, at(i, 768)] = value.astype(jnp.bfloat16)
    for i in range(2):
        yield "g%d" % i
        weight_grad(keep["ft"], dz, w["down"], add, i, 384)
    yield "ub"
    project_back(dhid, w["up"], work["dm"])
    yield "nb"
    norm_back(keep["m"], gains[1], work["dm"], up_ref, work["dm"], work["da"], gain_grads[1])
    for i in range(w["up"].shape[-1] // 768):
        yield "ug%d" % i
        weight_grad(keep["bt"], dhid, w["up"], add, i)
    yield "hg"
    do = dot_nt(weight_rows(w["out"]), work["da"][...])
    for h in range(do.shape[0] // HEAD_DIM):
        rows = slice(h * HEAD_DIM, (h + 1) * HEAD_DIM)
        work["do"][rows] = (do[rows] * keep["rl"][h // 2, h % 2 : h % 2 + 1]).astype(jnp.bfloat16)
    yield from attend_back(qkvs, [keep["p0"], keep["p1"]], work["do"], keep["ot"], work["dqkv"], dkv_refs)
    yield "og"
    weight_grad(keep["ot"], work["da"], w["out"], add, 0)
    yield "qb"
    project_back(work["dqkv"], w["qkv"], du_ref)
    yield "ni"
    norm_back(u_ref, gains[0], du_ref, work["dm"], du_ref, None, gain_grads[0], sum_ref)
    for i in range(w["qkv"].shape[-1] // 768):
        yield "qg%d" % i
        weight_grad(keep["at"], work["dqkv"], w["qkv"], add, i)
    yield "end"


KEPT = ("at", "qkv", "rl", "ot", "m", "bt", "ft", "gp", "p0", "p1")
LOCAL = ("a", "o", "b", "f")
NAMES_OF_WEIGHTS = tuple("w_" + n for n in NAMES)
VMEM_LIMIT = 63 << 20
VMEM = pl.BlockSpec(memory_space=pltpu.VMEM)
FAR = pl.BlockSpec(memory_space=pl.ANY)


def shapes_of(length, model, hidden, passes):
    f32, bf16 = jnp.float32, jnp.bfloat16
    shape = jax.ShapeDtypeStruct
    pairs = model // 128
    table = {
        "a": shape((length, model), bf16),
        "at": shape((model, length), bf16),
        "qkv": shape((length, 3 * model), bf16),
        "rl": shape((pairs, 2, length), f32),
        "o": shape((length, model), bf16),
        "ot": shape((model, length), f32),
        "m": shape((length, model), f32),
        "b": shape((length, model), bf16),
        "bt": shape((model, length), bf16),
        "f": shape((length, hidden), bf16),
        "ft": shape((hidden, length), bf16),
        "gp": shape((length, hidden), bf16),
        "dz": shape((length, model), bf16),
        "dm": shape((length, model), f32),
        "dqkv": shape((length, 3 * model), bf16),
        "dkv": shape((length, 2 * model), f32),
        "bias": shape((length, length), f32),
        "u": shape((length, model), f32),
        "vectors": shape((8, model), f32),
    }
    for b in range(length // QB):
        table["p%d" % b] = shape((pairs, passes * (b + 1) * QB, 2 * QB), bf16)
    return table


FIRST_ORDER = (
    "b3", "b2", "b1", "13", "b0", "b4", "12", "10", "b7", "/bias", "11", "23", "b5", "b6", "20", "22", "21", "14", "17", "30",
    "24", "33", "43", "34", "32", "40", "27", "42", "f2", "f0", "b8", "/vec", "37", "44", "15", "/ln1", "25", "f3", "f4", "16",
    "/q0", "/q1", "/q2", "/a0", "31", "/a1", "35", "47", "/a2", "41", "45", "26", "/a3", "/a4", "/a5", "36", "18", "f5", "f1",
    "46", "/o", "/ln2", "/u0", "28", "/u1", "f6", "/u2", "38", "/u3", "48", "f7", "/d0", "f8", "/d1",
)
LAST_ORDER = (
    "/cast", "/b0", "/b1", "/b2", "/b3", "/g0", "b0", "/g1", "b1", "10", "/ub", "11", "/nb", "/ug0", "/ug1", "20", "/ug2",
    "/ug3", "b2", "b3", "/hg", "21", "/a0", "12", "/a1", "13", "/a2", "31", "/a3", "/a4", "30", "/a5", "/og", "b4", "22", "/qb",
    "14", "/ni", "23", "32", "/qg0", "b5", "/qg1", "b6", "24", "15", "33", "/qg2", "16", "b7", "b8", "f0", "25", "17", "34",
    "26", "18", "35", "27", "f1", "36", "28", "38", "37", "f8", "f2", "f3", "f6", "f4", "f5", "f7",
)


class Room:
    def __init__(self):
        self.names, self.shapes, self.moves = [], [], []

    def scratch(self, **shapes):
        for name, s in shapes.items():
            self.names.append(name)
            self.shapes.append(pltpu.VMEM(s.shape, s.dtype))

    def bind(self, refs):
        return dict(zip(self.names, refs))


class Mover:
    def __init__(self, sems):
        self.sems, self.open, self.used = sems, {}, 0

    def start(self, src, dst, key):
        copy = pltpu.make_async_copy(src, dst, self.sems.at[self.used])
        self.used += 1
        copy.start()
        self.open[key] = copy

    def wait(self, *keys):
        for key in keys:
            if key in self.open:
                self.open.pop(key).wait()

    def close(self):
        self.wait(*list(self.open))


def make_bias(docs, bias_ref):
    length = bias_ref.shape[0]
    docs = docs[...].astype(jnp.float32)
    down = jnp.broadcast_to(docs, (128, length)).T

    def step(i):
        place_down = lax.broadcasted_iota(jnp.int32, (length, 128), 0)
        place_across = lax.broadcasted_iota(jnp.int32, (length, 128), 1) + i * 128
        seen = (down == docs[:, i * 128 : (i + 1) * 128]) & (place_down <= place_across)
        bias_ref[:, at(i, 128)] = jnp.where(seen, 0.0, -1e30)

    tiles(length // 128, step, length // 128)


def spread_vectors(small, vectors_ref, rows):
    count, model = small.shape[0] * small.shape[1], vectors_ref.shape[1]
    lane = lax.broadcasted_iota(jnp.int32, (128, model), 1)
    place = lax.broadcasted_iota(jnp.int32, (128, model), 0)
    block = (lane * 2731) >> 16
    pick = jnp.where(lane - block * rows == place, 1.0, 0.0).astype(jnp.bfloat16)
    wide = dot(small[...].reshape(-1, 128), pick)
    row = lax.broadcasted_iota(jnp.int32, wide.shape, 0)
    owner = (lax.broadcasted_iota(jnp.int32, wide.shape, 1) * 2731) >> 16
    wide = jnp.where((row >> 3) == owner, wide, 0.0)
    vectors_ref[...] = jnp.sum(wide.reshape(count, 8, model), 0)


def gather_chunks(weights):
    chunks = [("small", ((0, 128),), False)]
    for name, parts in (("out", 1), ("qkv", 3), ("up", 2), ("down", 2)):
        chunks += [(name, halves, name == "out") for halves in pieces(weights[name].shape[-1], parts)]
    return chunks


def first_kernel(near, table, room, chunks, *refs):
    it = iter(refs)
    tokens, docs = next(it), next(it)
    shards = {n: next(it) for n in NAMES}
    if near:
        shards["small"] = next(it)
    else:
        vectors = next(it)
    far = {n: next(it) for n in ("u",) + KEPT}
    if near:
        whole = {n: next(it) for n in NAMES}
        vectors = next(it)
    refs = list(it)
    v = room.bind(refs)
    sems = refs[len(room.names) :]
    mover = Mover(sems[0])
    w = {n: v["w_" + n] for n in NAMES}
    gather = None
    before, needs = {}, {}
    if near:
        gather = Gather(chunks, shards, {**w, "small": v["small"]}, sems[1:])
        gather.links.greet()
        before = events_before(FIRST_ORDER)
    else:
        for n in NAMES:
            mover.start(shards[n], w[n], "w_" + n)
        needs = {"q0": ("w_qkv",), "o": ("w_out",), "u0": ("w_up",), "d0": ("w_down",)}

    def keep(*names):
        def go():
            for n in names:
                mover.start(v[n], far[n], "far_" + n)

        return go

    after = {
        "ln1": keep("at"),
        "q2": keep("qkv"),
        "a5": keep("p0", "p1", "rl", "ot"),
        "ln2": keep("m", "bt"),
        "u3": keep("ft", "gp"),
        "d1": keep("u"),
    }
    finished = []

    def step(what, n):
        gather.step(what, n)
        if what == "finish":
            finished.append(n)
            name = chunks[n][0]
            if name in NAMES and all(k in finished for k, chunk in enumerate(chunks) if chunk[0] == name):
                mover.start(w[name], whole[name], "whole_" + name)

    def blocks():
        yield "bias"
        make_bias(docs, v["bias"])
        yield "vec"
        if near:
            spread_vectors(v["small"], vectors, 24)
        gains = [vectors[n : n + 1] for n in (1, 2)]
        yield from forward_pass(tokens, None, v["bias"], gains, w, v, v["u"], vectors.at[0:1])

    in_turn(blocks(), before, needs, after, step, mover)
    if near:
        for n in range(len(chunks)):
            gather.step("close", n)
    mover.close()


def run_first(near, tokens, docs, small, vectors, shards):
    length, model = tokens.shape
    weights = shards
    if near:
        weights = {n: jax.ShapeDtypeStruct((4, 8) + s.shape, s.dtype) for n, s in shards.items()}
    table = shapes_of(length, model, weights["up"].shape[-1], 1)
    room = Room()
    room.scratch(**{n: table[n] for n in KEPT + LOCAL + ("bias", "u")}, **{"w_" + n: weights[n] for n in NAMES})
    chunks = gather_chunks(weights) if near else []
    out_shape = [table[n] for n in ("u",) + KEPT]
    semaphores = [pltpu.SemaphoreType.DMA((24,))]
    params = dict(vmem_limit_bytes=VMEM_LIMIT)
    out_specs = [FAR] * len(out_shape)
    inputs = [tokens, docs] + [shards[n] for n in NAMES]
    if near:
        room.scratch(small=jax.ShapeDtypeStruct((4, 8, 1, 8, 128), jnp.bfloat16))
        out_shape += [weights[n] for n in NAMES] + [table["vectors"]]
        out_specs += [FAR] * 4 + [VMEM]
        semaphores += link_semaphores(len(chunks))
        params.update(collective_id=0, has_side_effects=True)
        inputs, in_specs = inputs + [small], [VMEM] * 2 + [FAR] * 5
    else:
        inputs, in_specs = inputs + [vectors], [VMEM] * 2 + [FAR] * 4 + [VMEM]
    outs = pl.pallas_call(
        functools.partial(first_kernel, near, table, room, chunks),
        out_shape=out_shape,
        in_specs=in_specs,
        out_specs=out_specs,
        scratch_shapes=room.shapes + semaphores,
        name="first",
        compiler_params=pltpu.CompilerParams(**params),
    )(*inputs)
    kept = dict(zip(("u",) + KEPT, outs))
    if near:
        return kept, outs[-1], dict(zip(NAMES, outs[1 + len(KEPT) :]))
    return kept, vectors, shards


def middle_kernel(table, room, *refs):
    it = iter(refs)
    u, docs, vectors = next(it), next(it), next(it)
    cotangent, qkv_before = next(it), next(it)
    weights = {n: next(it) for n in NAMES}
    ln1, ln2, whole = next(it), next(it), next(it)
    layer_out, du, dkv = next(it), next(it), next(it)
    grads = {n: next(it) for n in NAMES}
    refs = list(it)
    v = room.bind(refs)
    mover = Mover(refs[len(room.names)])
    w = {n: v["w_" + n] for n in NAMES}
    mover.start(weights["qkv"], w["qkv"], "w_qkv")
    mover.start(qkv_before, v["before"], "before")
    for n in NAMES[1:]:
        mover.start(weights[n], w[n], "w_" + n)
    mover.start(cotangent, v["dz"], "dz")
    gains = [vectors[n : n + 1] for n in (1, 2)]
    needs = {"q0": ("w_qkv",), "a0": ("before",), "o": ("w_out",), "u0": ("w_up",), "d0": ("w_down",), "cast": ("dz",)}

    def store(src, dst):
        return lambda: mover.start(src, dst, id(dst))

    after = {
        "d1": store(v["b"], layer_out),
        "g1": store(w["down"], grads["down"]),
        "ug3": store(w["up"], grads["up"]),
        "og": store(w["out"], grads["out"]),
        "qg2": store(w["qkv"], grads["qkv"]),
        "a5": store(v["dkv"], dkv),
        "ni": store(v["m"], du),
    }
    work = dict(dz=v["dz"], da=v["a"], do=v["bt"], dm=v["dm"], dhid=v["f"], dqkv=v["dqkv"])
    first = forward_pass(u, v["before"], v["bias"], gains, w, v, v["b"], None)
    make_bias(docs, v["bias"])
    in_turn(first, {}, needs, {}, None, mover)
    after["d1"]()
    second = backward_pass(
        v["dz"], u, [v["before"], v["qkv"]], [v["dkv"], None], gains, w, v, work, False, v["m"], (ln1, ln2), whole
    )
    in_turn(second, {}, needs, after, None, mover)
    mover.close()


def run_middle(u, docs, vectors, cotangent, qkv_before, weights):
    length, model = u.shape
    table = shapes_of(length, model, weights["up"].shape[-1], 2)
    room = Room()
    room.scratch(**{n: table[n] for n in KEPT + LOCAL + ("bias", "dz", "dm", "dqkv", "dkv")}, before=table["qkv"])
    room.scratch(**{"w_" + n: weights[n] for n in NAMES})
    out_shape = [table["vectors"]] * 3 + [table["b"], table["u"], table["dkv"]] + [weights[n] for n in NAMES]
    outs = pl.pallas_call(
        functools.partial(middle_kernel, table, room),
        out_shape=out_shape,
        in_specs=[VMEM] * 3 + [FAR] * 6,
        out_specs=[VMEM] * 3 + [FAR] * 7,
        scratch_shapes=room.shapes + [pltpu.SemaphoreType.DMA((16,))],
        name="middle",
        compiler_params=pltpu.CompilerParams(vmem_limit_bytes=VMEM_LIMIT),
    )(u, docs, vectors, cotangent, qkv_before, *(weights[n] for n in NAMES))
    return outs[:3], outs[3], outs[4], outs[5], dict(zip(NAMES, outs[6:]))


def reduce_chunks(weights):
    chunks = []
    for name, parts in (("down", 2), ("up", 2), ("out", 1), ("qkv", 3)):
        chunks += [(name, halves, False) for halves in pieces(weights[name].shape[-1], parts)]
    return chunks + [("small", ((0, 128),), False)]


def fold_vectors(vector, small, rows):
    count, model = small.shape[0] * small.shape[1], vector.shape[1]
    lane = lax.broadcasted_iota(jnp.int32, (128, model), 1)
    place = lax.broadcasted_iota(jnp.int32, (128, model), 0)
    block = (lane * 2731) >> 16
    pick = jnp.where(lane - block * rows == place, 1.0, 0.0).astype(jnp.bfloat16)
    wide = jnp.broadcast_to(vector[None], (count, 8, model)).reshape(count * 8, model)
    row = lax.broadcasted_iota(jnp.int32, wide.shape, 0)
    owner = (lax.broadcasted_iota(jnp.int32, wide.shape, 1) * 2731) >> 16
    wide = jnp.where((row >> 3) == owner, wide, 0.0).astype(jnp.bfloat16)
    small[...] = dot_nt(wide, pick).astype(jnp.bfloat16).reshape(small.shape)


def last_kernel(near, room, chunks, *refs):
    it = iter(refs)
    tokens, vectors, late1, late2, embed = next(it), next(it), next(it), next(it), next(it)
    far = {n: next(it) for n in ("upstream", "dkv") + KEPT}
    weights = {n: next(it) for n in NAMES}
    before = {n: next(it) for n in NAMES}
    du = next(it)
    outs = {n: next(it) for n in NAMES + ("small",)}
    refs = list(it)
    v = room.bind(refs)
    sems = refs[len(room.names) :]
    mover = Mover(sems[0])
    w = {n: v["w_" + n] for n in NAMES}
    def load(*names):
        def go():
            for n in names:
                if n in NAMES_OF_WEIGHTS:
                    mover.start(weights[n[2:]], w[n[2:]], n)
                else:
                    mover.start(far[n], v[n], n)

        return go

    def late(name, i=None, *names):
        def go():
            if i is None:
                mover.start(before[name], w[name], "late_" + name)
            else:
                mover.start(before[name].at[i], w[name].at[i], "late_%s%d" % (name, i))
            load(*names)()

        return go

    mover.start(far["upstream"], v["upstream"], "upstream")
    for i in range(4):
        cols = at(i, 768)
        mover.start(weights["down"].at[i], w["down"].at[i], "w_down%d" % i)
        mover.start(far["gp"].at[:, cols], v["gp"].at[:, cols], "gp%d" % i)
    needs = {
        "cast": ("upstream",),
        "b0": ("w_down0", "gp0"),
        "b1": ("w_down1", "gp1"),
        "b2": ("w_down2", "gp2"),
        "b3": ("w_down3", "gp3"),
        "g0": ("ft", "late_down0", "late_down1", "late_down2", "late_down3"),
        "ub": ("w_up",),
        "nb": ("m",),
        "ug0": ("bt", "late_up"),
        "hg": ("w_out", "rl"),
        "a0": ("qkv", "p0", "p1", "dkv", "ot"),
        "og": ("late_out",),
        "qb": ("w_qkv",),
        "qg0": ("at", "late_qkv"),
    }
    reduce = None
    events = {}
    if near:
        reduce = Reduce(
            chunks, {**w, "small": v["small"]}, *({n: v["r%d_%s" % (k, n)] for n in NAMES + ("small",)} for k in range(4)), outs, sems[1:]
        )
        reduce.links.greet()
        events = events_before(LAST_ORDER)

    def inputs_done():
        mover.start(v["m"], du, "du")
        row = lax.broadcasted_iota(jnp.int32, embed.shape, 0)
        vector = jnp.where(row == 2, late2[...] + v["ln2"][...], 0.0)
        vector = jnp.where(row == 0, embed[...], jnp.where(row == 1, late1[...] + v["ln1"][...], vector))
        if near:
            fold_vectors(vector, v["small"], 24)
        else:
            outs["small"][...] = vector

    after = {
        "b0": late("down", 0, "ft"),
        "b1": late("down", 1, "w_up"),
        "b2": late("down", 2, "m"),
        "b3": late("down", 3, "bt", "w_out", "rl"),
        "g1": load("qkv", "p0", "p1", "ot"),
        "ub": late("up"),
        "nb": load("dkv"),
        "hg": late("out"),
        "a0": load("w_qkv", "at"),
        "qb": late("qkv"),
        "ni": inputs_done,
    }
    if not near:
        stores = {"g1": "down", "ug3": "up", "og": "out", "qg2": "qkv"}
        for block, name in stores.items():

            def store(name=name, then=after.get(block)):
                mover.start(w[name], outs[name], "g_" + name)
                if then:
                    then()

            after[block] = store
    work = dict(dz=v["dz"], da=v["dz"], do=v["bt"], dm=v["dm"], dhid=v["gp"], dqkv=v["dqkv"])
    gains = [vectors[n : n + 1] for n in (1, 2)]
    blocks = backward_pass(
        v["upstream"], tokens, [v["qkv"]], [v["dkv"]], gains, w, v, work, True, v["m"], (v["ln1"], v["ln2"]), None
    )
    in_turn(blocks, events, needs, after, reduce and reduce.step, mover)
    if near:
        for n in range(len(chunks)):
            reduce.step("close", n)
    mover.close()


def run_last(near, tokens, vectors, late1, late2, embed, upstream, dkv, kept, weights, before):
    length, model = tokens.shape
    bf16 = jnp.bfloat16
    shape = jax.ShapeDtypeStruct
    table = shapes_of(length, model, weights["up"].shape[-1], 1)
    room = Room()
    room.scratch(**{n: table[n] for n in KEPT + ("dz", "dm", "dqkv", "dkv")}, upstream=table["u"])
    room.scratch(ln1=table["vectors"], ln2=table["vectors"])
    room.scratch(**{"w_" + n: weights[n] for n in NAMES})
    chunks = reduce_chunks(weights) if near else []
    semaphores = [pltpu.SemaphoreType.DMA((40,))]
    params = dict(vmem_limit_bytes=VMEM_LIMIT)
    if near:
        parts = {**weights, "small": shape((4, 8, 1, 8, 128), bf16)}
        room.scratch(small=parts["small"])
        for k, blocks in enumerate(((4, 4), (2, 4), (4,), (3,))):
            room.scratch(**{"r%d_%s" % (k, n): shape(blocks + p.shape[2:], bf16) for n, p in parts.items()})
        out_shape = [shape(parts[n].shape[2:], jnp.float32) for n in NAMES + ("small",)]
        out_specs = [VMEM] * 5
        semaphores += link_semaphores(len(chunks))
        params.update(collective_id=1, has_side_effects=True)
    else:
        out_shape = [weights[n] for n in NAMES] + [table["vectors"]]
        out_specs = [FAR] * 4 + [VMEM]
    outs = pl.pallas_call(
        functools.partial(last_kernel, near, room, chunks),
        out_shape=[table["u"]] + out_shape,
        in_specs=[VMEM] * 5 + [FAR] * (2 + len(KEPT) + 8),
        out_specs=[FAR] + out_specs,
        scratch_shapes=room.shapes + semaphores,
        name="last",
        compiler_params=pltpu.CompilerParams(**params),
    )(tokens, vectors, late1, late2, embed, upstream, dkv, *(kept[n] for n in KEPT), *(weights[n] for n in NAMES), *(before[n] for n in NAMES))
    return outs[0], dict(zip(NAMES, outs[1:])), outs[5]


AXES = ("dp", "fsdp")


def cut(w):
    return w.reshape(w.shape[0] // 8, 8, w.shape[1])


def join(w):
    return w.reshape(-1, w.shape[-1])


def whole(w):
    return w.reshape(4, 8, w.shape[0] // 256, 8, w.shape[1])


def body(near, tokens, doc_ids, pass_embed, ln1_gain, w_qkv, w_out, ln2_gain, w_up, w_down, cotangent):
    shards = {"qkv": w_qkv, "out": w_out, "up": w_up, "down": w_down}
    docs = doc_ids.reshape(1, -1)
    rows = pass_embed.shape[0]
    small = vectors = None
    if near:
        wide = [jnp.pad(v[None], ((n, 7 - n), (0, 128 - rows))) for n, v in enumerate((pass_embed, ln1_gain, ln2_gain))]
        small = (wide[0] + wide[1] + wide[2])[None]
        shards = {n: cut(s) for n, s in shards.items()}
    else:
        vectors = jnp.stack([lax.all_gather(v, AXES, axis=0, tiled=True) for v in (pass_embed, ln1_gain, ln2_gain)])
        vectors = jnp.pad(vectors.astype(jnp.float32), ((0, 5), (0, 0)))
        shards = {n: whole(lax.all_gather(s, AXES, axis=0, tiled=True)) for n, s in shards.items()}
    kept, vectors, weights = run_first(near, tokens, docs, small, vectors, shards)
    (late1, late2, embed), layer_out, second_g, dkv, late = run_middle(kept["u"], docs, vectors, cotangent, kept["qkv"], weights)
    tokens_grad, sums, small = run_last(near, tokens, vectors, late1, late2, embed, second_g, dkv, kept, weights, late)
    if near:
        sums = {n: join(s) for n, s in sums.items()}
        small = [small[0, n, :rows] for n in range(3)]
    else:
        scatter = lambda v: lax.psum_scatter(v, AXES, scatter_dimension=0, tiled=True)
        sums = {n: scatter(join(s).astype(jnp.float32)) for n, s in sums.items()}
        small = [scatter(small[n]) for n in range(3)]
    return (layer_out, tokens_grad, small[0], small[1], sums["qkv"], sums["out"], small[2], sums["up"], sums["down"])


def solution(mesh):
    near = dict(mesh.shape) == {"dp": 8, "fsdp": 4}
    placed = (
        P(("dp", "fsdp"), None),
        P(("dp", "fsdp")),
        P(("dp", "fsdp")),
        P(("dp", "fsdp")),
        P(("dp", "fsdp"), None),
        P(("dp", "fsdp"), None),
        P(("dp", "fsdp")),
        P(("dp", "fsdp"), None),
        P(("dp", "fsdp"), None),
        P(("dp", "fsdp"), None),
    )
    return jax.shard_map(
        functools.partial(body, near),
        mesh=mesh,
        in_specs=placed,
        out_specs=(
            P(("dp", "fsdp"), None),
            P(("dp", "fsdp"), None),
            P(("dp", "fsdp")),
            P(("dp", "fsdp")),
            P(("dp", "fsdp"), None),
            P(("dp", "fsdp"), None),
            P(("dp", "fsdp")),
            P(("dp", "fsdp"), None),
            P(("dp", "fsdp"), None),
        ),
        check_vma=False,
    )
```

```python
import functools
import math

import jax
import jax.numpy as jnp
from jax import lax
from jax.experimental import pallas as pl
from jax.experimental.pallas import tpu as pltpu
from jax.sharding import PartitionSpec as P

HEAD_DIM = 64


MESH = pl.DeviceIdType.MESH
NAMES = ("qkv", "out", "up", "down")


def pieces(width, parts):
    count = width // 128 // parts
    result = []
    for n in range(parts):
        first = (count + 1 - n % 2) // 2
        start = n * count * 128
        result.append(((start, first * 128), (start + first * 128, (count - first) * 128)))
    return result


class Links:
    def __init__(self, chunks):
        d, z = lax.axis_index("dp"), lax.axis_index("fsdp")
        y, x, c = d // 4, lax.rem(d // 2, 2), lax.rem(d, 2)
        self.z, self.y, self.x, self.c = z, y, x, c
        self.sideways = (y * 4 + (1 - x) * 2 + c, z)
        self.upward = ((1 - y) * 4 + x * 2 + c, z)
        self.sibling = (y * 4 + x * 2 + 1 - c, z)
        self.along = [(d, lax.rem(z + k, 4)) for k in (1, 2, 3)]
        self.chunks = chunks

    def greet(self):
        peers = [self.sideways, self.upward, self.sibling, *self.along]
        barrier = pltpu.get_barrier_semaphore()
        for peer in peers:
            pl.semaphore_signal(barrier, inc=1, device_id=peer, device_id_type=MESH)
        pl.semaphore_wait(barrier, len(peers))

    def columns(self, n):
        halves = self.chunks[n][1]
        return pl.ds(halves[0][0], sum(size for _, size in halves))

    def hops(self, h):
        return (self.sideways, self.upward) if h == 0 else (self.upward, self.sideways)


def remote(src, dst, send, recv, peer):
    return pltpu.make_async_remote_copy(
        src_ref=src, dst_ref=dst, send_sem=send, recv_sem=recv, device_id=peer, device_id_type=MESH
    )


def link_semaphores(count):
    dma = pltpu.SemaphoreType.DMA
    return [dma((count,)), dma((count,)), dma((count, 2, 2)), dma((count, 2, 3)), dma((count,)), dma((count, 2)), dma((count,))]


class Gather:
    def __init__(self, chunks, shards, wholes, sems):
        self.links = Links(chunks)
        self.chunks, self.shards, self.wholes = chunks, shards, wholes
        self.z_send, self.z_recv, self.p_send, self.p_recv, self.d_send, self.d_recv, self.own_sem = sems

    def near(self, n, cols):
        name, at = self.chunks[n][0], self.links
        return self.shards[name].at[:, :, cols], self.wholes[name].at[at.y, at.x, at.c * 4 + at.z, :, :, cols]

    def line(self, n, y, x, cols):
        return self.wholes[self.chunks[n][0]].at[y, x, pl.ds(self.links.c * 4, 4), :, :, cols]

    def plane(self, n, z, cols):
        return self.wholes[self.chunks[n][0]].at[:, :, self.links.c * 4 + z, :, :, cols]

    def own(self, n):
        return pltpu.make_async_copy(*self.near(n, self.links.columns(n)), self.own_sem.at[n])

    def ahead(self, n, k):
        at, cols = self.links, self.links.columns(n)
        src, dst = self.near(n, cols)
        if self.chunks[n][2]:
            src = dst = self.plane(n, at.z, cols)
        if k is None:
            whole = self.wholes[self.chunks[n][0]]
            src = dst = whole.at[:, :, pl.ds(0, 3), :, :, cols] if self.chunks[n][2] else whole.at[0, 0, pl.ds(0, 3), :, :, cols]
        return remote(src, dst, self.z_send.at[n], self.z_recv.at[n], at.along[k or 0])

    def hop(self, n, h, i):
        at, cols = self.links, pl.ds(*self.chunks[n][1][h])
        one, two = at.hops(h)
        other = (at.y, 1 - at.x) if h == 0 else (1 - at.y, at.x)
        if self.chunks[n][2]:
            src, dst = self.near(n, cols)
            if i == 2:
                src = dst = self.wholes[self.chunks[n][0]].at[*other, at.c * 4 + at.z, :, :, cols]
        else:
            src = dst = self.line(n, *(other if i == 2 else (at.y, at.x)), cols)
        return remote(src, dst, self.p_send.at[n, h, int(i == 2)], self.p_recv.at[n, h, i], one if i == 0 else two)

    def both_hops(self, n, h):
        cols, whole = pl.ds(*self.chunks[n][1][h]), self.wholes[self.chunks[n][0]]
        block = whole.at[0, :, 0, :, :, cols] if self.chunks[n][2] else whole.at[0, :, pl.ds(0, 4), :, :, cols]
        return remote(block, block, self.p_send.at[n, h, 0], self.p_recv.at[n, h, 0], self.links.sideways)

    def share(self, n, g):
        at, cols = self.links, self.links.columns(n)
        whole, lines = self.wholes[self.chunks[n][0]], pl.ds(at.c * 4, 4)
        if self.chunks[n][2] or g is None:
            block = whole.at[:, :, lines, :, :, cols]
        else:
            block = whole.at[1 - at.y if g else at.y, :, lines, :, :, cols]
        return remote(block, block, self.d_send.at[n], self.d_recv.at[n, g or 0], at.sibling)

    def halves(self, n):
        return range(len(self.chunks[n][1]))

    def step(self, what, n):
        if self.chunks[n][2]:
            self.plane_step(what, n)
        elif what == "begin":
            self.own(n).start()
            for k in range(3):
                self.ahead(n, k).start()
        elif what == "first":
            self.own(n).wait()
            self.ahead(n, None).wait_recv()
            for h in self.halves(n):
                self.hop(n, h, 0).start()
                self.hop(n, h, 1).start()
        elif what == "second":
            for h in self.halves(n):
                self.hop(n, h, 0).wait_recv()
                self.hop(n, h, 2).start()
        elif what == "third":
            for h in self.halves(n):
                self.hop(n, h, 1).wait_recv()
            self.share(n, 0).start()
        elif what == "fourth":
            for h in self.halves(n):
                self.hop(n, h, 2).wait_recv()
            self.share(n, 1).start()
        elif what == "finish":
            for g in range(2):
                self.share(n, g).wait_recv()
        if what == "close":
            self.ahead(n, None).wait_send()
            for h in self.halves(n):
                self.both_hops(n, h).wait_send()
                self.hop(n, h, 2).wait_send()
            self.share(n, None).wait_send()

    def plane_step(self, what, n):
        if what == "begin":
            self.own(n).start()
            for h in self.halves(n):
                self.hop(n, h, 0).start()
                self.hop(n, h, 1).start()
        elif what == "first":
            for h in self.halves(n):
                self.hop(n, h, 0).wait_recv()
                self.hop(n, h, 2).start()
        elif what == "second":
            self.own(n).wait()
            for h in self.halves(n):
                self.hop(n, h, 1).wait_recv()
                self.hop(n, h, 2).wait_recv()
            for k in range(3):
                self.ahead(n, k).start()
        elif what == "third":
            self.ahead(n, None).wait_recv()
            self.share(n, 0).start()
        elif what == "finish":
            self.share(n, 0).wait_recv()


def in_turn(blocks, before, needs, after, step, mover):
    last = None
    for name in blocks:
        if last in after:
            after[last]()
        for event in before.get(name, ()):
            step(*event)
        mover.wait(*needs.get(name, ()))
        last = name


def events_before(order):
    stages = {"b": "begin", "1": "first", "2": "second", "3": "third", "4": "fourth", "f": "finish"}
    table, waiting = {}, []
    for word in order:
        if word[0] == "/":
            table[word[1:]], waiting = waiting, []
        else:
            waiting.append((stages[word[0]], int(word[1:])))
    table["end"] = table.get("end", []) + waiting
    return table


class Reduce:
    def __init__(self, chunks, parts, r0, r1, r2, r3, outs, sems):
        self.links = Links(chunks)
        self.chunks, self.parts, self.outs = chunks, parts, outs
        self.r0, self.r1, self.r2, self.r3 = r0, r1, r2, r3
        self.z_send, self.z_recv, self.p_send, self.p_recv, self.d_send, self.d_recv, _ = sems

    def share(self, n):
        at, name, cols = self.links, self.chunks[n][0], self.links.columns(n)
        src = self.parts[name].at[:, :, pl.ds((1 - at.c) * 4, 4), :, :, cols]
        dst = self.r0[name].at[:, :, :, :, :, cols]
        return remote(src, dst, self.d_send.at[n], self.d_recv.at[n, 0], at.sibling)

    def hop(self, n, h, i):
        at, name, cols = self.links, self.chunks[n][0], pl.ds(*self.chunks[n][1][h])
        two, one = at.hops(h)
        if i == 1:
            src = self.r1[name].at[1 - at.x if h == 0 else 1 - at.y, :, :, :, cols]
            dst = self.r2[name].at[:, :, :, cols]
        else:
            src = self.r0[name].at[1 - at.y, :, :, :, :, cols] if h == 0 else self.r0[name].at[:, 1 - at.x, :, :, :, cols]
            dst = self.r1[name].at[:, :, :, :, cols]
        return remote(src, dst, self.p_send.at[n, h, i], self.p_recv.at[n, h, i], two if i == 1 else one)

    def ahead(self, n, k):
        at, name, cols = self.links, self.chunks[n][0], self.links.columns(n)
        if k is None:
            src = dst = self.r3[name].at[:, :, :, cols]
        else:
            src = self.r2[name].at[lax.rem(at.z + k + 1, 4), :, :, cols]
            dst = self.r3[name].at[k, :, :, cols]
        return remote(src, dst, self.z_send.at[n], self.z_recv.at[n], at.along[k or 0])

    def add(self, into, other, cols, rows):
        (ref, lead), (source, place, start) = into, other

        def one(i, carry):
            z, row = i // rows, lax.rem(i, rows)
            ref[*lead, z, row, :, cols] = ref[*lead, z, row, :, cols] + source[*place, start + z, row, :, cols]
            return carry

        lax.fori_loop(0, 4 * rows, one, 0, unroll=4)

    def halves(self, n):
        return range(len(self.chunks[n][1]))

    def step(self, what, n):
        at, name = self.links, self.chunks[n][0]
        r0, r1, r2, r3, out = self.r0[name], self.r1[name], self.r2[name], self.r3[name], self.outs[name]
        rows = out.shape[0]
        cols = at.columns(n)
        if what == "begin":
            self.share(n).start()
        elif what == "first":
            self.share(n).wait_recv()
            for y in range(2):
                for x in range(2):
                    self.add((r0, (y, x)), (self.parts[name], (y, x), at.c * 4), cols, rows)
            for h in self.halves(n):
                self.hop(n, h, 0).start()
        elif what == "second":
            for h in self.halves(n):
                half = pl.ds(*self.chunks[n][1][h])
                self.hop(n, h, 0).wait_recv()
                for i in range(2):
                    self.add((r1, (i,)), (r0, (at.y, i) if h == 0 else (i, at.x), 0), half, rows)
                self.hop(n, h, 1).start()
        elif what == "third":
            for h in self.halves(n):
                half = pl.ds(*self.chunks[n][1][h])
                self.hop(n, h, 1).wait_recv()
                self.add((r2, ()), (r1, (at.x if h == 0 else at.y,), 0), half, rows)
            for k in range(3):
                self.ahead(n, k).start()
        elif what == "finish":
            self.ahead(n, None).wait_recv()

            def one(i, carry):
                total = r2[at.z, i, :, cols].astype(jnp.float32)
                for k in range(3):
                    total = total + r3[k, i, :, cols].astype(jnp.float32)
                out[i, :, cols] = total
                return carry

            lax.fori_loop(0, rows, one, 0)
        elif what == "close":
            self.share(n).wait_send()
            for h in self.halves(n):
                for i in range(2):
                    self.hop(n, h, i).wait_send()
            self.ahead(n, None).wait_send()


EPS = 1e-05
QB = 256
SCALE = HEAD_DIM ** (-0.5)
NT = (((1,), (1,)), ((), ()))


def dot(left, right):
    return jnp.dot(left, right, preferred_element_type=jnp.float32)


def dot_nt(left, right):
    return lax.dot_general(left, right, NT, preferred_element_type=jnp.float32)


def tiles(count, step, by=1):
    def go(i, carry):
        for k in range(by):
            step(i * by + k)
        return carry

    if by >= count:
        for k in range(count):
            step(k)
    else:
        lax.fori_loop(0, count // by, go, 0)


def at(i, size, start=0):
    if isinstance(i, int):
        return pl.ds(start + i * size, size)
    return pl.ds(pl.multiple_of(start + i * size, 128 if size % 128 == 0 else size), size)


def weight_columns(w, i, size):
    block = w[:, :, :, :, :, at(i, size)]
    return block.reshape(-1, size)


def weight_rows(w, *place):
    block = w[place] if place else w[...]
    return block.reshape(-1, block.shape[-1])


def normal(u):
    center = u - jnp.mean(u, -1, keepdims=True)
    spread = lax.rsqrt(jnp.mean(center * center, -1, keepdims=True) + EPS)
    return center * spread, spread


def norm_rows(u_ref, gain, out_ref):
    def step(i):
        hat, spread = normal(u_ref[at(i, 128)].astype(jnp.float32))
        out_ref[at(i, 128)] = (hat * gain).astype(jnp.bfloat16)

    tiles(u_ref.shape[0] // 128, step)


def gelu_both(x):
    e = jnp.exp(x * x * -0.5)
    t = 1.0 / (1.0 + jnp.abs(x) * (0.3275911 * 0.5**0.5))
    poly = 0.5 * 1.061405429
    for term in (-1.453152027, 1.421413741, -0.284496736, 0.254829592):
        poly = poly * t + 0.5 * term
    tail = poly * t * e
    cdf = jnp.where(x >= 0, 1.0 - tail, tail)
    return x * cdf, cdf + x * e * (0.5 / math.pi) ** 0.5


def both_heads(block, axis):
    half = lax.broadcasted_iota(jnp.int32, block.shape, axis) < HEAD_DIM
    zero = jnp.zeros_like(block)
    return jnp.concatenate([jnp.where(half, block, zero), jnp.where(half, zero, block)], 1 - axis)


def own_heads(wide):
    count = wide.shape[1] // 2
    return jnp.concatenate([wide[:HEAD_DIM, :count], wide[HEAD_DIM:, count:]], 0)


def right(model, n, pair):
    return at(pair, 128, n * model)


def attend(qkvs, bias_ref, p_refs, rl_ref, o_ref, ot_ref, by=6, depth=2):
    model = o_ref.shape[1]
    own = qkvs[-1]

    def score(pair, b):
        span = (b + 1) * QB
        queries = both_heads(own[b * QB : span, at(pair, 128)] * SCALE, 1)
        bias = bias_ref[:span, b * QB : span]
        bias = jnp.concatenate([bias, bias], 1)
        return [dot_nt(ref[:span, right(model, 1, pair)], queries) + bias for ref in qkvs]

    def finish(pair, b, scores):
        span = (b + 1) * QB
        lanes = at(pair, 128)
        peak = jnp.max(scores[0], 0, keepdims=True)
        for s in scores[1:]:
            peak = jnp.maximum(peak, jnp.max(s, 0, keepdims=True))
        total, out = None, None
        for n, s in enumerate(scores):
            p = jnp.exp(s - peak)
            part = jnp.sum(p, 0, keepdims=True)
            p = p.astype(jnp.bfloat16)
            p_refs[b][pair, n * span : (n + 1) * span] = p
            product = dot(qkvs[n][:span, right(model, 2, pair)].T, p)
            total = part if total is None else total + part
            out = product if out is None else out + product
        scale = 1.0 / total
        rl_ref[pair, 0:1, b * QB : span] = scale[:, :QB]
        rl_ref[pair, 1:2, b * QB : span] = scale[:, QB:]
        out = own_heads(out * scale)
        ot_ref[at(pair, 128), b * QB : span] = out
        o_ref[b * QB : span, lanes] = out.astype(jnp.bfloat16).T

    def step(i):
        items = [(i * by + k, b) for k in range(by) for b in range(own.shape[0] // QB - 1, -1, -1)]
        waiting = []
        for n, item in enumerate(items):
            if n % (own.shape[0] // QB) == 0:
                yield "a%d" % item[0]
            waiting.append((item, score(*item)))
            if len(waiting) > depth:
                item, s = waiting.pop(0)
                finish(*item, s)
        for item, s in waiting:
            finish(*item, s)

    yield from step(0)


def attend_back(qkvs, p_of, do_ref, ot_ref, dqkv_ref, dkv_ref, extra_of):
    model = do_ref.shape[0]
    own = qkvs[-1]

    def step(pair):
        lanes = at(pair, 128)
        keys = [ref[:, right(model, 1, pair)] for ref in qkvs]
        values = [ref[:, right(model, 2, pair)] for ref in qkvs]
        turned = [k.T for k in keys]
        dk, dv = [None] * len(qkvs), [None] * len(qkvs)
        for b in reversed(range(own.shape[0] // QB)):
            span = (b + 1) * QB
            block = slice(b * QB, span)
            queries = both_heads(own[block, lanes] * SCALE, 1)
            do = do_ref[lanes, block]
            do_down, do_across = both_heads(do, 0), both_heads(do.T, 1)
            product = do.astype(jnp.float32) * ot_ref[lanes, block]
            delta = jnp.concatenate([jnp.sum(product[h * HEAD_DIM : (h + 1) * HEAD_DIM], 0, keepdims=True) for h in range(2)], 1)
            dq = None
            for n in range(len(qkvs)):
                p = p_of(b, pair)[n * span : (n + 1) * span]
                ds = dot(values[n][:span], do_down) - delta
                ds = (p.astype(jnp.float32) * ds).astype(jnp.bfloat16)
                more_dv, more_dk = dot(p, do_across), dot(ds, queries)
                more_dq = dot(turned[n][:, :span], ds)
                dq = more_dq if dq is None else dq + more_dq
                if dk[n] is None:
                    dk[n], dv[n] = more_dk, more_dv
                else:
                    dk[n] = jnp.concatenate([dk[n][:span] + more_dk, dk[n][span:]], 0)
                    dv[n] = jnp.concatenate([dv[n][:span] + more_dv, dv[n][span:]], 0)
            dqkv_ref[block, lanes] = (own_heads(dq) * SCALE).astype(jnp.bfloat16).T
        if len(qkvs) > 1:
            dkv_ref[:, lanes] = dk[0]
            dkv_ref[:, right(model, 1, pair)] = dv[0]
        dk, dv = dk[-1], dv[-1]
        if extra_of is not None:
            extra = extra_of(pair)
            dk, dv = dk + extra[0], dv + extra[1]
        dqkv_ref[:, right(model, 1, pair)] = dk.astype(jnp.bfloat16)
        dqkv_ref[:, right(model, 2, pair)] = dv.astype(jnp.bfloat16)

    for pair in range(model // 128):
        yield "a%d" % pair
        step(pair)


def project(left_ref, w, add_ref, out_ref, shift, size, blocks):
    for i in blocks:
        value = dot(left_ref[...], weight_columns(w, i, size))
        if add_ref is not None:
            value = add_ref[:, at(i, size)].astype(jnp.float32) + value
        if shift is not None:
            value = value + shift[:, at(i, size)]
        out_ref[:, at(i, size)] = value.astype(out_ref.dtype)


def project_back(left_ref, w, out_ref, i):
    rows = weight_rows(w, i)
    out_ref[:, at(i, rows.shape[0])] = dot_nt(left_ref[...], rows).astype(out_ref.dtype)


def forward_pass(u_ref, qkv_before, bias_ref, gains, w, keep, out_ref, shift):
    yield "ln1"
    norm_rows(u_ref, gains[0], keep["a"])
    turn(keep["a"], keep["at"])
    for k in range(w["qkv"].shape[-1] // 768):
        yield "q%d" % k
        project(keep["a"], w["qkv"], None, keep["qkv"], None, 256, range(3 * k, 3 * k + 3))
    qkvs = [keep["qkv"]] if qkv_before is None else [qkv_before, keep["qkv"]]
    yield from attend(qkvs, bias_ref, [keep["p0"], keep["p1"]], keep["rl"], keep["o"], keep["ot"])
    yield "o"
    project(keep["o"], w["out"], u_ref, keep["m"], None, 256, range(3))
    yield "ln2"
    norm_rows(keep["m"], gains[1], keep["b"])
    turn(keep["b"], keep["bt"])
    for k in range(w["up"].shape[-1] // 768):
        yield "u%d" % k
        cols = at(k, 768)
        hidden = dot(keep["b"][...], weight_columns(w["up"], k, 768))
        active, slope = gelu_both(hidden)
        active = active.astype(jnp.bfloat16)
        keep["f"][:, cols] = active
        keep["ft"][cols] = active.T
        keep["gp"][:, cols] = slope.astype(jnp.bfloat16)
    for k in range(2):
        yield "d%d" % k
        project(keep["f"], w["down"], keep["m"], out_ref, shift, 384, (k,))
    yield "end"


def norm_back(u_ref, gain, dy_ref, add_ref, out_ref, rounded_ref, gain_grad_ref, sum_ref=None):
    def step(i, totals):
        total, whole = totals
        hat, spread = normal(u_ref[at(i, 128)].astype(jnp.float32))
        dy = dy_ref[at(i, 128)]
        total = total + jnp.sum((dy * hat).reshape(16, 8, dy.shape[1]), 0)
        dy = dy * gain
        down = dy - jnp.mean(dy, -1, keepdims=True) - hat * jnp.mean(dy * hat, -1, keepdims=True)
        value = add_ref[at(i, 128)].astype(jnp.float32) + spread * down
        out_ref[at(i, 128)] = value
        if rounded_ref is not None:
            rounded_ref[at(i, 128)] = value.astype(jnp.bfloat16)
        if sum_ref is not None:
            whole = whole + jnp.sum(value.reshape(16, 8, dy.shape[1]), 0)
        return total, whole

    zero = jnp.zeros((8, u_ref.shape[1]), jnp.float32)
    total, whole = lax.fori_loop(0, u_ref.shape[0] // 128, step, (zero, zero))
    gain_grad_ref[...] = jnp.broadcast_to(jnp.sum(total, 0, keepdims=True), gain_grad_ref.shape)
    if sum_ref is not None:
        sum_ref[...] = jnp.broadcast_to(jnp.sum(whole, 0, keepdims=True), sum_ref.shape)


def weight_grad(turned_ref, right_ref, out_ref, add, cols):
    value = dot(turned_ref[...].astype(jnp.bfloat16), right_ref[:, cols])
    value = value.reshape(*out_ref.shape[:5], value.shape[1])
    if add:
        value = value + out_ref[:, :, :, :, :, cols].astype(jnp.float32)
    out_ref[:, :, :, :, :, cols] = value.astype(out_ref.dtype)


def turn(ref, out_ref):
    def step(i):
        out_ref[at(i, 256)] = ref[:, at(i, 256)].T

    tiles(ref.shape[1] // 256, step)


def backward_pass(up_ref, u_ref, qkvs, p_of, dkv_ref, extra_of, gains, w, grads, keep, work, add, du_ref, gain_grads, sum_ref):
    yield "cast"
    dz = up_ref
    if up_ref.dtype != jnp.bfloat16:
        dz = work["dz"]

        def cast(i):
            dz[at(i, 128)] = up_ref[at(i, 128)].astype(jnp.bfloat16)

        tiles(up_ref.shape[0] // 128, cast)
    dhid = work["dhid"]

    def hidden_grads():
        for i in range(4):
            yield "b%d" % i
            value = dot_nt(dz[...], weight_rows(w["down"], i // 2, i % 2)) * keep["gp"][:, at(i, 768)].astype(jnp.float32)
            dhid[:, at(i, 768)] = value.astype(jnp.bfloat16)

    def down_grads():
        for i, block in enumerate((pl.ds(0, 256), pl.ds(256, 512))):
            yield "g%d" % i
            weight_grad(keep["ft"], dz, grads["down"], add, block)

    for part in (hidden_grads, down_grads) if grads["down"] is w["down"] else (down_grads, hidden_grads):
        yield from part()
    for i in range(2):
        yield "ub%d" % i
        project_back(dhid, w["up"], work["dm"], i)
    yield "nb"
    norm_back(keep["m"], gains[1], work["dm"], up_ref, work["dm"], work["da"], gain_grads[1])
    yield "hg"
    do = dot_nt(weight_rows(w["out"]), work["da"][...])
    for h in range(do.shape[0] // HEAD_DIM):
        rows = slice(h * HEAD_DIM, (h + 1) * HEAD_DIM)
        work["do"][rows] = (do[rows] * keep["rl"][h // 2, h % 2 : h % 2 + 1]).astype(jnp.bfloat16)
    for i in range(w["up"].shape[-1] // 768):
        yield "ug%d" % i
        weight_grad(keep["bt"], dhid, grads["up"], add, at(i, 768))
    yield "og"
    weight_grad(keep["ot"], work["da"], grads["out"], add, at(0, 768))
    yield from attend_back(qkvs, p_of, work["do"], keep["ot"], work["dqkv"], dkv_ref, extra_of)
    for i in range(2):
        yield "qb%d" % i
        project_back(work["dqkv"], w["qkv"], du_ref, i)
    yield "ni"
    norm_back(u_ref, gains[0], du_ref, work["dm"], du_ref, None, gain_grads[0], sum_ref)
    for i in range(w["qkv"].shape[-1] // 768):
        yield "qg%d" % i
        weight_grad(keep["at"], work["dqkv"], grads["qkv"], add, at(i, 768))
    yield "end"


KEPT = ("at", "qkv", "rl", "ot", "m", "bt", "ft", "gp", "p0", "p1")
LOCAL = ("a", "o", "b", "f")
NAMES_OF_WEIGHTS = tuple("w_" + n for n in NAMES)
VMEM_LIMIT = 63 << 20
VMEM = pl.BlockSpec(memory_space=pltpu.VMEM)
FAR = pl.BlockSpec(memory_space=pl.ANY)


def shapes_of(length, model, hidden, passes):
    f32, bf16 = jnp.float32, jnp.bfloat16
    shape = jax.ShapeDtypeStruct
    pairs = model // 128
    table = {
        "a": shape((length, model), bf16),
        "at": shape((model, length), bf16),
        "qkv": shape((length, 3 * model), bf16),
        "rl": shape((pairs, 2, length), f32),
        "o": shape((length, model), bf16),
        "ot": shape((model, length), f32),
        "m": shape((length, model), f32),
        "b": shape((length, model), bf16),
        "bt": shape((model, length), bf16),
        "f": shape((length, hidden), bf16),
        "ft": shape((hidden, length), bf16),
        "gp": shape((length, hidden), bf16),
        "dz": shape((length, model), bf16),
        "dm": shape((length, model), f32),
        "do": shape((model, length), bf16),
        "dqkv": shape((length, 3 * model), bf16),
        "dkv": shape((length, 2 * model), f32),
        "bias": shape((length, length), f32),
        "u": shape((length, model), f32),
        "vectors": shape((8, model), f32),
    }
    for b in range(length // QB):
        table["p%d" % b] = shape((pairs, passes * (b + 1) * QB, 2 * QB), bf16)
    return table


FIRST_ORDER = (
    "b3", "b2", "b1", "13", "b0", "b4", "12", "10", "b7", "/bias", "11", "23", "b5", "b6", "20", "22", "21", "14", "17", "30",
    "24", "33", "43", "34", "32", "40", "27", "42", "f2", "f0", "b8", "/vec", "37", "44", "15", "/ln1", "25", "f3", "f4", "16",
    "/q0", "/q1", "/q2", "/a0", "31", "/a1", "35", "47", "/a2", "41", "45", "26", "/a3", "/a4", "/a5", "36", "18", "f5", "f1",
    "46", "/o", "/ln2", "/u0", "28", "/u1", "f6", "/u2", "38", "/u3", "48", "f7", "/d0", "f8", "/d1",
)
LAST_ORDER = (
    "/cast", "/g0", "b0", "/g1", "b1", "/b0", "10", "/b1", "/b2", "/b3", "11", "/ub0", "/ub1", "20", "/nb", "/hg", "/ug0",
    "/ug1", "b2", "21", "/ug2", "30", "/ug3", "12", "b3", "/og", "b4", "/a0", "/a1", "/a2", "13", "/a3", "31", "/a4", "22",
    "/a5", "/qb0", "14", "/qb1", "/ni", "32", "23", "/qg0", "b5", "f0", "b8", "/qg1", "24", "b6", "15", "33", "16", "/qg2", "b7",
    "18", "34", "25", "17", "28", "26", "f2", "35", "27", "38", "36", "37", "f4", "f5", "f8", "f6", "f1", "f3", "f7",
)


class Room:
    def __init__(self):
        self.names, self.shapes, self.moves = [], [], []

    def scratch(self, **shapes):
        for name, s in shapes.items():
            self.names.append(name)
            self.shapes.append(pltpu.VMEM(s.shape, s.dtype))

    def bind(self, refs):
        return dict(zip(self.names, refs))


class Mover:
    def __init__(self, sems):
        self.sems, self.open, self.used = sems, {}, 0

    def start(self, src, dst, key):
        copy = pltpu.make_async_copy(src, dst, self.sems.at[self.used])
        self.used += 1
        copy.start()
        self.open[key] = copy

    def wait(self, *keys):
        for key in keys:
            if key in self.open:
                self.open.pop(key).wait()

    def close(self):
        self.wait(*list(self.open))


def make_bias(docs, bias_ref):
    length = bias_ref.shape[0]
    docs = docs[...].astype(jnp.float32)
    down = jnp.broadcast_to(docs, (128, length)).T

    def step(i):
        place_down = lax.broadcasted_iota(jnp.int32, (length, 128), 0)
        place_across = lax.broadcasted_iota(jnp.int32, (length, 128), 1) + i * 128
        seen = (down == docs[:, i * 128 : (i + 1) * 128]) & (place_down <= place_across)
        bias_ref[:, at(i, 128)] = jnp.where(seen, 0.0, -1e30)

    tiles(length // 128, step, length // 128)


def spread_vectors(small, vectors_ref, rows):
    count, model = small.size // 1024, vectors_ref.shape[1]
    lane = lax.broadcasted_iota(jnp.int32, (128, model), 1)
    place = lax.broadcasted_iota(jnp.int32, (128, model), 0)
    block = (lane * 2731) >> 16
    pick = jnp.where(lane - block * rows == place, 1.0, 0.0).astype(jnp.bfloat16)
    wide = dot(small[...].reshape(-1, 128), pick)
    row = lax.broadcasted_iota(jnp.int32, wide.shape, 0)
    owner = (lax.broadcasted_iota(jnp.int32, wide.shape, 1) * 2731) >> 16
    wide = jnp.where((row >> 3) == owner, wide, 0.0)
    vectors_ref[...] = jnp.sum(wide.reshape(count, 8, model), 0)


def gather_chunks(weights):
    chunks = [("small", ((0, 128),), False)]
    for name, parts in (("out", 1), ("qkv", 3), ("up", 2), ("down", 2)):
        chunks += [(name, halves, name == "out") for halves in pieces(weights[name].shape[-1], parts)]
    return chunks


def first_kernel(near, table, room, chunks, *refs):
    it = iter(refs)
    tokens, docs = next(it), next(it)
    shards = {n: next(it) for n in NAMES}
    if near:
        shards["small"] = next(it)
    else:
        vectors = next(it)
    far = {n: next(it) for n in ("u",) + KEPT}
    if near:
        whole = {n: next(it) for n in NAMES}
        vectors = next(it)
    refs = list(it)
    v = room.bind(refs)
    sems = refs[len(room.names) :]
    mover = Mover(sems[0])
    w = {n: v["w_" + n] for n in NAMES}
    gather = None
    before, needs = {}, {}
    if near:
        gather = Gather(chunks, shards, {**w, "small": v["small"]}, sems[1:])
        gather.links.greet()
        before = events_before(FIRST_ORDER)
    else:
        for n in NAMES:
            mover.start(shards[n], w[n], "w_" + n)
        needs = {"q0": ("w_qkv",), "o": ("w_out",), "u0": ("w_up",), "d0": ("w_down",)}

    def keep(*names):
        def go():
            for n in names:
                mover.start(v[n], far[n], "far_" + n)

        return go

    after = {
        "ln1": keep("at"),
        "q2": keep("qkv"),
        "a5": keep("p0", "p1", "rl", "ot"),
        "ln2": keep("m", "bt"),
        "u3": keep("ft", "gp"),
        "d1": keep("u"),
    }
    finished = []

    def step(what, n):
        gather.step(what, n)
        if what == "finish":
            finished.append(n)
            name = chunks[n][0]
            if name in NAMES and all(k in finished for k, chunk in enumerate(chunks) if chunk[0] == name):
                mover.start(w[name], whole[name], "whole_" + name)

    def blocks():
        yield "bias"
        make_bias(docs, v["bias"])
        yield "vec"
        if near:
            spread_vectors(v["small"], vectors, 24)
        gains = [vectors[n : n + 1] for n in (1, 2)]
        yield from forward_pass(tokens, None, v["bias"], gains, w, v, v["u"], vectors.at[0:1])

    in_turn(blocks(), before, needs, after, step, mover)
    if near:
        for n in range(len(chunks)):
            gather.step("close", n)
    mover.close()


def run_first(near, tokens, docs, small, vectors, shards):
    length, model = tokens.shape
    weights = shards
    if near:
        weights = {n: jax.ShapeDtypeStruct((2, 2, 8) + s.shape, s.dtype) for n, s in shards.items()}
    table = shapes_of(length, model, weights["up"].shape[-1], 1)
    room = Room()
    room.scratch(**{n: table[n] for n in KEPT + LOCAL + ("bias", "u")}, **{"w_" + n: weights[n] for n in NAMES})
    chunks = gather_chunks(weights) if near else []
    out_shape = [table[n] for n in ("u",) + KEPT]
    semaphores = [pltpu.SemaphoreType.DMA((24,))]
    params = dict(vmem_limit_bytes=VMEM_LIMIT)
    out_specs = [FAR] * len(out_shape)
    inputs = [tokens, docs] + [shards[n] for n in NAMES]
    if near:
        room.scratch(small=jax.ShapeDtypeStruct((2, 2, 8, 1, 8, 128), jnp.bfloat16))
        out_shape += [weights[n] for n in NAMES] + [table["vectors"]]
        out_specs += [FAR] * 4 + [VMEM]
        semaphores += link_semaphores(len(chunks))
        params.update(collective_id=0, has_side_effects=True)
        inputs, in_specs = inputs + [small], [VMEM] * 2 + [FAR] * 5
    else:
        inputs, in_specs = inputs + [vectors], [VMEM] * 2 + [FAR] * 4 + [VMEM]
    outs = pl.pallas_call(
        functools.partial(first_kernel, near, table, room, chunks),
        out_shape=out_shape,
        in_specs=in_specs,
        out_specs=out_specs,
        scratch_shapes=room.shapes + semaphores,
        name="first",
        compiler_params=pltpu.CompilerParams(**params),
    )(*inputs)
    kept = dict(zip(("u",) + KEPT, outs))
    if near:
        return kept, outs[-1], dict(zip(NAMES, outs[1 + len(KEPT) :]))
    return kept, vectors, shards


def middle_kernel(table, room, *refs):
    it = iter(refs)
    u, docs, vectors = next(it), next(it), next(it)
    cotangent, qkv_before = next(it), next(it)
    weights = {n: next(it) for n in NAMES}
    ln1, ln2, whole = next(it), next(it), next(it)
    layer_out, du, dkv = next(it), next(it), next(it)
    grads = {n: next(it) for n in NAMES}
    refs = list(it)
    v = room.bind(refs)
    mover = Mover(refs[len(room.names)])
    w = {n: v["w_" + n] for n in NAMES}
    mover.start(weights["qkv"], w["qkv"], "w_qkv")
    mover.start(qkv_before, v["before"], "before")
    for n in NAMES[1:]:
        mover.start(weights[n], w[n], "w_" + n)
    mover.start(cotangent, v["dz"], "dz")
    gains = [vectors[n : n + 1] for n in (1, 2)]
    needs = {"q0": ("w_qkv",), "a0": ("before",), "o": ("w_out",), "u0": ("w_up",), "d0": ("w_down",), "cast": ("dz",)}

    def store(src, dst):
        return lambda: mover.start(src, dst, id(dst))

    after = {
        "d1": store(v["b"], layer_out),
        "g1": store(w["down"], grads["down"]),
        "ug3": store(w["up"], grads["up"]),
        "og": store(w["out"], grads["out"]),
        "qg2": store(w["qkv"], grads["qkv"]),
        "a5": store(v["dkv"], dkv),
        "ni": store(v["m"], du),
    }
    work = dict(dz=v["dz"], da=v["a"], do=v["do"], dm=v["dm"], dhid=v["f"], dqkv=v["dqkv"])
    first = forward_pass(u, v["before"], v["bias"], gains, w, v, v["b"], None)
    make_bias(docs, v["bias"])
    in_turn(first, {}, needs, {}, None, mover)
    after["d1"]()
    p_of = lambda b, pair: v["p%d" % b].at[pair]
    second = backward_pass(
        v["dz"], u, [v["before"], v["qkv"]], p_of, v["dkv"], None, gains, w, w, v, work, False, v["m"], (ln1, ln2), whole
    )
    in_turn(second, {}, needs, after, None, mover)
    mover.close()


def run_middle(u, docs, vectors, cotangent, qkv_before, weights):
    length, model = u.shape
    table = shapes_of(length, model, weights["up"].shape[-1], 2)
    room = Room()
    room.scratch(**{n: table[n] for n in KEPT + LOCAL + ("bias", "dz", "do", "dm", "dqkv", "dkv")}, before=table["qkv"])
    room.scratch(**{"w_" + n: weights[n] for n in NAMES})
    out_shape = [table["vectors"]] * 3 + [table["b"], table["u"], table["dkv"]] + [weights[n] for n in NAMES]
    outs = pl.pallas_call(
        functools.partial(middle_kernel, table, room),
        out_shape=out_shape,
        in_specs=[VMEM] * 3 + [FAR] * 6,
        out_specs=[VMEM] * 3 + [FAR] * 7,
        scratch_shapes=room.shapes + [pltpu.SemaphoreType.DMA((16,))],
        name="middle",
        compiler_params=pltpu.CompilerParams(vmem_limit_bytes=VMEM_LIMIT),
    )(u, docs, vectors, cotangent, qkv_before, *(weights[n] for n in NAMES))
    return outs[:3], outs[3], outs[4], outs[5], dict(zip(NAMES, outs[6:]))


def reduce_chunks(weights):
    chunks = [("down", ((0, 128), (128, 128)), False), ("down", ((256, 256), (512, 256)), False)]
    for name, parts in (("up", 2), ("out", 1), ("qkv", 3)):
        chunks += [(name, halves, False) for halves in pieces(weights[name].shape[-1], parts)]
    return chunks + [("small", ((0, 128),), False)]


def fold_vectors(vector, small, rows):
    count, model = small.size // 1024, vector.shape[1]
    lane = lax.broadcasted_iota(jnp.int32, (128, model), 1)
    place = lax.broadcasted_iota(jnp.int32, (128, model), 0)
    block = (lane * 2731) >> 16
    pick = jnp.where(lane - block * rows == place, 1.0, 0.0).astype(jnp.bfloat16)
    wide = jnp.broadcast_to(vector[None], (count, 8, model)).reshape(count * 8, model)
    row = lax.broadcasted_iota(jnp.int32, wide.shape, 0)
    owner = (lax.broadcasted_iota(jnp.int32, wide.shape, 1) * 2731) >> 16
    wide = jnp.where((row >> 3) == owner, wide, 0.0).astype(jnp.bfloat16)
    small[...] = dot_nt(wide, pick).astype(jnp.bfloat16).reshape(small.shape)


def last_kernel(near, room, chunks, *refs):
    it = iter(refs)
    tokens, vectors, late1, late2, embed = next(it), next(it), next(it), next(it), next(it)
    far = {n: next(it) for n in ("upstream", "dkv") + KEPT}
    weights = {n: next(it) for n in NAMES}
    before = {n: next(it) for n in NAMES}
    du = next(it)
    outs = {n: next(it) for n in NAMES + ("small",)}
    refs = list(it)
    v = room.bind(refs)
    sems = refs[len(room.names) :]
    mover = Mover(sems[0])
    w = {n: v["w_" + n] for n in NAMES}
    grads = {**w, "down": v["g_down"]}
    model = tokens.shape[1]

    def load(*names):
        def go():
            for n in names:
                if n in NAMES_OF_WEIGHTS:
                    mover.start(weights[n[2:]], w[n[2:]], n)
                elif n[0] == "#":
                    pair = int(n[1:])
                    slot = pair % 2
                    for b in range(2):
                        mover.start(far["p%d" % b].at[pair], v["s%d" % b].at[slot], "p%d_%d" % (b, pair))
                    for k in range(2):
                        mover.start(far["dkv"].at[:, at(pair, 128, k * model)], v["dkv"].at[slot, k], "dkv%d_%d" % (k, pair))
                else:
                    mover.start(far[n], v[n], n)

        return go

    def late(name, *names):
        def go():
            mover.start(before[name], grads[name], "late_" + name)
            load(*names)()

        return go

    def load_down(i):
        def go():
            cols = at(i, 768)
            mover.start(weights["down"].at[i // 2, i % 2], w["down"].at[i // 2, i % 2], "w_down%d" % i)
            mover.start(far["gp"].at[:, cols], v["gp"].at[:, cols], "gp%d" % i)

        return go

    def both(*steps):
        def go():
            for one in steps:
                one()

        return go

    load("upstream", "ft")()
    for i, cols in enumerate((pl.ds(0, 256), pl.ds(256, 512))):
        mover.start(before["down"].at[:, :, :, :, :, cols], grads["down"].at[:, :, :, :, :, cols], "late_down%d" % i)
    load_down(0)()
    needs = {"cast": ("upstream",), "g0": ("ft", "late_down0"), "g1": ("late_down1",)}
    for i in range(4):
        needs["b%d" % i] = ("w_down%d" % i, "gp%d" % i)
    needs.update({
        "ub0": ("w_up",),
        "nb": ("m",),
        "hg": ("w_out", "rl"),
        "ug0": ("bt", "late_up"),
        "og": ("late_out", "ot"),
        "qb0": ("w_qkv",),
        "qg0": ("at", "late_qkv"),
    })
    for i in range(6):
        needs["a%d" % i] = tuple(n % i for n in ("p0_%d", "p1_%d", "dkv0_%d", "dkv1_%d")) + (("qkv",) if i == 0 else ())
    reduce = None
    events = {}
    if near:
        reduce = Reduce(
            chunks, {**grads, "small": v["small"]}, *({n: v["r%d_%s" % (k, n)] for n in NAMES + ("small",)} for k in range(4)), outs, sems[1:]
        )
        reduce.links.greet()
        events = events_before(LAST_ORDER)

    def inputs_done():
        mover.start(v["m"], du, "du")
        row = lax.broadcasted_iota(jnp.int32, embed.shape, 0)
        vector = jnp.where(row == 2, late2[...] + v["ln2"][...], 0.0)
        vector = jnp.where(row == 0, embed[...], jnp.where(row == 1, late1[...] + v["ln1"][...], vector))
        if near:
            fold_vectors(vector, v["small"], 24)
        else:
            outs["small"][...] = vector

    after = {
        "g0": load_down(1),
        "g1": both(load_down(2), load_down(3)),
        "b0": load("w_up"),
        "b2": load("m", "w_out", "rl"),
        "ub1": late("up", "bt"),
        "hg": late("out", "ot"),
        "ug1": load("qkv"),
        "ug2": load("#0"),
        "ug3": load("#1"),
        "a0": load("#2"),
        "a1": load("#3"),
        "a2": load("#4", "w_qkv"),
        "a3": load("#5"),
        "a5": load("at"),
        "qb1": late("qkv"),
        "ni": inputs_done,
    }
    if not near:
        stores = {"g1": "down", "ug3": "up", "og": "out", "qg2": "qkv"}
        for block, name in stores.items():

            def store(name=name, then=after.get(block)):
                mover.start(grads[name], outs[name], "g_" + name)
                if then:
                    then()

            after[block] = store
    work = dict(dz=v["dz"], da=v["dz"], do=v["at"], dm=v["dm"], dhid=v["gp"], dqkv=v["dqkv"])
    gains = [vectors[n : n + 1] for n in (1, 2)]
    p_of = lambda b, pair: v["s%d" % b].at[pair % 2]
    extra_of = lambda pair: (v["dkv"][pair % 2, 0], v["dkv"][pair % 2, 1])
    blocks = backward_pass(
        v["upstream"], tokens, [v["qkv"]], p_of, None, extra_of, gains, w, grads, v, work, True, v["m"], (v["ln1"], v["ln2"]), None
    )
    in_turn(blocks, events, needs, after, reduce and reduce.step, mover)
    if near:
        for n in range(len(chunks)):
            reduce.step("close", n)
    mover.close()


def run_last(near, tokens, vectors, late1, late2, embed, upstream, dkv, kept, weights, before):
    length, model = tokens.shape
    bf16 = jnp.bfloat16
    shape = jax.ShapeDtypeStruct
    table = shapes_of(length, model, weights["up"].shape[-1], 1)
    room = Room()
    room.scratch(**{n: table[n] for n in KEPT + ("dz", "dm", "dqkv") if n not in ("p0", "p1")}, upstream=table["u"])
    for b in range(2):
        room.scratch(**{"s%d" % b: shape((2,) + table["p%d" % b].shape[1:], bf16)})
    room.scratch(dkv=shape((2, 2, length, 128), jnp.float32), g_down=weights["down"])
    room.scratch(ln1=table["vectors"], ln2=table["vectors"])
    room.scratch(**{"w_" + n: weights[n] for n in NAMES})
    chunks = reduce_chunks(weights) if near else []
    semaphores = [pltpu.SemaphoreType.DMA((72,))]
    params = dict(vmem_limit_bytes=VMEM_LIMIT)
    if near:
        parts = {**weights, "small": shape((2, 2, 8, 1, 8, 128), bf16)}
        room.scratch(small=parts["small"])
        for k, blocks in enumerate(((2, 2, 4), (2, 4), (4,), (3,))):
            room.scratch(**{"r%d_%s" % (k, n): shape(blocks + p.shape[3:], bf16) for n, p in parts.items()})
        out_shape = [shape(parts[n].shape[3:], jnp.float32) for n in NAMES + ("small",)]
        out_specs = [VMEM] * 5
        semaphores += link_semaphores(len(chunks))
        params.update(collective_id=1, has_side_effects=True)
    else:
        out_shape = [weights[n] for n in NAMES] + [table["vectors"]]
        out_specs = [FAR] * 4 + [VMEM]
    outs = pl.pallas_call(
        functools.partial(last_kernel, near, room, chunks),
        out_shape=[table["u"]] + out_shape,
        in_specs=[VMEM] * 5 + [FAR] * (2 + len(KEPT) + 8),
        out_specs=[FAR] + out_specs,
        scratch_shapes=room.shapes + semaphores,
        name="last",
        compiler_params=pltpu.CompilerParams(**params),
    )(tokens, vectors, late1, late2, embed, upstream, dkv, *(kept[n] for n in KEPT), *(weights[n] for n in NAMES), *(before[n] for n in NAMES))
    return outs[0], dict(zip(NAMES, outs[1:])), outs[5]


AXES = ("dp", "fsdp")


def cut(w):
    return w.reshape(w.shape[0] // 8, 8, w.shape[1])


def join(w):
    return w.reshape(-1, w.shape[-1])


def whole(w):
    return w.reshape(2, 2, 8, w.shape[0] // 256, 8, w.shape[1])


def body(near, tokens, doc_ids, pass_embed, ln1_gain, w_qkv, w_out, ln2_gain, w_up, w_down, cotangent):
    shards = {"qkv": w_qkv, "out": w_out, "up": w_up, "down": w_down}
    docs = doc_ids.reshape(1, -1)
    rows = pass_embed.shape[0]
    small = vectors = None
    if near:
        wide = [jnp.pad(v[None], ((n, 7 - n), (0, 128 - rows))) for n, v in enumerate((pass_embed, ln1_gain, ln2_gain))]
        small = (wide[0] + wide[1] + wide[2])[None]
        shards = {n: cut(s) for n, s in shards.items()}
    else:
        vectors = jnp.stack([lax.all_gather(v, AXES, axis=0, tiled=True) for v in (pass_embed, ln1_gain, ln2_gain)])
        vectors = jnp.pad(vectors.astype(jnp.float32), ((0, 5), (0, 0)))
        shards = {n: whole(lax.all_gather(s, AXES, axis=0, tiled=True)) for n, s in shards.items()}
    kept, vectors, weights = run_first(near, tokens, docs, small, vectors, shards)
    (late1, late2, embed), layer_out, second_g, dkv, late = run_middle(kept["u"], docs, vectors, cotangent, kept["qkv"], weights)
    tokens_grad, sums, small = run_last(near, tokens, vectors, late1, late2, embed, second_g, dkv, kept, weights, late)
    if near:
        sums = {n: join(s) for n, s in sums.items()}
        small = [small[0, n, :rows] for n in range(3)]
    else:
        scatter = lambda v: lax.psum_scatter(v, AXES, scatter_dimension=0, tiled=True)
        sums = {n: scatter(join(s).astype(jnp.float32)) for n, s in sums.items()}
        small = [scatter(small[n]) for n in range(3)]
    return (layer_out, tokens_grad, small[0], small[1], sums["qkv"], sums["out"], small[2], sums["up"], sums["down"])


def solution(mesh):
    near = dict(mesh.shape) == {"dp": 8, "fsdp": 4}
    placed = (
        P(("dp", "fsdp"), None),
        P(("dp", "fsdp")),
        P(("dp", "fsdp")),
        P(("dp", "fsdp")),
        P(("dp", "fsdp"), None),
        P(("dp", "fsdp"), None),
        P(("dp", "fsdp")),
        P(("dp", "fsdp"), None),
        P(("dp", "fsdp"), None),
        P(("dp", "fsdp"), None),
    )
    return jax.shard_map(
        functools.partial(body, near),
        mesh=mesh,
        in_specs=placed,
        out_specs=(
            P(("dp", "fsdp"), None),
            P(("dp", "fsdp"), None),
            P(("dp", "fsdp")),
            P(("dp", "fsdp")),
            P(("dp", "fsdp"), None),
            P(("dp", "fsdp"), None),
            P(("dp", "fsdp")),
            P(("dp", "fsdp"), None),
            P(("dp", "fsdp"), None),
        ),
        check_vma=False,
    )
```

```python
import functools
import math

import jax
import jax.numpy as jnp
from jax import lax
from jax.experimental import pallas as pl
from jax.experimental.pallas import tpu as pltpu
from jax.sharding import PartitionSpec as P

HEAD_DIM = 64


MESH = pl.DeviceIdType.MESH
NAMES = ("qkv", "out", "up", "down")


def pieces(width, parts):
    count = width // 128 // parts
    result = []
    for n in range(parts):
        first = (count + 1 - n % 2) // 2
        start = n * count * 128
        result.append(((start, first * 128), (start + first * 128, (count - first) * 128)))
    return result


class Links:
    def __init__(self, chunks):
        d, z = lax.axis_index("dp"), lax.axis_index("fsdp")
        y, x, c = d // 4, lax.rem(d // 2, 2), lax.rem(d, 2)
        self.z, self.y, self.x, self.c = z, y, x, c
        self.sideways = (y * 4 + (1 - x) * 2 + c, z)
        self.upward = ((1 - y) * 4 + x * 2 + c, z)
        self.sibling = (y * 4 + x * 2 + 1 - c, z)
        self.along = [(d, lax.rem(z + k, 4)) for k in (1, 2, 3)]
        self.chunks = chunks

    def greet(self):
        peers = [self.sideways, self.upward, self.sibling, *self.along]
        barrier = pltpu.get_barrier_semaphore()
        for peer in peers:
            pl.semaphore_signal(barrier, inc=1, device_id=peer, device_id_type=MESH)
        pl.semaphore_wait(barrier, len(peers))

    def columns(self, n):
        halves = self.chunks[n][1]
        return pl.ds(halves[0][0], sum(size for _, size in halves))

    def hops(self, h):
        return (self.sideways, self.upward) if h == 0 else (self.upward, self.sideways)


def remote(src, dst, send, recv, peer):
    return pltpu.make_async_remote_copy(
        src_ref=src, dst_ref=dst, send_sem=send, recv_sem=recv, device_id=peer, device_id_type=MESH
    )


def link_semaphores(count):
    dma = pltpu.SemaphoreType.DMA
    return [dma((count,)), dma((count,)), dma((count, 2, 2)), dma((count, 2, 3)), dma((count,)), dma((count, 2)), dma((count,))]


class Gather:
    def __init__(self, chunks, shards, wholes, sems):
        self.links = Links(chunks)
        self.chunks, self.shards, self.wholes = chunks, shards, wholes
        self.z_send, self.z_recv, self.p_send, self.p_recv, self.d_send, self.d_recv, self.own_sem = sems

    def near(self, n, cols):
        name, at = self.chunks[n][0], self.links
        return self.shards[name].at[:, :, cols], self.wholes[name].at[at.y, at.x, at.c * 4 + at.z, :, :, cols]

    def line(self, n, y, x, cols):
        return self.wholes[self.chunks[n][0]].at[y, x, pl.ds(self.links.c * 4, 4), :, :, cols]

    def plane(self, n, z, cols):
        return self.wholes[self.chunks[n][0]].at[:, :, self.links.c * 4 + z, :, :, cols]

    def own(self, n):
        return pltpu.make_async_copy(*self.near(n, self.links.columns(n)), self.own_sem.at[n])

    def ahead(self, n, k):
        at, cols = self.links, self.links.columns(n)
        src, dst = self.near(n, cols)
        if self.chunks[n][2]:
            src = dst = self.plane(n, at.z, cols)
        if k is None:
            whole = self.wholes[self.chunks[n][0]]
            src = dst = whole.at[:, :, pl.ds(0, 3), :, :, cols] if self.chunks[n][2] else whole.at[0, 0, pl.ds(0, 3), :, :, cols]
        return remote(src, dst, self.z_send.at[n], self.z_recv.at[n], at.along[k or 0])

    def hop(self, n, h, i):
        at, cols = self.links, pl.ds(*self.chunks[n][1][h])
        one, two = at.hops(h)
        other = (at.y, 1 - at.x) if h == 0 else (1 - at.y, at.x)
        if self.chunks[n][2]:
            src, dst = self.near(n, cols)
            if i == 2:
                src = dst = self.wholes[self.chunks[n][0]].at[*other, at.c * 4 + at.z, :, :, cols]
        else:
            src = dst = self.line(n, *(other if i == 2 else (at.y, at.x)), cols)
        return remote(src, dst, self.p_send.at[n, h, int(i == 2)], self.p_recv.at[n, h, i], one if i == 0 else two)

    def both_hops(self, n, h):
        cols, whole = pl.ds(*self.chunks[n][1][h]), self.wholes[self.chunks[n][0]]
        block = whole.at[0, :, 0, :, :, cols] if self.chunks[n][2] else whole.at[0, :, pl.ds(0, 4), :, :, cols]
        return remote(block, block, self.p_send.at[n, h, 0], self.p_recv.at[n, h, 0], self.links.sideways)

    def share(self, n, g):
        at, cols = self.links, self.links.columns(n)
        whole, lines = self.wholes[self.chunks[n][0]], pl.ds(at.c * 4, 4)
        if self.chunks[n][2] or g is None:
            block = whole.at[:, :, lines, :, :, cols]
        else:
            block = whole.at[1 - at.y if g else at.y, :, lines, :, :, cols]
        return remote(block, block, self.d_send.at[n], self.d_recv.at[n, g or 0], at.sibling)

    def halves(self, n):
        return range(len(self.chunks[n][1]))

    def step(self, what, n):
        if self.chunks[n][2]:
            self.plane_step(what, n)
        elif what == "begin":
            self.own(n).start()
            for k in range(3):
                self.ahead(n, k).start()
        elif what == "first":
            self.own(n).wait()
            self.ahead(n, None).wait_recv()
            for h in self.halves(n):
                self.hop(n, h, 0).start()
                self.hop(n, h, 1).start()
        elif what == "second":
            for h in self.halves(n):
                self.hop(n, h, 0).wait_recv()
                self.hop(n, h, 2).start()
        elif what == "third":
            for h in self.halves(n):
                self.hop(n, h, 1).wait_recv()
            self.share(n, 0).start()
        elif what == "fourth":
            for h in self.halves(n):
                self.hop(n, h, 2).wait_recv()
            self.share(n, 1).start()
        elif what == "finish":
            for g in range(2):
                self.share(n, g).wait_recv()
        if what == "close":
            self.ahead(n, None).wait_send()
            for h in self.halves(n):
                self.both_hops(n, h).wait_send()
                self.hop(n, h, 2).wait_send()
            self.share(n, None).wait_send()

    def plane_step(self, what, n):
        if what == "begin":
            self.own(n).start()
            for h in self.halves(n):
                self.hop(n, h, 0).start()
                self.hop(n, h, 1).start()
        elif what == "first":
            for h in self.halves(n):
                self.hop(n, h, 0).wait_recv()
                self.hop(n, h, 2).start()
        elif what == "second":
            self.own(n).wait()
            for h in self.halves(n):
                self.hop(n, h, 1).wait_recv()
                self.hop(n, h, 2).wait_recv()
            for k in range(3):
                self.ahead(n, k).start()
        elif what == "third":
            self.ahead(n, None).wait_recv()
            self.share(n, 0).start()
        elif what == "finish":
            self.share(n, 0).wait_recv()


def in_turn(blocks, before, needs, after, step, mover):
    last = None
    for name in blocks:
        if last in after:
            after[last]()
        for event in before.get(name, ()):
            step(*event)
        mover.wait(*needs.get(name, ()))
        last = name


def events_before(order):
    stages = {"b": "begin", "1": "first", "2": "second", "3": "third", "4": "fourth", "f": "finish"}
    table, waiting = {}, []
    for word in order:
        if word[0] == "/":
            table[word[1:]], waiting = waiting, []
        else:
            waiting.append((stages[word[0]], int(word[1:])))
    table["end"] = table.get("end", []) + waiting
    return table


class Reduce:
    def __init__(self, chunks, parts, r0, r1, r2, r3, outs, sems):
        self.links = Links(chunks)
        self.chunks, self.parts, self.outs = chunks, parts, outs
        self.r0, self.r1, self.r2, self.r3 = r0, r1, r2, r3
        self.z_send, self.z_recv, self.p_send, self.p_recv, self.d_send, self.d_recv, _ = sems

    def share(self, n):
        at, name, cols = self.links, self.chunks[n][0], self.links.columns(n)
        src = self.parts[name].at[:, :, pl.ds((1 - at.c) * 4, 4), :, :, cols]
        dst = self.r0[name].at[:, :, :, :, :, cols]
        return remote(src, dst, self.d_send.at[n], self.d_recv.at[n, 0], at.sibling)

    def hop(self, n, h, i):
        at, name, cols = self.links, self.chunks[n][0], pl.ds(*self.chunks[n][1][h])
        two, one = at.hops(h)
        if i == 1:
            src = self.r1[name].at[1 - at.x if h == 0 else 1 - at.y, :, :, :, cols]
            dst = self.r2[name].at[:, :, :, cols]
        else:
            src = self.r0[name].at[1 - at.y, :, :, :, :, cols] if h == 0 else self.r0[name].at[:, 1 - at.x, :, :, :, cols]
            dst = self.r1[name].at[:, :, :, :, cols]
        return remote(src, dst, self.p_send.at[n, h, i], self.p_recv.at[n, h, i], two if i == 1 else one)

    def ahead(self, n, k):
        at, name, cols = self.links, self.chunks[n][0], self.links.columns(n)
        if k is None:
            src = dst = self.r3[name].at[:, :, :, cols]
        else:
            src = self.r2[name].at[lax.rem(at.z + k + 1, 4), :, :, cols]
            dst = self.r3[name].at[k, :, :, cols]
        return remote(src, dst, self.z_send.at[n], self.z_recv.at[n], at.along[k or 0])

    def add(self, into, other, cols):
        (ref, lead), (source, place, start) = into, other
        for z in range(4):
            ref[*lead, z, :, :, cols] = ref[*lead, z, :, :, cols] + source[*place, start + z, :, :, cols]

    def halves(self, n):
        return range(len(self.chunks[n][1]))

    def step(self, what, n):
        at, name = self.links, self.chunks[n][0]
        r0, r1, r2, r3, out = self.r0[name], self.r1[name], self.r2[name], self.r3[name], self.outs[name]
        cols = at.columns(n)
        if what == "begin":
            self.share(n).start()
        elif what == "first":
            self.share(n).wait_recv()
            for y in range(2):
                for x in range(2):
                    self.add((r0, (y, x)), (self.parts[name], (y, x), at.c * 4), cols)
            for h in self.halves(n):
                self.hop(n, h, 0).start()
        elif what == "second":
            for h in self.halves(n):
                half = pl.ds(*self.chunks[n][1][h])
                self.hop(n, h, 0).wait_recv()
                for i in range(2):
                    self.add((r1, (i,)), (r0, (at.y, i) if h == 0 else (i, at.x), 0), half)
                self.hop(n, h, 1).start()
        elif what == "third":
            for h in self.halves(n):
                half = pl.ds(*self.chunks[n][1][h])
                self.hop(n, h, 1).wait_recv()
                self.add((r2, ()), (r1, (at.x if h == 0 else at.y,), 0), half)
            for k in range(3):
                self.ahead(n, k).start()
        elif what == "finish":
            self.ahead(n, None).wait_recv()

            total = r2[at.z, :, :, cols].astype(jnp.float32)
            for k in range(3):
                total = total + r3[k, :, :, cols].astype(jnp.float32)
            out[:, :, cols] = total
        elif what == "close":
            self.share(n).wait_send()
            for h in self.halves(n):
                for i in range(2):
                    self.hop(n, h, i).wait_send()
            self.ahead(n, None).wait_send()


EPS = 1e-05
QB = 256
SCALE = HEAD_DIM ** (-0.5)
NT = (((1,), (1,)), ((), ()))


def dot(left, right):
    return jnp.dot(left, right, preferred_element_type=jnp.float32)


def dot_nt(left, right):
    return lax.dot_general(left, right, NT, preferred_element_type=jnp.float32)


def tiles(count, step, by=1):
    def go(i, carry):
        for k in range(by):
            step(i * by + k)
        return carry

    if by >= count:
        for k in range(count):
            step(k)
    else:
        lax.fori_loop(0, count // by, go, 0)


def at(i, size, start=0):
    if isinstance(i, int):
        return pl.ds(start + i * size, size)
    return pl.ds(pl.multiple_of(start + i * size, 128 if size % 128 == 0 else size), size)


def weight_columns(w, i, size):
    block = w[:, :, :, :, :, at(i, size)]
    return block.reshape(-1, size)


def weight_rows(w, *place):
    block = w[place] if place else w[...]
    return block.reshape(-1, block.shape[-1])


def normal(u):
    center = u - jnp.mean(u, -1, keepdims=True)
    spread = lax.rsqrt(jnp.mean(center * center, -1, keepdims=True) + EPS)
    return center * spread, spread


def norm_rows(u_ref, gain, out_ref):
    def step(i):
        hat, spread = normal(u_ref[at(i, 128)].astype(jnp.float32))
        out_ref[at(i, 128)] = (hat * gain).astype(jnp.bfloat16)

    tiles(u_ref.shape[0] // 128, step)


def gelu_both(x):
    e = jnp.exp(x * x * -0.5)
    t = 1.0 / (1.0 + jnp.abs(x) * (0.3275911 * 0.5**0.5))
    poly = 0.5 * 1.061405429
    for term in (-1.453152027, 1.421413741, -0.284496736, 0.254829592):
        poly = poly * t + 0.5 * term
    tail = poly * t * e
    cdf = jnp.where(x >= 0, 1.0 - tail, tail)
    return x * cdf, cdf + x * e * (0.5 / math.pi) ** 0.5


def both_heads(block, axis):
    half = lax.broadcasted_iota(jnp.int32, block.shape, axis) < HEAD_DIM
    zero = jnp.zeros_like(block)
    return jnp.concatenate([jnp.where(half, block, zero), jnp.where(half, zero, block)], 1 - axis)


def own_heads(wide):
    count = wide.shape[1] // 2
    return jnp.concatenate([wide[:HEAD_DIM, :count], wide[HEAD_DIM:, count:]], 0)


def right(model, n, pair):
    return at(pair, 128, n * model)


def attend(qkvs, bias_ref, p_refs, rl_ref, o_ref, ot_ref, by=6, depth=2):
    model = o_ref.shape[1]
    own = qkvs[-1]

    def score(pair, b):
        span = (b + 1) * QB
        queries = both_heads(own[b * QB : span, at(pair, 128)] * SCALE, 1)
        bias = bias_ref[:span, b * QB : span]
        bias = jnp.concatenate([bias, bias], 1)
        return [dot_nt(ref[:span, right(model, 1, pair)], queries) + bias for ref in qkvs]

    def finish(pair, b, scores):
        span = (b + 1) * QB
        lanes = at(pair, 128)
        peak = jnp.max(scores[0], 0, keepdims=True)
        for s in scores[1:]:
            peak = jnp.maximum(peak, jnp.max(s, 0, keepdims=True))
        total, out = None, None
        for n, s in enumerate(scores):
            p = jnp.exp(s - peak)
            part = jnp.sum(p, 0, keepdims=True)
            p = p.astype(jnp.bfloat16)
            p_refs[b][pair, n * span : (n + 1) * span] = p
            product = dot(qkvs[n][:span, right(model, 2, pair)].T, p)
            total = part if total is None else total + part
            out = product if out is None else out + product
        scale = 1.0 / total
        rl_ref[pair, 0:1, b * QB : span] = scale[:, :QB]
        rl_ref[pair, 1:2, b * QB : span] = scale[:, QB:]
        out = own_heads(out * scale)
        ot_ref[at(pair, 128), b * QB : span] = out
        o_ref[b * QB : span, lanes] = out.astype(jnp.bfloat16).T

    def step(i):
        items = [(i * by + k, b) for k in range(by) for b in range(own.shape[0] // QB - 1, -1, -1)]
        waiting = []
        for n, item in enumerate(items):
            if n % (own.shape[0] // QB) == 0:
                yield "a%d" % item[0]
            waiting.append((item, score(*item)))
            if len(waiting) > depth:
                item, s = waiting.pop(0)
                finish(*item, s)
        for item, s in waiting:
            finish(*item, s)

    yield from step(0)


def attend_back(qkvs, p_of, do_ref, ot_ref, dqkv_ref, dkv_ref, extra_of):
    model = do_ref.shape[0]
    own = qkvs[-1]

    def step(pair):
        lanes = at(pair, 128)
        keys = [ref[:, right(model, 1, pair)] for ref in qkvs]
        values = [ref[:, right(model, 2, pair)] for ref in qkvs]
        turned = [k.T for k in keys]
        dk, dv = [None] * len(qkvs), [None] * len(qkvs)
        for b in reversed(range(own.shape[0] // QB)):
            span = (b + 1) * QB
            block = slice(b * QB, span)
            queries = both_heads(own[block, lanes] * SCALE, 1)
            do = do_ref[lanes, block]
            do_down, do_across = both_heads(do, 0), both_heads(do.T, 1)
            product = do.astype(jnp.float32) * ot_ref[lanes, block]
            delta = jnp.concatenate([jnp.sum(product[h * HEAD_DIM : (h + 1) * HEAD_DIM], 0, keepdims=True) for h in range(2)], 1)
            dq = None
            for n in range(len(qkvs)):
                p = p_of(b, pair)[n * span : (n + 1) * span]
                ds = dot(values[n][:span], do_down) - delta
                ds = (p.astype(jnp.float32) * ds).astype(jnp.bfloat16)
                more_dv, more_dk = dot(p, do_across), dot(ds, queries)
                more_dq = dot(turned[n][:, :span], ds)
                dq = more_dq if dq is None else dq + more_dq
                if dk[n] is None:
                    dk[n], dv[n] = more_dk, more_dv
                else:
                    dk[n] = jnp.concatenate([dk[n][:span] + more_dk, dk[n][span:]], 0)
                    dv[n] = jnp.concatenate([dv[n][:span] + more_dv, dv[n][span:]], 0)
            dqkv_ref[block, lanes] = (own_heads(dq) * SCALE).astype(jnp.bfloat16).T
        if len(qkvs) > 1:
            dkv_ref[:, lanes] = dk[0]
            dkv_ref[:, right(model, 1, pair)] = dv[0]
        dk, dv = dk[-1], dv[-1]
        if extra_of is not None:
            extra = extra_of(pair)
            dk, dv = dk + extra[0], dv + extra[1]
        dqkv_ref[:, right(model, 1, pair)] = dk.astype(jnp.bfloat16)
        dqkv_ref[:, right(model, 2, pair)] = dv.astype(jnp.bfloat16)

    for pair in range(model // 128):
        yield "a%d" % pair
        step(pair)


def project(left_ref, w, add_ref, out_ref, shift, size, blocks):
    for i in blocks:
        value = dot(left_ref[...], weight_columns(w, i, size))
        if add_ref is not None:
            value = add_ref[:, at(i, size)].astype(jnp.float32) + value
        if shift is not None:
            value = value + shift[:, at(i, size)]
        out_ref[:, at(i, size)] = value.astype(out_ref.dtype)


def project_back(left_ref, w, out_ref, i):
    rows = weight_rows(w, i)
    out_ref[:, at(i, rows.shape[0])] = dot_nt(left_ref[...], rows).astype(out_ref.dtype)


def forward_pass(u_ref, qkv_before, bias_ref, gains, w, keep, out_ref, shift):
    yield "ln1"
    norm_rows(u_ref, gains[0], keep["a"])
    turn(keep["a"], keep["at"])
    for k in range(w["qkv"].shape[-1] // 768):
        yield "q%d" % k
        project(keep["a"], w["qkv"], None, keep["qkv"], None, 256, range(3 * k, 3 * k + 3))
    qkvs = [keep["qkv"]] if qkv_before is None else [qkv_before, keep["qkv"]]
    yield from attend(qkvs, bias_ref, [keep["p0"], keep["p1"]], keep["rl"], keep["o"], keep["ot"])
    yield "o"
    project(keep["o"], w["out"], u_ref, keep["m"], None, 256, range(3))
    yield "ln2"
    norm_rows(keep["m"], gains[1], keep["b"])
    turn(keep["b"], keep["bt"])
    for k in range(w["up"].shape[-1] // 768):
        yield "u%d" % k
        cols = at(k, 768)
        hidden = dot(keep["b"][...], weight_columns(w["up"], k, 768))
        active, slope = gelu_both(hidden)
        active = active.astype(jnp.bfloat16)
        keep["f"][:, cols] = active
        keep["ft"][cols] = active.T
        keep["gp"][:, cols] = slope.astype(jnp.bfloat16)
    for k in range(2):
        yield "d%d" % k
        project(keep["f"], w["down"], keep["m"], out_ref, shift, 384, (k,))
    yield "end"


def norm_back(u_ref, gain, dy_ref, add_ref, out_ref, rounded_ref, gain_grad_ref, sum_ref=None):
    def step(i, totals):
        total, whole = totals
        hat, spread = normal(u_ref[at(i, 128)].astype(jnp.float32))
        dy = dy_ref[at(i, 128)]
        total = total + jnp.sum((dy * hat).reshape(16, 8, dy.shape[1]), 0)
        dy = dy * gain
        down = dy - jnp.mean(dy, -1, keepdims=True) - hat * jnp.mean(dy * hat, -1, keepdims=True)
        value = add_ref[at(i, 128)].astype(jnp.float32) + spread * down
        out_ref[at(i, 128)] = value
        if rounded_ref is not None:
            rounded_ref[at(i, 128)] = value.astype(jnp.bfloat16)
        if sum_ref is not None:
            whole = whole + jnp.sum(value.reshape(16, 8, dy.shape[1]), 0)
        return total, whole

    zero = jnp.zeros((8, u_ref.shape[1]), jnp.float32)
    total, whole = lax.fori_loop(0, u_ref.shape[0] // 128, step, (zero, zero))
    gain_grad_ref[...] = jnp.broadcast_to(jnp.sum(total, 0, keepdims=True), gain_grad_ref.shape)
    if sum_ref is not None:
        sum_ref[...] = jnp.broadcast_to(jnp.sum(whole, 0, keepdims=True), sum_ref.shape)


def weight_grad(turned_ref, right_ref, out_ref, add, cols):
    value = dot(turned_ref[...].astype(jnp.bfloat16), right_ref[:, cols])
    value = value.reshape(*out_ref.shape[:5], value.shape[1])
    if add:
        value = value + out_ref[:, :, :, :, :, cols].astype(jnp.float32)
    out_ref[:, :, :, :, :, cols] = value.astype(out_ref.dtype)


def turn(ref, out_ref):
    def step(i):
        out_ref[at(i, 256)] = ref[:, at(i, 256)].T

    tiles(ref.shape[1] // 256, step)


def backward_pass(up_ref, u_ref, qkvs, p_of, dkv_ref, extra_of, gains, w, grads, keep, work, add, du_ref, gain_grads, sum_ref):
    yield "cast"
    dz = up_ref
    if up_ref.dtype != jnp.bfloat16:
        dz = work["dz"]

        def cast(i):
            dz[at(i, 128)] = up_ref[at(i, 128)].astype(jnp.bfloat16)

        tiles(up_ref.shape[0] // 128, cast)
    dhid = work["dhid"]

    def hidden_grads():
        for i in range(4):
            yield "b%d" % i
            value = dot_nt(dz[...], weight_rows(w["down"], i // 2, i % 2)) * keep["gp"][:, at(i, 768)].astype(jnp.float32)
            dhid[:, at(i, 768)] = value.astype(jnp.bfloat16)

    def down_grads():
        for i, block in enumerate((pl.ds(0, 256), pl.ds(256, 512))):
            yield "g%d" % i
            weight_grad(keep["ft"], dz, grads["down"], add, block)

    for part in (hidden_grads, down_grads) if grads["down"] is w["down"] else (down_grads, hidden_grads):
        yield from part()
    for i in range(2):
        yield "ub%d" % i
        project_back(dhid, w["up"], work["dm"], i)
    yield "nb"
    norm_back(keep["m"], gains[1], work["dm"], up_ref, work["dm"], work["da"], gain_grads[1])
    yield "hg"
    do = dot_nt(weight_rows(w["out"]), work["da"][...])
    for h in range(do.shape[0] // HEAD_DIM):
        rows = slice(h * HEAD_DIM, (h + 1) * HEAD_DIM)
        work["do"][rows] = (do[rows] * keep["rl"][h // 2, h % 2 : h % 2 + 1]).astype(jnp.bfloat16)
    for i in range(w["up"].shape[-1] // 768):
        yield "ug%d" % i
        weight_grad(keep["bt"], dhid, grads["up"], add, at(i, 768))
    yield "og"
    weight_grad(keep["ot"], work["da"], grads["out"], add, at(0, 768))
    yield from attend_back(qkvs, p_of, work["do"], keep["ot"], work["dqkv"], dkv_ref, extra_of)
    for i in range(2):
        yield "qb%d" % i
        project_back(work["dqkv"], w["qkv"], du_ref, i)
    yield "ni"
    norm_back(u_ref, gains[0], du_ref, work["dm"], du_ref, None, gain_grads[0], sum_ref)
    for i in range(w["qkv"].shape[-1] // 768):
        yield "qg%d" % i
        weight_grad(keep["at"], work["dqkv"], grads["qkv"], add, at(i, 768))
    yield "end"


KEPT = ("at", "qkv", "rl", "ot", "m", "bt", "ft", "gp", "p0", "p1")
LOCAL = ("a", "o", "b", "f")
NAMES_OF_WEIGHTS = tuple("w_" + n for n in NAMES)
VMEM_LIMIT = 63 << 20
VMEM = pl.BlockSpec(memory_space=pltpu.VMEM)
FAR = pl.BlockSpec(memory_space=pl.ANY)


def shapes_of(length, model, hidden, passes):
    f32, bf16 = jnp.float32, jnp.bfloat16
    shape = jax.ShapeDtypeStruct
    pairs = model // 128
    table = {
        "a": shape((length, model), bf16),
        "at": shape((model, length), bf16),
        "qkv": shape((length, 3 * model), bf16),
        "rl": shape((pairs, 2, length), f32),
        "o": shape((length, model), bf16),
        "ot": shape((model, length), f32),
        "m": shape((length, model), f32),
        "b": shape((length, model), bf16),
        "bt": shape((model, length), bf16),
        "f": shape((length, hidden), bf16),
        "ft": shape((hidden, length), bf16),
        "gp": shape((length, hidden), bf16),
        "dz": shape((length, model), bf16),
        "dm": shape((length, model), f32),
        "do": shape((model, length), bf16),
        "dqkv": shape((length, 3 * model), bf16),
        "dkv": shape((length, 2 * model), f32),
        "bias": shape((length, length), f32),
        "u": shape((length, model), f32),
        "vectors": shape((8, model), f32),
    }
    for b in range(length // QB):
        table["p%d" % b] = shape((pairs, passes * (b + 1) * QB, 2 * QB), bf16)
    return table


FIRST_ORDER = (
    "b2", "b1", "b0", "b4", "b3", "12", "11", "14", "10", "b6", "b5", "/bias", "13", "23", "24", "20", "16", "34", "b7", "22",
    "30", "26", "21", "15", "32", "40", "42", "33", "f0", "/vec", "43", "36", "/ln1", "f3", "17", "f2", "25", "/q0", "b8", "44",
    "f4", "35", "/q1", "/q2", "/a0", "/a1", "/a2", "27", "/a3", "31", "/a4", "46", "/a5", "41", "37", "f1", "45", "/o", "/ln2",
    "18", "f5", "f6", "47", "/u0", "/u1", "f7", "28", "/u2", "38", "/u3", "48", "/d0", "f8", "/d1",
)
LAST_ORDER = (
    "/cast", "/g0", "b0", "/g1", "b1", "/b0", "10", "/b1", "/b2", "/b3", "11", "/ub0", "/ub1", "20", "/nb", "/hg", "/ug0",
    "/ug1", "b2", "21", "/ug2", "30", "/ug3", "12", "b3", "/og", "b4", "/a0", "/a1", "/a2", "13", "/a3", "31", "/a4", "22",
    "/a5", "/qb0", "14", "/qb1", "/ni", "32", "23", "/qg0", "b5", "f0", "b8", "/qg1", "24", "b6", "15", "33", "16", "/qg2", "b7",
    "18", "34", "25", "17", "28", "26", "f2", "35", "27", "38", "36", "37", "f4", "f5", "f8", "f6", "f1", "f3", "f7",
)


class Room:
    def __init__(self):
        self.names, self.shapes, self.moves = [], [], []

    def scratch(self, **shapes):
        for name, s in shapes.items():
            self.names.append(name)
            self.shapes.append(pltpu.VMEM(s.shape, s.dtype))

    def bind(self, refs):
        return dict(zip(self.names, refs))


class Mover:
    def __init__(self, sems):
        self.sems, self.open, self.used = sems, {}, 0

    def start(self, src, dst, key):
        copy = pltpu.make_async_copy(src, dst, self.sems.at[self.used])
        self.used += 1
        copy.start()
        self.open[key] = copy

    def wait(self, *keys):
        for key in keys:
            if key in self.open:
                self.open.pop(key).wait()

    def close(self):
        self.wait(*list(self.open))


def make_bias(docs, bias_ref):
    length = bias_ref.shape[0]
    docs = docs[...].astype(jnp.float32)
    down = jnp.broadcast_to(docs, (128, length)).T

    def step(i):
        place_down = lax.broadcasted_iota(jnp.int32, (length, 128), 0)
        place_across = lax.broadcasted_iota(jnp.int32, (length, 128), 1) + i * 128
        seen = (down == docs[:, i * 128 : (i + 1) * 128]) & (place_down <= place_across)
        bias_ref[:, at(i, 128)] = jnp.where(seen, 0.0, -1e30)

    tiles(length // 128, step, length // 128)


def spread_vectors(small, vectors_ref, rows):
    count, model = small.size // 1024, vectors_ref.shape[1]
    lane = lax.broadcasted_iota(jnp.int32, (128, model), 1)
    place = lax.broadcasted_iota(jnp.int32, (128, model), 0)
    block = (lane * 2731) >> 16
    pick = jnp.where(lane - block * rows == place, 1.0, 0.0).astype(jnp.bfloat16)
    wide = dot(small[...].reshape(-1, 128), pick)
    row = lax.broadcasted_iota(jnp.int32, wide.shape, 0)
    owner = (lax.broadcasted_iota(jnp.int32, wide.shape, 1) * 2731) >> 16
    wide = jnp.where((row >> 3) == owner, wide, 0.0)
    vectors_ref[...] = jnp.sum(wide.reshape(count, 8, model), 0)


def gather_chunks(weights):
    chunks = [("small", ((0, 128),), False)]
    for name, parts in (("out", 1), ("qkv", 3), ("up", 2), ("down", 2)):
        chunks += [(name, halves, name == "out") for halves in pieces(weights[name].shape[-1], parts)]
    return chunks


def first_kernel(near, table, room, chunks, *refs):
    it = iter(refs)
    tokens, docs = next(it), next(it)
    shards = {n: next(it) for n in NAMES}
    if near:
        shards["small"] = next(it)
    else:
        vectors = next(it)
    far = {n: next(it) for n in ("u",) + KEPT}
    if near:
        whole = {n: next(it) for n in NAMES}
        vectors = next(it)
    refs = list(it)
    v = room.bind(refs)
    sems = refs[len(room.names) :]
    mover = Mover(sems[0])
    w = {n: v["w_" + n] for n in NAMES}
    gather = None
    before, needs = {}, {}
    if near:
        gather = Gather(chunks, shards, {**w, "small": v["small"]}, sems[1:])
        gather.links.greet()
        before = events_before(FIRST_ORDER)
    else:
        for n in NAMES:
            mover.start(shards[n], w[n], "w_" + n)
        needs = {"q0": ("w_qkv",), "o": ("w_out",), "u0": ("w_up",), "d0": ("w_down",)}

    def keep(*names):
        def go():
            for n in names:
                mover.start(v[n], far[n], "far_" + n)

        return go

    after = {
        "ln1": keep("at"),
        "q2": keep("qkv"),
        "a5": keep("p0", "p1", "rl", "ot"),
        "ln2": keep("m", "bt"),
        "u3": keep("ft", "gp"),
        "d1": keep("u"),
    }
    finished = []

    def step(what, n):
        gather.step(what, n)
        if what == "finish":
            finished.append(n)
            name = chunks[n][0]
            if name in NAMES and all(k in finished for k, chunk in enumerate(chunks) if chunk[0] == name):
                mover.start(w[name], whole[name], "whole_" + name)

    def blocks():
        yield "bias"
        make_bias(docs, v["bias"])
        yield "vec"
        if near:
            spread_vectors(v["small"], vectors, 24)
        gains = [vectors[n : n + 1] for n in (1, 2)]
        yield from forward_pass(tokens, None, v["bias"], gains, w, v, v["u"], vectors.at[0:1])

    in_turn(blocks(), before, needs, after, step, mover)
    if near:
        for n in range(len(chunks)):
            gather.step("close", n)
    mover.close()


def run_first(near, tokens, docs, small, vectors, shards):
    length, model = tokens.shape
    weights = shards
    if near:
        weights = {n: jax.ShapeDtypeStruct((2, 2, 8) + s.shape, s.dtype) for n, s in shards.items()}
    table = shapes_of(length, model, weights["up"].shape[-1], 1)
    room = Room()
    room.scratch(**{n: table[n] for n in KEPT + LOCAL + ("bias", "u")}, **{"w_" + n: weights[n] for n in NAMES})
    chunks = gather_chunks(weights) if near else []
    out_shape = [table[n] for n in ("u",) + KEPT]
    semaphores = [pltpu.SemaphoreType.DMA((24,))]
    params = dict(vmem_limit_bytes=VMEM_LIMIT)
    out_specs = [FAR] * len(out_shape)
    inputs = [tokens, docs] + [shards[n] for n in NAMES]
    if near:
        room.scratch(small=jax.ShapeDtypeStruct((2, 2, 8, 1, 8, 128), jnp.bfloat16))
        out_shape += [weights[n] for n in NAMES] + [table["vectors"]]
        out_specs += [FAR] * 4 + [VMEM]
        semaphores += link_semaphores(len(chunks))
        params.update(collective_id=0, has_side_effects=True)
        inputs, in_specs = inputs + [small], [VMEM] * 2 + [FAR] * 5
    else:
        inputs, in_specs = inputs + [vectors], [VMEM] * 2 + [FAR] * 4 + [VMEM]
    outs = pl.pallas_call(
        functools.partial(first_kernel, near, table, room, chunks),
        out_shape=out_shape,
        in_specs=in_specs,
        out_specs=out_specs,
        scratch_shapes=room.shapes + semaphores,
        name="first",
        compiler_params=pltpu.CompilerParams(**params),
    )(*inputs)
    kept = dict(zip(("u",) + KEPT, outs))
    if near:
        return kept, outs[-1], dict(zip(NAMES, outs[1 + len(KEPT) :]))
    return kept, vectors, shards


def middle_kernel(table, room, *refs):
    it = iter(refs)
    u, docs, vectors = next(it), next(it), next(it)
    cotangent, qkv_before = next(it), next(it)
    weights = {n: next(it) for n in NAMES}
    ln1, ln2, whole = next(it), next(it), next(it)
    layer_out, du, dkv = next(it), next(it), next(it)
    grads = {n: next(it) for n in NAMES}
    refs = list(it)
    v = room.bind(refs)
    mover = Mover(refs[len(room.names)])
    w = {n: v["w_" + n] for n in NAMES}
    mover.start(weights["qkv"], w["qkv"], "w_qkv")
    mover.start(qkv_before, v["before"], "before")
    for n in NAMES[1:]:
        mover.start(weights[n], w[n], "w_" + n)
    mover.start(cotangent, v["dz"], "dz")
    gains = [vectors[n : n + 1] for n in (1, 2)]
    needs = {"q0": ("w_qkv",), "a0": ("before",), "o": ("w_out",), "u0": ("w_up",), "d0": ("w_down",), "cast": ("dz",)}

    def store(src, dst):
        return lambda: mover.start(src, dst, id(dst))

    after = {
        "d1": store(v["b"], layer_out),
        "g1": store(w["down"], grads["down"]),
        "ug3": store(w["up"], grads["up"]),
        "og": store(w["out"], grads["out"]),
        "qg2": store(w["qkv"], grads["qkv"]),
        "a5": store(v["dkv"], dkv),
        "ni": store(v["m"], du),
    }
    work = dict(dz=v["dz"], da=v["a"], do=v["do"], dm=v["dm"], dhid=v["f"], dqkv=v["dqkv"])
    first = forward_pass(u, v["before"], v["bias"], gains, w, v, v["b"], None)
    make_bias(docs, v["bias"])
    in_turn(first, {}, needs, {}, None, mover)
    after["d1"]()
    p_of = lambda b, pair: v["p%d" % b].at[pair]
    second = backward_pass(
        v["dz"], u, [v["before"], v["qkv"]], p_of, v["dkv"], None, gains, w, w, v, work, False, v["m"], (ln1, ln2), whole
    )
    in_turn(second, {}, needs, after, None, mover)
    mover.close()


def run_middle(u, docs, vectors, cotangent, qkv_before, weights):
    length, model = u.shape
    table = shapes_of(length, model, weights["up"].shape[-1], 2)
    room = Room()
    room.scratch(**{n: table[n] for n in KEPT + LOCAL + ("bias", "dz", "do", "dm", "dqkv", "dkv")}, before=table["qkv"])
    room.scratch(**{"w_" + n: weights[n] for n in NAMES})
    out_shape = [table["vectors"]] * 3 + [table["b"], table["u"], table["dkv"]] + [weights[n] for n in NAMES]
    outs = pl.pallas_call(
        functools.partial(middle_kernel, table, room),
        out_shape=out_shape,
        in_specs=[VMEM] * 3 + [FAR] * 6,
        out_specs=[VMEM] * 3 + [FAR] * 7,
        scratch_shapes=room.shapes + [pltpu.SemaphoreType.DMA((16,))],
        name="middle",
        compiler_params=pltpu.CompilerParams(vmem_limit_bytes=VMEM_LIMIT),
    )(u, docs, vectors, cotangent, qkv_before, *(weights[n] for n in NAMES))
    return outs[:3], outs[3], outs[4], outs[5], dict(zip(NAMES, outs[6:]))


def reduce_chunks(weights):
    chunks = [("down", ((0, 128), (128, 128)), False), ("down", ((256, 256), (512, 256)), False)]
    for name, parts in (("up", 2), ("out", 1), ("qkv", 3)):
        chunks += [(name, halves, False) for halves in pieces(weights[name].shape[-1], parts)]
    return chunks + [("small", ((0, 128),), False)]


def fold_vectors(vector, small, rows):
    count, model = small.size // 1024, vector.shape[1]
    lane = lax.broadcasted_iota(jnp.int32, (128, model), 1)
    place = lax.broadcasted_iota(jnp.int32, (128, model), 0)
    block = (lane * 2731) >> 16
    pick = jnp.where(lane - block * rows == place, 1.0, 0.0).astype(jnp.bfloat16)
    wide = jnp.broadcast_to(vector[None], (count, 8, model)).reshape(count * 8, model)
    row = lax.broadcasted_iota(jnp.int32, wide.shape, 0)
    owner = (lax.broadcasted_iota(jnp.int32, wide.shape, 1) * 2731) >> 16
    wide = jnp.where((row >> 3) == owner, wide, 0.0).astype(jnp.bfloat16)
    small[...] = dot_nt(wide, pick).astype(jnp.bfloat16).reshape(small.shape)


def last_kernel(near, room, chunks, *refs):
    it = iter(refs)
    tokens, vectors, late1, late2, embed = next(it), next(it), next(it), next(it), next(it)
    far = {n: next(it) for n in ("upstream", "dkv") + KEPT}
    weights = {n: next(it) for n in NAMES}
    before = {n: next(it) for n in NAMES}
    du = next(it)
    outs = {n: next(it) for n in NAMES + ("small",)}
    refs = list(it)
    v = room.bind(refs)
    sems = refs[len(room.names) :]
    mover = Mover(sems[0])
    w = {n: v["w_" + n] for n in NAMES}
    grads = {**w, "down": v["g_down"]}
    model = tokens.shape[1]

    def load(*names):
        def go():
            for n in names:
                if n in NAMES_OF_WEIGHTS:
                    mover.start(weights[n[2:]], w[n[2:]], n)
                elif n[0] == "#":
                    pair = int(n[1:])
                    slot = pair % 2
                    for b in range(2):
                        mover.start(far["p%d" % b].at[pair], v["s%d" % b].at[slot], "p%d_%d" % (b, pair))
                    for k in range(2):
                        mover.start(far["dkv"].at[:, at(pair, 128, k * model)], v["dkv"].at[slot, k], "dkv%d_%d" % (k, pair))
                else:
                    mover.start(far[n], v[n], n)

        return go

    def late(name, *names):
        def go():
            mover.start(before[name], grads[name], "late_" + name)
            load(*names)()

        return go

    def load_down(i):
        def go():
            cols = at(i, 768)
            mover.start(weights["down"].at[i // 2, i % 2], w["down"].at[i // 2, i % 2], "w_down%d" % i)
            mover.start(far["gp"].at[:, cols], v["gp"].at[:, cols], "gp%d" % i)

        return go

    def both(*steps):
        def go():
            for one in steps:
                one()

        return go

    load("upstream", "ft")()
    for i, cols in enumerate((pl.ds(0, 256), pl.ds(256, 512))):
        mover.start(before["down"].at[:, :, :, :, :, cols], grads["down"].at[:, :, :, :, :, cols], "late_down%d" % i)
    load_down(0)()
    needs = {"cast": ("upstream",), "g0": ("ft", "late_down0"), "g1": ("late_down1",)}
    for i in range(4):
        needs["b%d" % i] = ("w_down%d" % i, "gp%d" % i)
    needs.update({
        "ub0": ("w_up",),
        "nb": ("m",),
        "hg": ("w_out", "rl"),
        "ug0": ("bt", "late_up"),
        "og": ("late_out", "ot"),
        "qb0": ("w_qkv",),
        "qg0": ("at", "late_qkv"),
    })
    for i in range(6):
        needs["a%d" % i] = tuple(n % i for n in ("p0_%d", "p1_%d", "dkv0_%d", "dkv1_%d")) + (("qkv",) if i == 0 else ())
    reduce = None
    events = {}
    if near:
        reduce = Reduce(
            chunks, {**grads, "small": v["small"]}, *({n: v["r%d_%s" % (k, n)] for n in NAMES + ("small",)} for k in range(4)), outs, sems[1:]
        )
        reduce.links.greet()
        events = events_before(LAST_ORDER)

    def inputs_done():
        mover.start(v["m"], du, "du")
        row = lax.broadcasted_iota(jnp.int32, embed.shape, 0)
        vector = jnp.where(row == 2, late2[...] + v["ln2"][...], 0.0)
        vector = jnp.where(row == 0, embed[...], jnp.where(row == 1, late1[...] + v["ln1"][...], vector))
        if near:
            fold_vectors(vector, v["small"], 24)
        else:
            outs["small"][...] = vector

    after = {
        "g0": load_down(1),
        "g1": both(load_down(2), load_down(3)),
        "b0": load("w_up"),
        "b2": load("m", "w_out", "rl"),
        "ub1": late("up", "bt"),
        "hg": late("out", "ot"),
        "ug1": load("qkv"),
        "ug2": load("#0"),
        "ug3": load("#1"),
        "a0": load("#2"),
        "a1": load("#3"),
        "a2": load("#4", "w_qkv"),
        "a3": load("#5"),
        "a5": load("at"),
        "qb1": late("qkv"),
        "ni": inputs_done,
    }
    if not near:
        stores = {"g1": "down", "ug3": "up", "og": "out", "qg2": "qkv"}
        for block, name in stores.items():

            def store(name=name, then=after.get(block)):
                mover.start(grads[name], outs[name], "g_" + name)
                if then:
                    then()

            after[block] = store
    work = dict(dz=v["dz"], da=v["dz"], do=v["at"], dm=v["dm"], dhid=v["gp"], dqkv=v["dqkv"])
    gains = [vectors[n : n + 1] for n in (1, 2)]
    p_of = lambda b, pair: v["s%d" % b].at[pair % 2]
    extra_of = lambda pair: (v["dkv"][pair % 2, 0], v["dkv"][pair % 2, 1])
    blocks = backward_pass(
        v["upstream"], tokens, [v["qkv"]], p_of, None, extra_of, gains, w, grads, v, work, True, v["m"], (v["ln1"], v["ln2"]), None
    )
    in_turn(blocks, events, needs, after, reduce and reduce.step, mover)
    if near:
        for n in range(len(chunks)):
            reduce.step("close", n)
    mover.close()


def run_last(near, tokens, vectors, late1, late2, embed, upstream, dkv, kept, weights, before):
    length, model = tokens.shape
    bf16 = jnp.bfloat16
    shape = jax.ShapeDtypeStruct
    table = shapes_of(length, model, weights["up"].shape[-1], 1)
    room = Room()
    room.scratch(**{n: table[n] for n in KEPT + ("dz", "dm", "dqkv") if n not in ("p0", "p1")}, upstream=table["u"])
    for b in range(2):
        room.scratch(**{"s%d" % b: shape((2,) + table["p%d" % b].shape[1:], bf16)})
    room.scratch(dkv=shape((2, 2, length, 128), jnp.float32), g_down=weights["down"])
    room.scratch(ln1=table["vectors"], ln2=table["vectors"])
    room.scratch(**{"w_" + n: weights[n] for n in NAMES})
    chunks = reduce_chunks(weights) if near else []
    semaphores = [pltpu.SemaphoreType.DMA((72,))]
    params = dict(vmem_limit_bytes=VMEM_LIMIT)
    if near:
        parts = {**weights, "small": shape((2, 2, 8, 1, 8, 128), bf16)}
        room.scratch(small=parts["small"])
        for k, blocks in enumerate(((2, 2, 4), (2, 4), (4,), (3,))):
            room.scratch(**{"r%d_%s" % (k, n): shape(blocks + p.shape[3:], bf16) for n, p in parts.items()})
        out_shape = [shape(parts[n].shape[3:], jnp.float32) for n in NAMES + ("small",)]
        out_specs = [VMEM] * 5
        semaphores += link_semaphores(len(chunks))
        params.update(collective_id=1, has_side_effects=True)
    else:
        out_shape = [weights[n] for n in NAMES] + [table["vectors"]]
        out_specs = [FAR] * 4 + [VMEM]
    outs = pl.pallas_call(
        functools.partial(last_kernel, near, room, chunks),
        out_shape=[table["u"]] + out_shape,
        in_specs=[VMEM] * 5 + [FAR] * (2 + len(KEPT) + 8),
        out_specs=[FAR] + out_specs,
        scratch_shapes=room.shapes + semaphores,
        name="last",
        compiler_params=pltpu.CompilerParams(**params),
    )(tokens, vectors, late1, late2, embed, upstream, dkv, *(kept[n] for n in KEPT), *(weights[n] for n in NAMES), *(before[n] for n in NAMES))
    return outs[0], dict(zip(NAMES, outs[1:])), outs[5]


AXES = ("dp", "fsdp")


def cut(w):
    return w.reshape(w.shape[0] // 8, 8, w.shape[1])


def join(w):
    return w.reshape(-1, w.shape[-1])


def whole(w):
    return w.reshape(2, 2, 8, w.shape[0] // 256, 8, w.shape[1])


def body(near, tokens, doc_ids, pass_embed, ln1_gain, w_qkv, w_out, ln2_gain, w_up, w_down, cotangent):
    shards = {"qkv": w_qkv, "out": w_out, "up": w_up, "down": w_down}
    docs = doc_ids.reshape(1, -1)
    rows = pass_embed.shape[0]
    small = vectors = None
    if near:
        wide = [jnp.pad(v[None], ((n, 7 - n), (0, 128 - rows))) for n, v in enumerate((pass_embed, ln1_gain, ln2_gain))]
        small = (wide[0] + wide[1] + wide[2])[None]
        shards = {n: cut(s) for n, s in shards.items()}
    else:
        vectors = jnp.stack([lax.all_gather(v, AXES, axis=0, tiled=True) for v in (pass_embed, ln1_gain, ln2_gain)])
        vectors = jnp.pad(vectors.astype(jnp.float32), ((0, 5), (0, 0)))
        shards = {n: whole(lax.all_gather(s, AXES, axis=0, tiled=True)) for n, s in shards.items()}
    kept, vectors, weights = run_first(near, tokens, docs, small, vectors, shards)
    (late1, late2, embed), layer_out, second_g, dkv, late = run_middle(kept["u"], docs, vectors, cotangent, kept["qkv"], weights)
    tokens_grad, sums, small = run_last(near, tokens, vectors, late1, late2, embed, second_g, dkv, kept, weights, late)
    if near:
        sums = {n: join(s) for n, s in sums.items()}
        small = [small[0, n, :rows] for n in range(3)]
    else:
        scatter = lambda v: lax.psum_scatter(v, AXES, scatter_dimension=0, tiled=True)
        sums = {n: scatter(join(s).astype(jnp.float32)) for n, s in sums.items()}
        small = [scatter(small[n]) for n in range(3)]
    return (layer_out, tokens_grad, small[0], small[1], sums["qkv"], sums["out"], small[2], sums["up"], sums["down"])


def solution(mesh):
    near = dict(mesh.shape) == {"dp": 8, "fsdp": 4}
    placed = (
        P(("dp", "fsdp"), None),
        P(("dp", "fsdp")),
        P(("dp", "fsdp")),
        P(("dp", "fsdp")),
        P(("dp", "fsdp"), None),
        P(("dp", "fsdp"), None),
        P(("dp", "fsdp")),
        P(("dp", "fsdp"), None),
        P(("dp", "fsdp"), None),
        P(("dp", "fsdp"), None),
    )
    return jax.shard_map(
        functools.partial(body, near),
        mesh=mesh,
        in_specs=placed,
        out_specs=(
            P(("dp", "fsdp"), None),
            P(("dp", "fsdp"), None),
            P(("dp", "fsdp")),
            P(("dp", "fsdp")),
            P(("dp", "fsdp"), None),
            P(("dp", "fsdp"), None),
            P(("dp", "fsdp")),
            P(("dp", "fsdp"), None),
            P(("dp", "fsdp"), None),
        ),
        check_vma=False,
    )
```
